32 devices in a mesh: seq: 8 (over z, x), head: 4 (over y, core).
Axes of the slice: x: 2, y: 2, z: 4, core: 2. Of those that a mesh axis runs over, the one named last changes fastest.
Arguments:
- block_input: bfloat16 [8192, 1024], P('seq'), may hold values from -6 to 6
- first_gain: bfloat16 [1024], replicated, may hold values from 0.5 to 1.5
- w_mix: bfloat16 [1024, 5120], P(None, 'head'), may hold values from -0.1875 to 0.1875
- conv_taps: bfloat16 [4, 5120], P(None, 'head'), may hold values from -3 to 3
- w_rates: bfloat16 [1024, 24], P(None, 'head'), may hold values from -1 to 1
- log_rate: float32 [8], P('head'), may hold values from -6.9 to -4
- rate_bias: float32 [8], P('head'), may hold values from -5 to -3
- w_outgate: bfloat16 [1024, 1024], P(None, 'head'), may hold values from -0.1875 to 0.1875
- head_gain: bfloat16 [128], replicated, may hold values from 0.5 to 1.5
- w_out: bfloat16 [1024, 1024], P('head'), may hold values from -0.25 to 0.25
- second_gain: bfloat16 [1024], replicated, may hold values from 0.5 to 1.5
- w_ffn: bfloat16 [1024, 2, 2816], P(None, None, 'head'), may hold values from -0.1875 to 0.1875
- w_down: bfloat16 [2816, 1024], P('head'), may hold values from -0.21875 to 0.21875
- grad_output: bfloat16 [8192, 1024], P('seq'), may hold values from -6 to 6
- seq_starts: int32 [8], P('seq'), may hold values from 1 to 1024, as said below
Outputs:
- block_output: bfloat16 [8192, 1024], P('seq')
- grad_input: float32 [8192, 1024], P('seq')
- grad_first_gain: float32 [1024], P('seq')
- grad_mix: float32 [1024, 5120], P('seq', 'head')
- grad_conv: float32 [4, 5120], P(None, 'head')
- grad_rates: float32 [1024, 24], P('seq', 'head')
- grad_log_rate: float32 [8], P('head')
- grad_rate_bias: float32 [8], P('head')
- grad_outgate: float32 [1024, 1024], P('seq', 'head')
- grad_head_gain: float32 [128], replicated
- grad_out: float32 [1024, 1024], P('head', 'seq')
- grad_second_gain: float32 [1024], P('seq')
- grad_ffn: float32 [1024, 2, 2816], P('seq', None, 'head')
- grad_down: float32 [2816, 1024], P('head', 'seq')
The draws below stay inside these ranges and needn't reach their ends.
Inputs may be any that keep to these rules, and one draw needn't show every extreme that they name: `seq_starts`: token 0 starts a sequence; a block holds at most one more start, at an offset of 1 to 1021, and holds 1024 where none starts; blocks with starts are never neighbours and the last block has none, so every sequence is longer than 1024 tokens; 4 sequences in all.
All inputs are finite; a program needn't handle non-finite values.
Results may differ from the reference program's by a relative error of at most 0.011.
Values sent between devices are 32-bit elements; how exact they have to be, the bound alone decides.
No kernel may reach another device: no remote copies, remote signals or barrier semaphores. Data moves between devices by JAX's collectives and lax.ppermute only.
A program may use at most 256 MiB of HBM per device.

```python
import jax
import jax.numpy as jnp
from jax import lax

D = 1024
HEADS = 8
HEAD_DIM = 128
FF = 2816
STEPS = 2
CONV = 4
SPAN = 64
TOK_DEV = 1024
DOCS = 4
TOKENS = 8192
N_SEQ = 8


def common_mean(key):
    return jnp.clip(jax.random.normal(key, (D,), jnp.float32), -4.0, 4.0)


def draw_block_input(key, part):
    shared = common_mean(key)
    key = jax.random.fold_in(key, 11)
    noise_key = jax.random.fold_in(key, 0)
    noise_part = jnp.clip(jax.random.normal(noise_key, (TOKENS, D), jnp.float32), -4.0, 4.0)
    values = 0.4 * shared[None, :] + 0.92 * noise_part
    return jnp.clip(values, -6.0, 6.0).astype(jnp.bfloat16)


def draw_w_rates(key, part):
    shared = common_mean(key)
    key = jax.random.fold_in(key, 13)
    columns = HEADS * (STEPS + 1)
    random_part = jnp.clip(jax.random.normal(key, (D, columns), jnp.float32), -4.0, 4.0)
    random_part = random_part * D ** (-0.5)
    beta_cols = jnp.arange(columns) % (STEPS + 1) < STEPS
    beta_part = -8.5 * shared[:, None] / D + 0.6 * random_part
    return jnp.where(beta_cols[None, :], beta_part, random_part).astype(jnp.bfloat16)


def draw_seq_starts(key, part):
    key = jax.random.fold_in(key, 7)
    first_key, second_key = jax.random.split(key)
    count = DOCS - 1
    room = N_SEQ - 1 - count
    picks = jnp.sort(jax.random.permutation(first_key, room)[:count])
    blocks = picks + 1 + jnp.arange(count)
    offsets = jax.random.randint(second_key, (count,), 1, TOK_DEV - 2)
    result = jnp.full((N_SEQ,), TOK_DEV, jnp.int32)
    return result.at[blocks].set(offsets.astype(jnp.int32))


def block_levels(own_key, shape, shards, low, high):
    def one(axis_at, shards_of):
        steps = jax.random.uniform(jax.random.fold_in(jax.random.fold_in(own_key, 6), axis_at), (shards_of,), jnp.float32, low / len(shards), high / len(shards))
        return jnp.repeat(jnp.exp(steps), shape[axis_at] // shards_of).reshape((-1,) + (1,) * (len(shape) - axis_at - 1))

    loudness = one(*shards[0])
    for cut in shards[1:]:
        loudness = loudness * one(*cut)
    return loudness


def centred(key, shape, spread, bound, pieces=(), dtype=jnp.bfloat16):
    array = spread * jax.random.normal(key, shape, jnp.float32)
    if pieces:
        array = array * block_levels(key, shape, pieces, -0.22, 0.18)
    return jnp.clip(array, -bound, bound).astype(dtype)


def setup_inputs(seed: int = 0) -> dict:
    keys = jax.random.split(jax.random.key(seed), 16)
    block_input = draw_block_input(jax.random.fold_in(keys[15], 71), 0)
    first_gain = jnp.clip(1.0 + 0.1 * jax.random.normal(keys[1], (D,), jnp.float32), 0.5, 1.5).astype(jnp.bfloat16)
    w_mix = centred(keys[2], (D, HEADS * (1 + 2 * STEPS) * HEAD_DIM), D ** -0.5, 0.1875, ((1, 4),))
    conv_taps = centred(keys[3], (CONV, HEADS * (1 + 2 * STEPS) * HEAD_DIM), CONV ** -0.5, 3.0, ((1, 4),))
    w_rates = draw_w_rates(jax.random.fold_in(keys[15], 71), 0)
    log_rate = jnp.clip(-6.9 + 2.9 * jax.random.uniform(keys[5], (HEADS,), jnp.float32) ** block_levels(keys[5], (HEADS,), ((0, 4),), -0.2, 0.2), -6.9, -4.0)
    rate_bias = jnp.clip(-5.0 + 2.0 * jax.random.uniform(keys[6], (HEADS,), jnp.float32) ** block_levels(keys[6], (HEADS,), ((0, 4),), -0.2, 0.2), -5.0, -3.0)
    w_outgate = centred(keys[7], (D, HEADS * HEAD_DIM), D ** -0.5, 0.1875, ((1, 4),))
    head_gain = jnp.clip(1.0 + 0.1 * jax.random.normal(keys[8], (HEAD_DIM,), jnp.float32), 0.5, 1.5).astype(jnp.bfloat16)
    w_out = centred(keys[9], (HEADS * HEAD_DIM, D), (HEADS * HEAD_DIM // 2) ** -0.5, 0.25, ((0, 4),))
    second_gain = jnp.clip(1.0 + 0.1 * jax.random.normal(keys[10], (D,), jnp.float32), 0.5, 1.5).astype(jnp.bfloat16)
    w_ffn = centred(keys[11], (D, 2, FF), D ** -0.5, 0.1875, ((2, 4),))
    w_down = centred(keys[12], (FF, D), (FF // 4) ** -0.5, 0.21875, ((0, 4),))
    grad_output = centred(keys[13], (TOKENS, D), 1.0, 6.0, ((0, 8),))
    seq_starts = draw_seq_starts(jax.random.fold_in(keys[15], 71), 0)
    return dict(block_input=block_input, first_gain=first_gain, w_mix=w_mix, conv_taps=conv_taps, w_rates=w_rates, log_rate=log_rate, rate_bias=rate_bias, w_outgate=w_outgate, head_gain=head_gain, w_out=w_out, second_gain=second_gain, w_ffn=w_ffn, w_down=w_down, grad_output=grad_output, seq_starts=seq_starts)


EPSILON = 1e-06
HIGH_ACCURACY = lax.Precision.HIGHEST

@jax.custom_vjp
def low(v):
    return lax.optimization_barrier(v.astype(jnp.bfloat16)).astype(jnp.float32)

@jax.custom_vjp
def low_back(v):
    return v

def low_keep(v):
    return (low(v), None)

def low_pass(kept, grad):
    return (grad,)

def back_keep(v):
    return (v, None)

def back_low(kept, grad):
    return (low(grad),)
low.defvjp(low_keep, low_pass)
low_back.defvjp(back_keep, back_low)

def matmul(left, right):
    return jnp.dot(left, right, precision=HIGH_ACCURACY, preferred_element_type=jnp.float32)

def rms_gain(values, gain):
    return values * lax.rsqrt(lax.optimization_barrier(jnp.mean(values * values, -1, keepdims=True)) + EPSILON) * gain

def token_update(state, item):
    mult, query, key_rows, values, betas = item
    state = state * mult[:, None, None]
    for sub in range(STEPS):
        key = key_rows[:, sub]
        guess = jnp.einsum('hvk,hk->hv', state, key, precision=HIGH_ACCURACY)
        change = betas[:, sub, None] * (values[:, sub] - guess)
        state = state + change[:, :, None] * key[:, None, :]
    return (state, jnp.einsum('hvk,hk->hv', state, query, precision=HIGH_ACCURACY))

def span_update(state, items):
    return lax.scan(token_update, state, items)

def reference(block_input, first_gain, w_mix, conv_taps, w_rates, log_rate, rate_bias, w_outgate, head_gain, w_out, second_gain, w_ffn, w_down, grad_output, seq_starts):
    place = jnp.arange(TOKENS).astype(jnp.int32)
    block = place // TOK_DEV
    within = place % TOK_DEV
    resets = (within == seq_starts[block]) | (place == 0)
    begins = lax.cummax(jnp.where(resets, place, 0).astype(jnp.int32), axis=0)
    keep = 1.0 - resets.astype(jnp.float32)
    groups = 1 + 2 * STEPS
    blocks = TOKENS // SPAN

    def forward(inputs, gain1, mix, taps, rates_w, lrate, rbias, outgate_w, hgain, out_w, gain2, ffn, down):
        normed1 = low(rms_gain(inputs, gain1))
        mixing = low_back(matmul(normed1, mix))
        rates = low_back(matmul(normed1, rates_w))
        outgate = low_back(matmul(normed1, outgate_w))
        conv = jnp.zeros_like(mixing)
        for lag in range(CONV):
            back = CONV - 1 - lag
            shifted = jnp.pad(mixing, ((back, 0), (0, 0)))[:TOKENS]
            valid = (place - back >= begins).astype(jnp.float32)
            conv = conv + taps[lag] * shifted * valid[:, None]
        acts = jax.nn.silu(conv).reshape(TOKENS, HEADS, groups, HEAD_DIM)
        query = acts[:, :, 0]
        key_rows = acts[:, :, 1:1 + STEPS]
        values = acts[:, :, 1 + STEPS:]
        key_rows = key_rows * lax.rsqrt(lax.optimization_barrier(jnp.sum(key_rows * key_rows, -1, keepdims=True)) + EPSILON)
        rates3 = rates.reshape(TOKENS, HEADS, STEPS + 1)
        betas = jax.nn.sigmoid(rates3[..., :STEPS])
        decay = -jnp.exp(lrate) * jax.nn.softplus(rates3[..., STEPS] + rbias)
        mult = jnp.exp(decay) * keep[:, None]
        items = (mult.reshape(blocks, SPAN, HEADS), query.reshape(blocks, SPAN, HEADS, HEAD_DIM), key_rows.reshape(blocks, SPAN, HEADS, STEPS, HEAD_DIM), values.reshape(blocks, SPAN, HEADS, STEPS, HEAD_DIM), betas.reshape(blocks, SPAN, HEADS, STEPS))
        start = jnp.zeros((HEADS, HEAD_DIM, HEAD_DIM), jnp.float32)
        final, mixed = lax.scan(jax.checkpoint(span_update), start, items)
        mixed = mixed.reshape(TOKENS, HEADS, HEAD_DIM)
        gated = low(rms_gain(mixed, hgain).reshape(TOKENS, HEADS * HEAD_DIM) * jax.nn.silu(outgate))
        middle = inputs + low_back(matmul(gated, out_w))
        normed2 = low(rms_gain(middle, gain2))
        gate = low_back(matmul(normed2, ffn[:, 0]))
        up = low_back(matmul(normed2, ffn[:, 1]))
        activ = low(jax.nn.silu(gate) * up)
        return middle + matmul(activ, down)
    floats = (block_input.astype(jnp.float32), first_gain.astype(jnp.float32), w_mix.astype(jnp.float32), conv_taps.astype(jnp.float32), w_rates.astype(jnp.float32), log_rate.astype(jnp.float32), rate_bias.astype(jnp.float32), w_outgate.astype(jnp.float32), head_gain.astype(jnp.float32), w_out.astype(jnp.float32), second_gain.astype(jnp.float32), w_ffn.astype(jnp.float32), w_down.astype(jnp.float32))
    output, backward = jax.vjp(forward, *floats)
    grads = backward(grad_output.astype(jnp.float32))
    return (output.astype(jnp.bfloat16), grads[0], grads[1], grads[2], grads[3], grads[4], grads[5], grads[6], grads[7], grads[8], grads[9], grads[10], grads[11], grads[12])
```

```python
from functools import partial

import jax
import jax.numpy as jnp
from jax import lax
from jax.experimental import pallas as pl
from jax.experimental.pallas import tpu as pltpu
from jax.sharding import PartitionSpec as P

STEPS = 2
CONV = 4
SPAN = 64
EDGE = 8
LANES = 128
GROUPS = 1 + 2 * STEPS
PACK = 2
DOCS = 4
EPSILON = 1e-06
VMEM_LIMIT = 56 * 1024 * 1024

F32 = jnp.float32
BF16 = jnp.bfloat16
NN = (1, 0)
NT = (1, 1)
TN = (0, 0)


def dot1(left, right, dims):
    return lax.dot_general(
        left.astype(BF16),
        right.astype(BF16),
        (((dims[0],), (dims[1],)), ((), ())),
        preferred_element_type=F32,
    )


def halves(value):
    high = value.astype(BF16)
    return high, (value - high.astype(F32)).astype(BF16)


def dot3(left, right, dims):
    left_high, left_low = halves(left)
    right_high, right_low = halves(right)
    return dot1(
        jnp.concatenate([left_high, left_low, left_high], dims[0]),
        jnp.concatenate([right_high, right_high, right_low], dims[1]),
        dims,
    )


def iota(shape, dim):
    return lax.broadcasted_iota(jnp.int32, shape, dim)


def twice(value):
    return jnp.concatenate([value, value], 0)


def spread(column):
    return jnp.broadcast_to(column, (column.shape[0], LANES))


def crossing(place, reach, offset):
    return (place < offset) & (offset <= place + reach)


def rate_parts(raw, rate_row, bias_row):
    shifted_raw = raw + bias_row
    soft = jnp.maximum(shifted_raw, 0.0) + jnp.log1p(jnp.exp(-jnp.abs(shifted_raw)))
    slope = -jnp.exp(rate_row)
    return jax.nn.sigmoid(raw), slope * soft, slope * jax.nn.sigmoid(shifted_raw)


def decay_parts(cumul, begin, offset):
    place = begin + iota(cumul.shape, 0)
    inside = offset >= begin
    carried = jnp.where(inside & (place >= offset), 0.0, jnp.exp(cumul))
    cut = (place < offset) & (offset <= begin + (SPAN - 1))
    tail = jnp.exp(jnp.where(cut, -1e30, cumul[SPAN - 1 :] - cumul))
    return carried, tail


def decay_ratio(cumul, begin, offset):
    across = jnp.transpose(twice(cumul))[:SPAN]
    row = iota(across.shape, 0)
    col = iota(across.shape, 1) & (SPAN - 1)
    cut = (begin + col < offset) & (offset <= begin + row)
    return jnp.exp(jnp.where((col <= row) & jnp.logical_not(cut), cumul - across, -1e30))


def strict_mask():
    shape = (STEPS * SPAN, STEPS * SPAN)
    row, col = iota(shape, 0), iota(shape, 1)
    row_tok, col_tok = row & (SPAN - 1), col & (SPAN - 1)
    strict = (col_tok < row_tok) | ((col_tok == row_tok) & (col < row))
    return strict, row_tok ^ col_tok, (row == col).astype(F32)


def local_kernel(
    heads,
    offset_ref,
    edge_ref,
    halo_ref,
    mix_ref,
    taps_ref,
    rates_ref,
    rate_row_ref,
    bias_row_ref,
    conv_ref,
    q_ref,
    k_ref,
    x_ref,
    n_ref,
    cumul_ref,
    u_ref,
    w_ref,
    score_ref,
    query_ref,
    prefix_ref,
    phi_ref,
    total_ref,
    run_ref,
):
    step = pl.program_id(0)
    rows = mix_ref.shape[0]
    offset = offset_ref[0]
    width = LANES
    strict, apart, eye = strict_mask()

    @pl.when(step == 0)
    def _():
        run_ref[...] = jnp.concatenate([jnp.broadcast_to(eye, run_ref.shape[:2] + (width,)), jnp.zeros(run_ref.shape[:2] + (width,), F32)], 2)

    place = step * rows + iota((rows, width), 0)
    keep = [1.0 - crossing(place - back, back, offset).astype(F32) for back in range(CONV)]
    acts = []
    for part in range(heads * GROUPS):
        cols = slice(part * width, (part + 1) * width)
        before = jnp.where(step == 0, edge_ref[:, cols], halo_ref[:, cols])
        wide = jnp.concatenate([before, mix_ref[:, cols]], 0)
        conv = taps_ref[CONV - 1 : CONV, cols] * wide[EDGE:]
        for back in range(1, CONV):
            moved = pltpu.roll(wide, back, 0)[EDGE:]
            conv = conv + taps_ref[CONV - 1 - back : CONV - back, cols] * (moved * keep[back])
        conv_ref[:, cols] = conv
        act = conv * jax.nn.sigmoid(conv)
        if 1 <= part % GROUPS < 1 + STEPS:
            act = act * lax.rsqrt(jnp.sum(act * act, -1, keepdims=True) + EPSILON)
        acts.append(act)

    beta_all, decay_all, _ = rate_parts(rates_ref[...], rate_row_ref[...], bias_row_ref[...])
    lower = (iota((SPAN, SPAN), 1) <= iota((SPAN, SPAN), 0)).astype(F32)
    chains = [(pos, head) for pos in range(rows // SPAN) for head in range(heads)]
    cumuls = [
        jnp.dot(
            lower,
            decay_all[pos * SPAN : (pos + 1) * SPAN],
            precision=lax.Precision.HIGHEST,
            preferred_element_type=F32,
        )
        for pos in range(rows // SPAN)
    ]
    queries, keys, scaleds, tails, carries, ratios, systems = [], [], [], [], [], [], []
    for pos, head in chains:
        here = slice(pos * SPAN, (pos + 1) * SPAN)
        begin = step * rows + pos * SPAN
        query, key1, key2, value1, value2 = (
            act[here] for act in acts[head * GROUPS : (head + 1) * GROUPS]
        )
        key = jnp.concatenate([key1, key2], 0)
        value = jnp.concatenate([value1, value2], 0)
        lane = head * (STEPS + 1)
        beta = jnp.concatenate(
            [spread(beta_all[here, lane + sub : lane + sub + 1]) for sub in range(STEPS)], 0
        )
        cumul = spread(cumuls[pos][:, lane + STEPS : lane + STEPS + 1])
        cumul_ref[head, pos] = cumul
        carried, tail = decay_parts(cumul, begin, offset)
        ratio = decay_ratio(cumul, begin, offset)
        key_low = key.astype(BF16)
        q_ref[head, pos] = query
        k_ref[head, pos] = key_low
        queries.append(query)
        keys.append(key)
        tails.append(twice(tail))
        carries.append(carried)
        ratios.append(ratio)
        scaleds.append(jnp.concatenate([beta * value, beta * twice(carried) * key], 1))
        systems.append(jnp.where(strict, beta * twice(ratio), 0.0) * dot1(key_low, key_low, NT))
    inverses = [eye - jnp.where(apart == 0, system, 0.0) for system in systems]
    for level in range(SPAN.bit_length() - 1):
        off_blocks = [jnp.where((apart >> level) == 1, system, 0.0) for system in systems]
        lows = [inverse.astype(BF16) for inverse in inverses]
        halfway = [dot1(low, off, NN) for low, off in zip(lows, off_blocks)]
        inverses = [
            inverse - dot1(half, low, NN) for inverse, half, low in zip(inverses, halfway, lows)
        ]
    solveds = [dot3(inverse, scaled, NN) for inverse, scaled in zip(inverses, scaleds)]
    all_scores = [ratio * dot3(query, key, NT) for ratio, query, key in zip(ratios, queries, keys)]
    all_maps = [
        dot3(
            key,
            jnp.concatenate([tail * solved[:, width:], tail * solved[:, :width]], 1),
            TN,
        )
        for key, tail, solved in zip(keys, tails, solveds)
    ]
    inner = [dot1(scores, solved[:, width:], NN) for scores, solved in zip(all_scores, solveds)]
    for index, (pos, head) in enumerate(chains):
        solved, maps, carried = solveds[index], all_maps[index], carries[index]
        phi = carried[SPAN - 1 :] * eye - maps[:, :width]
        x_ref[head, pos] = inverses[index].astype(BF16)
        n_ref[head, pos] = systems[index].astype(BF16)
        u_ref[head, pos] = solved[:, :width]
        w_ref[head, pos] = solved[:, width:]
        score_ref[head, pos] = all_scores[index]
        query_ref[head, pos] = carried * queries[index] - inner[index]
        phi_ref[head, pos] = phi
        run = run_ref[head]
        prefix_ref[head, pos] = run
        moved_run = dot3(phi, run, NN)
        run_ref[head] = jnp.concatenate(
            [moved_run[:, :width], moved_run[:, width:] + maps[:, width:]], 1
        )
    total_ref[...] = run_ref[...]


def specs_of(heads, pack):
    def per_block(*dims):
        return pl.BlockSpec((heads, pack) + dims, lambda g: (0, g) + (0,) * len(dims))

    return per_block


def whole(shape):
    return pl.BlockSpec(shape, lambda g: (0,) * len(shape))


SCALARS = pl.BlockSpec(memory_space=pltpu.SMEM)


def params():
    return pltpu.CompilerParams(vmem_limit_bytes=VMEM_LIMIT)


def local_maps(offset, edge, mixing, taps, rates, rate_row, bias_row):
    rows, columns = mixing.shape
    width = LANES
    heads = columns // (GROUPS * width)
    blocks = rows // SPAN
    virt = STEPS * SPAN
    tile = PACK * SPAN
    per_block = specs_of(heads, PACK)
    saved = [
        (per_block(SPAN, width), (SPAN, width), F32),
        (per_block(virt, width), (virt, width), BF16),
        (per_block(virt, virt), (virt, virt), BF16),
        (per_block(virt, virt), (virt, virt), BF16),
        (per_block(SPAN, width), (SPAN, width), F32),
        (per_block(virt, width), (virt, width), F32),
        (per_block(virt, width), (virt, width), F32),
        (per_block(SPAN, virt), (SPAN, virt), F32),
        (per_block(SPAN, width), (SPAN, width), F32),
        (per_block(width, 2 * width), (width, 2 * width), F32),
        (per_block(width, width), (width, width), F32),
    ]
    return pl.pallas_call(
        partial(local_kernel, heads),
        grid=(blocks // PACK,),
        in_specs=[
            SCALARS,
            whole((EDGE, columns)),
            pl.BlockSpec((EDGE, columns), lambda g: (jnp.maximum(g * (tile // EDGE) - 1, 0), 0)),
            pl.BlockSpec((tile, columns), lambda g: (g, 0)),
            whole(taps.shape),
            pl.BlockSpec((tile, LANES), lambda g: (g, 0)),
            whole((1, LANES)),
            whole((1, LANES)),
        ],
        out_specs=[pl.BlockSpec((tile, columns), lambda g: (g, 0))]
        + [spec for spec, _, _ in saved]
        + [whole((heads, width, 2 * width))],
        out_shape=[jax.ShapeDtypeStruct((rows, columns), F32)]
        + [jax.ShapeDtypeStruct((heads, blocks) + dims, kind) for _, dims, kind in saved]
        + [jax.ShapeDtypeStruct((heads, width, 2 * width), F32)],
        scratch_shapes=[pltpu.VMEM((heads, width, 2 * width), F32)],
        compiler_params=params(),
        name="local_maps",
    )(offset, edge, mixing, mixing, taps, rates, rate_row, bias_row)


def output_kernel(
    heads,
    offset_ref,
    incoming_ref,
    prefix_ref,
    u_ref,
    w_ref,
    score_ref,
    q_ref,
    cumul_ref,
    outgate_ref,
    gain_ref,
    state_ref,
    fresh_ref,
    mixed_ref,
    gated_ref,
):
    step = pl.program_id(0)
    pack = prefix_ref.shape[1]
    width = LANES
    offset = offset_ref[0]
    chains = [(pos, head) for pos in range(pack) for head in range(heads)]
    states = [
        dot3(prefix_ref[head, pos, :, :width], incoming_ref[head], NN)
        + prefix_ref[head, pos, :, width:]
        for pos, head in chains
    ]
    freshes = [
        u_ref[head, pos] - dot3(w_ref[head, pos], state, NN)
        for (pos, head), state in zip(chains, states)
    ]
    outs = []
    for (pos, head), state, fresh in zip(chains, states, freshes):
        carried, _ = decay_parts(cumul_ref[head, pos], (step * pack + pos) * SPAN, offset)
        outs.append(
            dot3(
                jnp.concatenate([carried * q_ref[head, pos], score_ref[head, pos]], 1),
                jnp.concatenate([state, fresh], 0),
                NN,
            )
        )
    for (pos, head), state, fresh, mixed in zip(chains, states, freshes, outs):
        here = slice(pos * SPAN, (pos + 1) * SPAN)
        cols = slice(head * width, (head + 1) * width)
        state_ref[head, pos] = state.astype(BF16)
        fresh_ref[head, pos] = fresh.astype(BF16)
        mixed_ref[here, cols] = mixed
        scale = lax.rsqrt(jnp.mean(mixed * mixed, -1, keepdims=True) + EPSILON)
        outgate = outgate_ref[here, cols]
        gated = mixed * scale * gain_ref[...] * (outgate * jax.nn.sigmoid(outgate))
        gated_ref[here, cols] = gated.astype(BF16).astype(gated_ref.dtype)


def outputs_of(offset, incoming, saved, outgate, gain, gated_type):
    prefix, u, w, scores, q, cumul = saved
    heads, blocks = prefix.shape[:2]
    width = LANES
    virt = STEPS * SPAN
    tile = PACK * SPAN
    rows = outgate.shape[0]
    per_block = specs_of(heads, PACK)
    flat = pl.BlockSpec((tile, heads * width), lambda g: (g, 0))
    return pl.pallas_call(
        partial(output_kernel, heads),
        grid=(blocks // PACK,),
        in_specs=[
            SCALARS,
            whole((heads, width, width)),
            per_block(width, 2 * width),
            per_block(virt, width),
            per_block(virt, width),
            per_block(SPAN, virt),
            per_block(SPAN, width),
            per_block(SPAN, width),
            flat,
            whole((1, width)),
        ],
        out_specs=[per_block(width, width), per_block(virt, width), flat, flat],
        out_shape=[
            jax.ShapeDtypeStruct((heads, blocks, width, width), BF16),
            jax.ShapeDtypeStruct((heads, blocks, virt, width), BF16),
            jax.ShapeDtypeStruct((rows, heads * width), F32),
            jax.ShapeDtypeStruct((rows, heads * width), gated_type),
        ],
        compiler_params=params(),
        name="mixer_outputs",
    )(offset, incoming, prefix, u, w, scores, q, cumul, outgate, gain)


def gate_back_kernel(
    heads,
    grad_ref,
    mixed_ref,
    outgate_ref,
    gain_ref,
    query_ref,
    prefix_ref,
    grad_mixed_ref,
    grad_outgate_ref,
    grad_gain_ref,
    term_ref,
    total_ref,
):
    step = pl.program_id(0)
    pack = prefix_ref.shape[1]
    width = LANES

    @pl.when(step == 0)
    def _():
        grad_gain_ref[...] = jnp.zeros_like(grad_gain_ref)
        total_ref[...] = jnp.zeros_like(total_ref)

    for head in range(heads):
        cols = slice(head * width, (head + 1) * width)
        mixed = mixed_ref[:, cols]
        outgate = outgate_ref[:, cols]
        grad = grad_ref[:, cols]
        gain = gain_ref[...]
        scale = lax.rsqrt(jnp.mean(mixed * mixed, -1, keepdims=True) + EPSILON)
        normed = mixed * scale
        sigma = jax.nn.sigmoid(outgate)
        silu = outgate * sigma
        grad_outgate = grad * normed * gain * (sigma * (1.0 + outgate * (1.0 - sigma)))
        grad_outgate_ref[:, cols] = grad_outgate.astype(BF16)
        through = grad * silu
        product = through * normed
        grad_gain_ref[...] += jnp.sum(product.reshape(-1, 8, width), 0)
        grad_normed = through * gain
        grad_mixed = scale * (
            grad_normed - normed * jnp.mean(grad_normed * normed, -1, keepdims=True)
        )
        grad_low = grad_mixed.astype(BF16)
        grad_mixed_ref[:, cols] = grad_low
        total = total_ref[head]
        for pos in range(pack):
            here = slice(pos * SPAN, (pos + 1) * SPAN)
            term = dot3(query_ref[head, pos], grad_mixed[here], TN)
            term_ref[head, pos] = term
            total = total + dot3(prefix_ref[head, pos], term, TN)
        total_ref[head] = total


def gate_back(grad, mixed, outgate, gain, query, prefix):
    heads, blocks = prefix.shape[:2]
    width = LANES
    tile = PACK * SPAN
    rows = mixed.shape[0]
    per_block = specs_of(heads, PACK)
    flat = pl.BlockSpec((tile, heads * width), lambda g: (g, 0))
    return pl.pallas_call(
        partial(gate_back_kernel, heads),
        grid=(blocks // PACK,),
        in_specs=[flat, flat, flat, whole((1, width)), per_block(SPAN, width), per_block(width, width)],
        out_specs=[
            flat,
            flat,
            whole((8, width)),
            per_block(width, width),
            whole((heads, width, width)),
        ],
        out_shape=[
            jax.ShapeDtypeStruct((rows, heads * width), BF16),
            jax.ShapeDtypeStruct((rows, heads * width), BF16),
            jax.ShapeDtypeStruct((8, width), F32),
            jax.ShapeDtypeStruct((heads, blocks, width, width), F32),
            jax.ShapeDtypeStruct((heads, width, width), F32),
        ],
        compiler_params=params(),
        name="gate_back",
    )(grad, mixed, outgate, gain, query, prefix)


def back_kernel(
    heads,
    offset_ref,
    leaving_ref,
    term_ref,
    phi_ref,
    state_ref,
    fresh_ref,
    grad_ref,
    score_ref,
    x_ref,
    n_ref,
    cumul_ref,
    q_ref,
    k_ref,
    rates_ref,
    rate_row_ref,
    bias_row_ref,
    conv_ref,
    edge_ref,
    halo_ref,
    mix_ref,
    taps_ref,
    grad_mix_ref,
    last_ref,
    before_ref,
    grad_rates_ref,
    decay_sum_ref,
    grad_taps_ref,
    run_ref,
    next_ref,
    act_ref,
):
    step = pl.program_id(0)
    steps = pl.num_programs(0)
    group = steps - 1 - step
    rows = mix_ref.shape[0]
    offset = offset_ref[0]
    width = LANES
    virt = STEPS * SPAN
    strict, _, _ = strict_mask()
    lane = iota((SPAN, width), 1)

    @pl.when(step == 0)
    def _():
        run_ref[...] = leaving_ref[...]
        next_ref[...] = jnp.zeros_like(next_ref)
        decay_sum_ref[...] = jnp.zeros_like(decay_sum_ref)
        grad_taps_ref[...] = jnp.zeros_like(grad_taps_ref)

    tok_row, tok_col = iota((SPAN, SPAN), 0), iota((SPAN, SPAN), 1)
    later = (tok_col >= tok_row).astype(BF16)
    earlier = tok_col < tok_row
    sums = jnp.concatenate([later, earlier.astype(BF16)], 1)
    beta_all, decay_all, slope_all = rate_parts(
        rates_ref[...], rate_row_ref[...], bias_row_ref[...]
    )
    chains = [(pos, head) for pos in reversed(range(rows // SPAN)) for head in range(heads)]
    leavings = []
    for pos, head in chains:
        leaving = run_ref[head]
        leavings.append(leaving)
        run_ref[head] = dot3(phi_ref[head, pos], leaving, TN) + term_ref[head, pos]
    betas, parts_of, ratios, masked = [], [], [], []
    for pos, head in chains:
        here = slice(pos * SPAN, (pos + 1) * SPAN)
        begin = group * rows + pos * SPAN
        first_lane = head * (STEPS + 1)
        beta = jnp.concatenate(
            [
                spread(beta_all[here, first_lane + sub : first_lane + sub + 1])
                for sub in range(STEPS)
            ],
            0,
        )
        cumul = cumul_ref[head, pos]
        betas.append(beta)
        parts_of.append(decay_parts(cumul, begin, offset))
        ratio = decay_ratio(cumul, begin, offset)
        ratios.append(ratio)
        masked.append(jnp.where(strict, beta * twice(ratio), 0.0))
    lows = [leaving.astype(BF16) for leaving in leavings]
    grads = [
        grad_ref[pos * SPAN : (pos + 1) * SPAN, head * width : (head + 1) * width]
        for pos, head in chains
    ]
    scores_low = [score_ref[head, pos].astype(BF16) for pos, head in chains]
    states = [state_ref[head, pos] for pos, head in chains]
    freshes = [fresh_ref[head, pos] for pos, head in chains]
    queries = [q_ref[head, pos] for pos, head in chains]
    keys = [k_ref[head, pos] for pos, head in chains]
    key_leavings = [
        twice(tail) * dot1(key, low, NN) for key, low, (_, tail) in zip(keys, lows, parts_of)
    ]
    grad_freshes = [
        dot1(scores, grad, TN) + key_leaving
        for scores, grad, key_leaving in zip(scores_low, grads, key_leavings)
    ]
    solveds = [
        dot1(x_ref[head, pos], grad_fresh, TN)
        for (pos, head), grad_fresh in zip(chains, grad_freshes)
    ]
    scaleds = [beta * solved for beta, solved in zip(betas, solveds)]
    grad_scores = [dot1(grad, fresh, NT) for grad, fresh in zip(grads, freshes)]
    grad_systems = [-dot1(solved, fresh, NT) for solved, fresh in zip(solveds, freshes)]
    grad_states = [
        carried * dot1(grad, state, NT)
        for grad, state, (carried, _) in zip(grads, states, parts_of)
    ]
    scaled_states = [
        twice(carried) * dot1(scaled, state, NT)
        for scaled, state, (carried, _) in zip(scaleds, states, parts_of)
    ]
    boths = [
        jnp.concatenate([grad_score * ratio, grad_system * mask], 0).astype(BF16)
        for grad_score, ratio, grad_system, mask in zip(grad_scores, ratios, grad_systems, masked)
    ]
    from_keys = [dot1(both, key, NN) for both, key in zip(boths, keys)]
    to_keys = [
        dot1(both, jnp.concatenate([query.astype(BF16), key], 0), TN)
        for both, query, key in zip(boths, queries, keys)
    ]
    from_leavings = [
        twice(tail) * dot1(fresh, low, NT) for fresh, low, (_, tail) in zip(freshes, lows, parts_of)
    ]
    all_pairs = []
    for index, (pos, head) in enumerate(chains):
        system_pairs = grad_systems[index] * n_ref[head, pos].astype(F32)
        pairs = grad_scores[index] * score_ref[head, pos]
        pairs = pairs + system_pairs[:SPAN] + system_pairs[SPAN:]
        all_pairs.append(pairs[:, :SPAN] + pairs[:, SPAN:])
    crossed = [jnp.where(earlier, dot1(later, pairs, NN), 0.0) for pairs in all_pairs]
    all_ends = []
    for index, (pos, head) in enumerate(chains):
        read = scaled_states[index] * keys[index].astype(F32)
        arriving = grad_states[index] * queries[index] - read[:SPAN] - read[SPAN:]
        written = key_leavings[index] * freshes[index].astype(F32)
        written = written[:SPAN] + written[SPAN:]
        all_ends.append(dot1(sums, jnp.concatenate([arriving, written], 0), NN))
    rates_of = [jnp.zeros((SPAN, width), F32) for _ in range(rows // SPAN)]
    for index, (pos, head) in enumerate(chains):
        here = slice(pos * SPAN, (pos + 1) * SPAN)
        first_lane = head * (STEPS + 1)
        grad_query = from_keys[index][:SPAN] + grad_states[index]
        grad_key = (
            from_keys[index][SPAN:]
            - scaled_states[index]
            + to_keys[index]
            + from_leavings[index]
        )
        scaled = scaleds[index]
        for place_of, part in enumerate(
            (grad_query, grad_key[:SPAN], grad_key[SPAN:], scaled[:SPAN], scaled[SPAN:])
        ):
            at = (head * GROUPS + place_of) * width
            act_ref[here, at : at + width] = part
        fresh = freshes[index].astype(F32)
        step_part = (1.0 - betas[index]) * jnp.sum(solveds[index] * fresh, -1, keepdims=True)
        kept = parts_of[index][0][SPAN - 1 :] * jnp.sum(
            leavings[index] * states[index].astype(F32), 0, keepdims=True
        )
        grad_decay = jnp.sum(crossed[index], -1, keepdims=True) + jnp.sum(
            all_ends[index] + kept, -1, keepdims=True
        )
        for sub in range(STEPS):
            rates_of[pos] = jnp.where(
                lane == first_lane + sub,
                step_part[sub * SPAN : (sub + 1) * SPAN],
                rates_of[pos],
            )
        rates_of[pos] = jnp.where(lane == first_lane + STEPS, spread(grad_decay), rates_of[pos])
    is_decay = lane % (STEPS + 1) == STEPS
    for pos, grad_rates in enumerate(rates_of):
        here = slice(pos * SPAN, (pos + 1) * SPAN)
        decay_part = jnp.where(is_decay, grad_rates * decay_all[here], 0.0)
        grad_rates = jnp.where(is_decay, grad_rates * slope_all[here], grad_rates)
        grad_rates_ref[here] = grad_rates.astype(BF16)
        decay_sum_ref[0:1] += jnp.sum(decay_part, 0, keepdims=True)
        decay_sum_ref[1:2] += jnp.sum(jnp.where(is_decay, grad_rates, 0.0), 0, keepdims=True)

    place = group * rows + iota((rows, width), 0)
    keep_back = [1.0 - crossing(place - back, back, offset).astype(F32) for back in range(CONV)]
    keep_fore = [1.0 - crossing(place, fore, offset).astype(F32) for fore in range(CONV)]
    edge_place = iota((EDGE, width), 0) - EDGE
    keep_edge = [1.0 - crossing(edge_place, fore, offset).astype(F32) for fore in range(CONV)]
    for part in range(heads * GROUPS):
        cols = slice(part * width, (part + 1) * width)
        conv = conv_ref[:, cols]
        grad = act_ref[:, cols]
        sigma = jax.nn.sigmoid(conv)
        if 1 <= part % GROUPS < 1 + STEPS:
            act = conv * sigma
            scale = lax.rsqrt(jnp.sum(act * act, -1, keepdims=True) + EPSILON)
            unit = act * scale
            grad = scale * (grad - unit * jnp.sum(unit * grad, -1, keepdims=True))
        grad_conv = grad * (sigma * (1.0 + conv * (1.0 - sigma)))
        wide = jnp.concatenate([grad_conv, next_ref[:, cols]], 0)
        before = jnp.concatenate([jnp.zeros((EDGE, width), F32), grad_conv[:EDGE]], 0)
        above = jnp.where(group == 0, edge_ref[:, cols], halo_ref[:, cols])
        mix_wide = jnp.concatenate([above, mix_ref[:, cols]], 0)
        tap = taps_ref[CONV - 1 : CONV, cols]
        grad_mix = tap * grad_conv
        grad_before = jnp.zeros((EDGE, width), F32)
        sums_of = jnp.sum(grad_conv * mix_wide[EDGE:], 0, keepdims=True)
        grad_taps_ref[CONV - 1 : CONV, cols] += sums_of
        for shift in range(1, CONV):
            tap = taps_ref[CONV - 1 - shift : CONV - shift, cols]
            moved = pltpu.roll(wide, rows + EDGE - shift, 0)[:rows]
            grad_mix = grad_mix + tap * (moved * keep_fore[shift])
            moved = pltpu.roll(before, 2 * EDGE - shift, 0)[:EDGE]
            grad_before = grad_before + tap * (moved * keep_edge[shift])
            moved = pltpu.roll(mix_wide, shift, 0)[EDGE:] * keep_back[shift]
            grad_taps_ref[CONV - 1 - shift : CONV - shift, cols] += jnp.sum(
                grad_conv * moved, 0, keepdims=True
            )
        next_ref[:, cols] = grad_conv[:EDGE]
        grad_mix_ref[:, cols] = grad_mix.astype(BF16)
        before_ref[:, cols] = grad_before

        @pl.when(step == 0)
        def _():
            last_ref[:, cols] = grad_mix[rows - 2 * EDGE :]


def recurrence_back(offset, leaving, saved, rates, rate_row, bias_row, conv, edge, mixing, taps):
    term, phi, state, fresh, grad, scores, x, n, cumul, q, k = saved
    rows, columns = mixing.shape
    heads, blocks = term.shape[:2]
    width = LANES
    virt = STEPS * SPAN
    tile = PACK * SPAN
    steps = blocks // PACK

    def per_block(*dims):
        return pl.BlockSpec(
            (heads, PACK) + dims, lambda g: (0, steps - 1 - g) + (0,) * len(dims)
        )

    def flat(size):
        return pl.BlockSpec((tile, size), lambda g: (steps - 1 - g, 0))

    return pl.pallas_call(
        partial(back_kernel, heads),
        grid=(steps,),
        in_specs=[
            SCALARS,
            whole((heads, width, width)),
            per_block(width, width),
            per_block(width, width),
            per_block(width, width),
            per_block(virt, width),
            flat(heads * width),
            per_block(SPAN, virt),
            per_block(virt, virt),
            per_block(virt, virt),
            per_block(SPAN, width),
            per_block(SPAN, width),
            per_block(virt, width),
            flat(LANES),
            whole((1, LANES)),
            whole((1, LANES)),
            flat(columns),
            whole((EDGE, columns)),
            pl.BlockSpec(
                (EDGE, columns),
                lambda g: (jnp.maximum((steps - 1 - g) * (tile // EDGE) - 1, 0), 0),
            ),
            flat(columns),
            whole(taps.shape),
        ],
        out_specs=[
            flat(columns),
            whole((2 * EDGE, columns)),
            whole((EDGE, columns)),
            flat(LANES),
            whole((8, LANES)),
            whole((8, columns)),
        ],
        out_shape=[
            jax.ShapeDtypeStruct((rows, columns), BF16),
            jax.ShapeDtypeStruct((2 * EDGE, columns), F32),
            jax.ShapeDtypeStruct((EDGE, columns), F32),
            jax.ShapeDtypeStruct((rows, LANES), BF16),
            jax.ShapeDtypeStruct((8, LANES), F32),
            jax.ShapeDtypeStruct((8, columns), F32),
        ],
        scratch_shapes=[
            pltpu.VMEM((heads, width, width), F32),
            pltpu.VMEM((EDGE, columns), F32),
            pltpu.VMEM((tile, columns), F32),
        ],
        compiler_params=params(),
        name="recurrence_back",
    )(
        offset, leaving, term, phi, state, fresh, grad, scores, x, n, cumul, q, k,
        rates, rate_row, bias_row, conv, edge, mixing, mixing, taps,
    )


def exchange(value, axis, bit):
    count = lax.axis_size(axis)
    return lax.ppermute(value, axis, [(place, place ^ bit) for place in range(count)])


def shifted(value, axis, steps):
    count = lax.axis_size(axis)
    first, last = (max(0, -steps), min(count, count - steps))
    return lax.ppermute(value, axis, [(source, source + steps) for source in range(first, last)])


def bits_of(axis):
    count = lax.axis_size(axis)
    return [1 << power for power in range(count.bit_length() - 1)]


def gather_near(value, axis):
    found = [value]
    for bit in reversed(bits_of(axis)):
        found = [found, [exchange(part, axis, bit) for part in found]]
        found = found[0] + found[1]
    order = [0]
    for bit in reversed(bits_of(axis)):
        order = order + [place ^ bit for place in order]
    return [part for _, part in sorted(zip(order, found), key=lambda pair: pair[0])]


def scatter_sum(pieces, axis):
    mine = lax.axis_index(axis)
    for bit in bits_of(axis):
        side = (mine // bit) % 2
        pairs = pieces.reshape((pieces.shape[0] // 2, 2) + pieces.shape[1:])
        kept = lax.dynamic_index_in_dim(pairs, side, 1, keepdims=False)
        sent = lax.dynamic_index_in_dim(pairs, 1 - side, 1, keepdims=False)
        pieces = kept + exchange(sent, axis, bit)
    return pieces[0]


def contract(left, right, left_dim, right_dim):
    return lax.dot_general(
        left, right, (((left_dim,), (right_dim,)), ((), ())), preferred_element_type=F32
    )


def carried_in(total, own, axis, backward):
    count = lax.axis_size(axis)
    sign = -1 if backward else 1
    reach = count - DOCS - 1
    if reach > DOCS - 1:
        reach = count - 1
    dims = (1, 1) if backward else (2, 1)

    def move(map_of, state):
        return lax.dot_general(
            map_of, state, (((dims[0],), (1,)), ((0,), (0,))), precision=lax.Precision.HIGHEST
        )

    if reach < count - 1:
        maps = [shifted(total, axis, sign * step) for step in range(1, reach)]
        terms = [shifted(own, axis, sign * step) for step in range(1, reach + 1)]
    else:
        every_map, every_term = lax.all_gather(total, axis), lax.all_gather(own, axis)
        mine = lax.axis_index(axis)

        def at(array, step):
            place = mine - sign * step
            picked = lax.dynamic_index_in_dim(array, jnp.clip(place, 0, count - 1), 0, False)
            return jnp.where((place >= 0) & (place < count), picked, 0.0)

        maps = [at(every_map, step) for step in range(1, reach)]
        terms = [at(every_term, step) for step in range(1, reach + 1)]
    state = terms[-1]
    for map_of, term in zip(reversed(maps), reversed(terms[:-1])):
        state = move(map_of, state) + term
    return state


def normalize(values):
    return values * lax.rsqrt(jnp.mean(values * values, -1, keepdims=True) + EPSILON)


def norm_back(values, gain, grad):
    scale = lax.rsqrt(jnp.mean(values * values, -1, keepdims=True) + EPSILON)
    normed = values * scale
    through = grad * gain
    back = scale * (through - normed * jnp.mean(through * normed, -1, keepdims=True))
    return back, jnp.sum(grad * normed, 0)


def lanes_of(per_head):
    row = jnp.repeat(per_head, STEPS + 1)
    return jnp.pad(row, (0, LANES - row.shape[0]))[None]


def place_rows(parts, axis):
    mine = lax.axis_index(axis)
    count = len(parts)
    rows = parts[0].shape[0]
    out = jnp.zeros((count * rows,) + parts[0].shape[1:], parts[0].dtype)
    for near, part in enumerate(parts):
        out = lax.dynamic_update_slice_in_dim(out, part, (mine ^ near) * rows, 0)
    return out


def project_kernel(parts, *refs):
    gated_refs, weight_refs = refs[:parts], refs[parts : 2 * parts]
    input_ref, gain_ref, middle_ref, normed_ref, low_ref = refs[2 * parts :]

    @pl.when(pl.program_id(0) == 0)
    def _():
        for part in range(parts):
            low_ref[part] = weight_refs[part][...].astype(BF16)

    middle = input_ref[...].astype(F32)
    for part in range(parts):
        middle = middle + dot1(gated_refs[part][...], low_ref[part], NN)
    middle_ref[...] = middle
    scale = lax.rsqrt(jnp.mean(middle * middle, -1, keepdims=True) + EPSILON)
    normed_ref[...] = (middle * scale * gain_ref[...]).astype(BF16)


def mixer_project(gated_near, weight_near, block_input, gain):
    parts = len(gated_near)
    rows, model = block_input.shape
    tile = rows // 4
    depth = gated_near[0].shape[1]
    return pl.pallas_call(
        partial(project_kernel, parts),
        grid=(rows // tile,),
        in_specs=[pl.BlockSpec((tile, depth), lambda g: (g, 0))] * parts
        + [whole((depth, model))] * parts
        + [pl.BlockSpec((tile, model), lambda g: (g, 0)), whole((1, model))],
        out_specs=[pl.BlockSpec((tile, model), lambda g: (g, 0))] * 2,
        out_shape=[
            jax.ShapeDtypeStruct((rows, model), F32),
            jax.ShapeDtypeStruct((rows, model), BF16),
        ],
        scratch_shapes=[pltpu.VMEM((parts, depth, model), BF16)],
        compiler_params=params(),
        name="mixer_project",
    )(*gated_near, *weight_near, block_input, gain)


def body(
    block_input,
    first_gain,
    w_mix,
    conv_taps,
    w_rates,
    log_rate,
    rate_bias,
    w_outgate,
    head_gain,
    w_out,
    second_gain,
    w_ffn,
    w_down,
    grad_output,
    seq_starts,
):
    rows, model = block_input.shape
    heads = log_rate.shape[0]
    parts = lax.axis_size("head")
    quarter = rows // parts
    head_index = lax.axis_index("head")
    gain1, gain2 = first_gain.astype(F32), second_gain.astype(F32)
    head_gain_row = head_gain.astype(F32)[None]
    taps = conv_taps.astype(F32)
    rate_row, bias_row = lanes_of(log_rate), lanes_of(rate_bias)
    rate_lanes = w_rates.shape[1]
    w_rates_wide = jnp.pad(w_rates, ((0, 0), (0, LANES - rate_lanes)))

    inputs_f = block_input.astype(F32)
    normed1_low = (normalize(inputs_f) * gain1).astype(BF16)
    mixing = contract(normed1_low, w_mix, 1, 0)
    edge = shifted(mixing[rows - EDGE :], "seq", 1)
    rates = contract(normed1_low, w_rates_wide, 1, 0)
    outgate = contract(normed1_low, w_outgate, 1, 0)
    w_out_near = gather_near(w_out.astype(F32), "head")

    conv, q, k, x, system, cumul, u, w, scores, query_map, prefix, phi, total = local_maps(
        seq_starts, edge, mixing, taps, rates, rate_row, bias_row
    )
    width = LANES
    device_map, device_term = total[..., :width], total[..., width:]
    incoming = carried_in(device_map, device_term, "seq", False)
    state, fresh, mixed, gated = outputs_of(
        seq_starts, incoming, (prefix, u, w, scores, q, cumul), outgate, head_gain_row, F32
    )
    gated_near = gather_near(gated, "head")
    middle, normed2_low = mixer_project(gated_near, w_out_near, block_input, gain2[None])
    ffn_flat = w_ffn.reshape(model, -1)
    hidden_units = ffn_flat.shape[1] // 2
    both = contract(normed2_low, ffn_flat, 1, 0)
    gate, up = both[:, :hidden_units], both[:, hidden_units:]
    sigma = jax.nn.sigmoid(gate)
    activ_low = (gate * sigma * up).astype(BF16)
    grad_activ = contract(grad_output, w_down, 1, 1)
    grad_gate = grad_activ * up * (sigma * (1.0 + gate * (1.0 - sigma)))
    grad_up = grad_activ * (gate * sigma)
    grad_both = jnp.concatenate([grad_gate, grad_up], 1).astype(BF16)
    normed2_part = contract(grad_both, ffn_flat, 1, 1)
    grad_normed2 = scatter_sum(normed2_part.reshape(parts, quarter, model), "head")

    own_rows = lambda array: lax.dynamic_slice_in_dim(array, head_index * quarter, quarter, 0)
    grad_middle_own, grad_second_gain = norm_back(own_rows(middle), gain2, grad_normed2)
    grad_middle_own = grad_middle_own + own_rows(grad_output).astype(F32)
    grad_middle = place_rows(gather_near(grad_middle_own, "head"), "head")
    grad_branch = grad_middle.astype(BF16)
    grad_gated = contract(grad_branch, w_out, 1, 1)
    grad_mixed, outgate_low, grad_gain, term, grad_total = gate_back(
        grad_gated, mixed, outgate, head_gain_row, query_map, prefix
    )
    leaving = carried_in(device_map, grad_total, "seq", True)

    ffn_out = lax.psum(contract(activ_low, w_down, 1, 0), "head")
    block_output = (middle + ffn_out).astype(BF16)
    grad_ffn = contract(normed2_low, grad_both, 0, 0)
    grad_down = contract(activ_low, grad_output, 0, 0)
    grad_out = contract(gated.astype(BF16), grad_branch, 0, 0)

    grad_mix_rows, last_rows, before_rows, rate_low, decay_sums, grad_taps = recurrence_back(
        seq_starts,
        leaving,
        (term, phi, state, fresh, grad_mixed, scores, x, system, cumul, q, k),
        rates,
        rate_row,
        bias_row,
        conv,
        edge,
        mixing,
        taps,
    )
    returned = shifted(before_rows, "seq", -1)
    last_rows = last_rows + jnp.pad(returned, ((EDGE, 0), (0, 0)))
    mixing_low = lax.dynamic_update_slice_in_dim(
        grad_mix_rows, last_rows.astype(BF16), rows - 2 * EDGE, 0
    )
    normed1_part = (
        contract(mixing_low, w_mix, 1, 1)
        + contract(rate_low, w_rates_wide, 1, 1)
        + contract(outgate_low, w_outgate, 1, 1)
    )
    grad_normed1 = scatter_sum(normed1_part.reshape(parts, quarter, model), "head")
    from_norm, grad_first_gain = norm_back(own_rows(inputs_f), gain1, grad_normed1)
    grad_input = place_rows(gather_near(grad_middle_own + from_norm, "head"), "head")
    grad_mix = contract(normed1_low, mixing_low, 0, 0)
    grad_rates = contract(normed1_low, rate_low, 0, 0)[:, :rate_lanes]
    grad_outgate = contract(normed1_low, outgate_low, 0, 0)

    seq = lax.axis_size("seq")
    seq_index = lax.axis_index("seq")
    split_rows = lambda array: array.reshape(seq, array.shape[0] // seq, array.shape[1])
    split_columns = lambda array: jnp.moveaxis(array.reshape(array.shape[0], seq, -1), 1, 0)
    ffn_sum = scatter_sum(split_rows(grad_ffn), "seq")
    down_sum = scatter_sum(split_columns(grad_down), "seq")
    out_sum = scatter_sum(split_columns(grad_out), "seq")
    mix_sum = scatter_sum(split_rows(grad_mix), "seq")
    outgate_sum = scatter_sum(split_rows(grad_outgate), "seq")
    rates_sum = lax.psum_scatter(grad_rates, "seq", scatter_dimension=0, tiled=True)
    taps_sum, decay_sum = lax.psum((grad_taps[:CONV], decay_sums[:2]), "seq")
    gains = lax.psum(
        (grad_first_gain, grad_second_gain, jnp.sum(grad_gain, 0)), ("seq", "head")
    )
    own_gain = lambda array: lax.dynamic_slice_in_dim(
        array, seq_index * (model // seq), model // seq, 0
    )
    decay_lanes = decay_sum[:, STEPS : heads * (STEPS + 1) : STEPS + 1]
    return (
        block_output,
        grad_input,
        own_gain(gains[0]),
        mix_sum,
        taps_sum,
        rates_sum,
        decay_lanes[0],
        decay_lanes[1],
        outgate_sum,
        gains[2],
        out_sum,
        own_gain(gains[1]),
        ffn_sum.reshape((-1,) + w_ffn.shape[1:]),
        down_sum,
    )


def solution(mesh):
    return jax.shard_map(
        body,
        mesh=mesh,
        in_specs=(
            P("seq", None),
            P(),
            P(None, "head"),
            P(None, "head"),
            P(None, "head"),
            P("head"),
            P("head"),
            P(None, "head"),
            P(),
            P("head", None),
            P(),
            P(None, None, "head"),
            P("head", None),
            P("seq", None),
            P("seq"),
        ),
        out_specs=(
            P("seq", None),
            P("seq", None),
            P("seq"),
            P("seq", "head"),
            P(None, "head"),
            P("seq", "head"),
            P("head"),
            P("head"),
            P("seq", "head"),
            P(),
            P("head", "seq"),
            P("seq"),
            P("seq", None, "head"),
            P("head", "seq"),
        ),
        check_vma=False,
    )
```

```python
from functools import partial

import jax
import jax.numpy as jnp
from jax import lax
from jax.experimental import pallas as pl
from jax.experimental.pallas import tpu as pltpu
from jax.sharding import PartitionSpec as P

STEPS = 2
CONV = 4
SPAN = 64
EDGE = 8
LANES = 128
GROUPS = 1 + 2 * STEPS
PACK = 4
DOCS = 4
EPSILON = 1e-06
VMEM_LIMIT = 56 * 1024 * 1024

F32 = jnp.float32
BF16 = jnp.bfloat16
NN = (1, 0)
NT = (1, 1)
TN = (0, 0)


def dot1(left, right, dims):
    return lax.dot_general(
        left.astype(BF16),
        right.astype(BF16),
        (((dims[0],), (dims[1],)), ((), ())),
        preferred_element_type=F32,
    )


def halves(value):
    high = value.astype(BF16)
    return high, (value - high.astype(F32)).astype(BF16)


def dot3(left, right, dims):
    left_high, left_low = halves(left)
    right_high, right_low = halves(right)
    return dot1(
        jnp.concatenate([left_high, left_low, left_high], dims[0]),
        jnp.concatenate([right_high, right_high, right_low], dims[1]),
        dims,
    )


def iota(shape, dim):
    return lax.broadcasted_iota(jnp.int32, shape, dim)


def twice(value):
    return jnp.concatenate([value, value], 0)


def spread(column):
    return jnp.broadcast_to(column, (column.shape[0], LANES))


def crossing(place, reach, offset):
    return (place < offset) & (offset <= place + reach)


def rate_parts(raw, rate_row, bias_row):
    shifted_raw = raw + bias_row
    soft = jnp.maximum(shifted_raw, 0.0) + jnp.log1p(jnp.exp(-jnp.abs(shifted_raw)))
    slope = -jnp.exp(rate_row)
    return jax.nn.sigmoid(raw), slope * soft, slope * jax.nn.sigmoid(shifted_raw)


def decay_parts(cumul, begin, offset):
    place = begin + iota(cumul.shape, 0)
    inside = offset >= begin
    carried = jnp.where(inside & (place >= offset), 0.0, jnp.exp(cumul))
    cut = (place < offset) & (offset <= begin + (SPAN - 1))
    tail = jnp.exp(jnp.where(cut, -1e30, cumul[SPAN - 1 :] - cumul))
    return carried, tail


def decay_ratio(cumul, begin, offset):
    across = jnp.transpose(twice(cumul))[:SPAN]
    row = iota(across.shape, 0)
    col = iota(across.shape, 1) & (SPAN - 1)
    cut = (begin + col < offset) & (offset <= begin + row)
    return jnp.exp(jnp.where((col <= row) & jnp.logical_not(cut), cumul - across, -1e30))


def strict_mask():
    shape = (STEPS * SPAN, STEPS * SPAN)
    row, col = iota(shape, 0), iota(shape, 1)
    row_tok, col_tok = row & (SPAN - 1), col & (SPAN - 1)
    strict = (col_tok < row_tok) | ((col_tok == row_tok) & (col < row))
    return strict, row_tok ^ col_tok, (row == col).astype(F32)


def local_kernel(
    heads,
    offset_ref,
    raw_ref,
    gain_ref,
    weight_ref,
    halo_ref,
    mix_ref,
    taps_ref,
    rates_ref,
    rate_row_ref,
    bias_row_ref,
    edge_ref,
    conv_ref,
    q_ref,
    k_ref,
    x_ref,
    n_ref,
    cumul_ref,
    u_ref,
    w_ref,
    score_ref,
    query_ref,
    prefix_ref,
    phi_ref,
    total_ref,
    run_ref,
):
    step = pl.program_id(0)
    rows = mix_ref.shape[0]
    offset = offset_ref[0]
    width = LANES
    strict, apart, eye = strict_mask()

    @pl.when(step == 0)
    def _():
        raw = raw_ref[...]
        scale = lax.rsqrt(jnp.mean(raw * raw, -1, keepdims=True) + EPSILON)
        edge_ref[...] = dot1(raw * scale * gain_ref[...], weight_ref[...], NN)
        run_ref[...] = jnp.concatenate([jnp.broadcast_to(eye, run_ref.shape[:2] + (width,)), jnp.zeros(run_ref.shape[:2] + (width,), F32)], 2)

    place = step * rows + iota((rows, width), 0)
    keep = [1.0 - crossing(place - back, back, offset).astype(F32) for back in range(CONV)]
    acts = []
    for part in range(heads * GROUPS):
        cols = slice(part * width, (part + 1) * width)
        before = jnp.where(step == 0, edge_ref[:, cols], halo_ref[:, cols])
        wide = jnp.concatenate([before, mix_ref[:, cols]], 0)
        conv = taps_ref[CONV - 1 : CONV, cols] * wide[EDGE:]
        for back in range(1, CONV):
            moved = pltpu.roll(wide, back, 0)[EDGE:]
            conv = conv + taps_ref[CONV - 1 - back : CONV - back, cols] * (moved * keep[back])
        conv_ref[:, cols] = conv
        act = conv * jax.nn.sigmoid(conv)
        if 1 <= part % GROUPS < 1 + STEPS:
            act = act * lax.rsqrt(jnp.sum(act * act, -1, keepdims=True) + EPSILON)
        acts.append(act)

    beta_all, decay_all, _ = rate_parts(rates_ref[...], rate_row_ref[...], bias_row_ref[...])
    lower = (iota((SPAN, SPAN), 1) <= iota((SPAN, SPAN), 0)).astype(F32)
    chains = [(pos, head) for pos in range(rows // SPAN) for head in range(heads)]
    cumuls = [
        jnp.dot(
            lower,
            decay_all[pos * SPAN : (pos + 1) * SPAN],
            precision=lax.Precision.HIGHEST,
            preferred_element_type=F32,
        )
        for pos in range(rows // SPAN)
    ]
    queries, keys, scaleds, tails, carries, ratios, systems = [], [], [], [], [], [], []
    for pos, head in chains:
        here = slice(pos * SPAN, (pos + 1) * SPAN)
        begin = step * rows + pos * SPAN
        query, key1, key2, value1, value2 = (
            act[here] for act in acts[head * GROUPS : (head + 1) * GROUPS]
        )
        key = jnp.concatenate([key1, key2], 0)
        value = jnp.concatenate([value1, value2], 0)
        lane = head * (STEPS + 1)
        beta = jnp.concatenate(
            [spread(beta_all[here, lane + sub : lane + sub + 1]) for sub in range(STEPS)], 0
        )
        cumul = spread(cumuls[pos][:, lane + STEPS : lane + STEPS + 1])
        cumul_ref[head, pos] = cumul
        carried, tail = decay_parts(cumul, begin, offset)
        ratio = decay_ratio(cumul, begin, offset)
        key_low = key.astype(BF16)
        q_ref[head, pos] = query
        k_ref[head, pos] = key_low
        queries.append(query)
        keys.append(key)
        tails.append(twice(tail))
        carries.append(carried)
        ratios.append(ratio)
        scaleds.append(jnp.concatenate([beta * value, beta * twice(carried) * key], 1))
        systems.append(jnp.where(strict, beta * twice(ratio), 0.0) * dot3(key, key, NT))
    inverses = [eye - jnp.where(apart == 0, system, 0.0) for system in systems]
    for level in range(SPAN.bit_length() - 1):
        off_blocks = [jnp.where((apart >> level) == 1, system, 0.0) for system in systems]
        lows = [inverse.astype(BF16) for inverse in inverses]
        halfway = [dot1(low, off, NN) for low, off in zip(lows, off_blocks)]
        inverses = [
            inverse - dot1(half, low, NN) for inverse, half, low in zip(inverses, halfway, lows)
        ]
    residues = [
        (eye - inverse) - dot3(system, inverse, NN) for inverse, system in zip(inverses, systems)
    ]
    inverses = [
        inverse + dot1(inverse, residue, NN) for inverse, residue in zip(inverses, residues)
    ]
    solveds = [dot3(inverse, scaled, NN) for inverse, scaled in zip(inverses, scaleds)]
    all_scores = [ratio * dot3(query, key, NT) for ratio, query, key in zip(ratios, queries, keys)]
    all_maps = [
        dot3(
            key,
            jnp.concatenate([tail * solved[:, width:], tail * solved[:, :width]], 1),
            TN,
        )
        for key, tail, solved in zip(keys, tails, solveds)
    ]
    inner = [dot1(scores, solved[:, width:], NN) for scores, solved in zip(all_scores, solveds)]
    for index, (pos, head) in enumerate(chains):
        solved, maps, carried = solveds[index], all_maps[index], carries[index]
        phi = carried[SPAN - 1 :] * eye - maps[:, :width]
        x_ref[head, pos] = inverses[index].astype(BF16)
        n_ref[head, pos] = systems[index].astype(BF16)
        u_ref[head, pos] = solved[:, :width]
        w_ref[head, pos] = solved[:, width:]
        score_ref[head, pos] = all_scores[index]
        query_ref[head, pos] = carried * queries[index] - inner[index]
        phi_ref[head, pos] = phi
        run = run_ref[head]
        prefix_ref[head, pos] = run
        moved_run = dot3(phi, run, NN)
        run_ref[head] = jnp.concatenate(
            [moved_run[:, :width], moved_run[:, width:] + maps[:, width:]], 1
        )
    total_ref[...] = run_ref[...]


def specs_of(heads, pack):
    def per_block(*dims):
        return pl.BlockSpec((heads, pack) + dims, lambda g: (0, g) + (0,) * len(dims))

    return per_block


def whole(shape):
    return pl.BlockSpec(shape, lambda g: (0,) * len(shape))


SCALARS = pl.BlockSpec(memory_space=pltpu.SMEM)


def params():
    return pltpu.CompilerParams(vmem_limit_bytes=VMEM_LIMIT)


LIGHT = pl.CostEstimate(flops=1, bytes_accessed=1, transcendentals=0)


def local_maps(offset, raw, gain, weight, mixing, taps, rates, rate_row, bias_row):
    rows, columns = mixing.shape
    width = LANES
    heads = columns // (GROUPS * width)
    blocks = rows // SPAN
    virt = STEPS * SPAN
    tile = PACK * SPAN
    per_block = specs_of(heads, PACK)
    saved = [
        (per_block(SPAN, width), (SPAN, width), F32),
        (per_block(virt, width), (virt, width), BF16),
        (per_block(virt, virt), (virt, virt), BF16),
        (per_block(virt, virt), (virt, virt), BF16),
        (per_block(SPAN, width), (SPAN, width), F32),
        (per_block(virt, width), (virt, width), F32),
        (per_block(virt, width), (virt, width), F32),
        (per_block(SPAN, virt), (SPAN, virt), F32),
        (per_block(SPAN, width), (SPAN, width), F32),
        (per_block(width, 2 * width), (width, 2 * width), F32),
        (per_block(width, width), (width, width), F32),
    ]
    return pl.pallas_call(
        partial(local_kernel, heads),
        grid=(blocks // PACK,),
        in_specs=[
            SCALARS,
            whole(raw.shape),
            whole(gain.shape),
            whole(weight.shape),
            pl.BlockSpec((EDGE, columns), lambda g: (jnp.maximum(g * (tile // EDGE) - 1, 0), 0)),
            pl.BlockSpec((tile, columns), lambda g: (g, 0)),
            whole(taps.shape),
            pl.BlockSpec((tile, LANES), lambda g: (g, 0)),
            whole((1, LANES)),
            whole((1, LANES)),
        ],
        out_specs=[whole((EDGE, columns)), pl.BlockSpec((tile, columns), lambda g: (g, 0))]
        + [spec for spec, _, _ in saved]
        + [whole((heads, width, 2 * width))],
        out_shape=[
            jax.ShapeDtypeStruct((EDGE, columns), F32),
            jax.ShapeDtypeStruct((rows, columns), F32),
        ]
        + [jax.ShapeDtypeStruct((heads, blocks) + dims, kind) for _, dims, kind in saved]
        + [jax.ShapeDtypeStruct((heads, width, 2 * width), F32)],
        scratch_shapes=[pltpu.VMEM((heads, width, 2 * width), F32)],
        compiler_params=params(),
        cost_estimate=LIGHT,
        name="local_maps",
    )(offset, raw, gain, weight, mixing, mixing, taps, rates, rate_row, bias_row)


def output_kernel(
    heads,
    offset_ref,
    incoming_ref,
    prefix_ref,
    u_ref,
    w_ref,
    score_ref,
    q_ref,
    cumul_ref,
    outgate_ref,
    gain_ref,
    state_ref,
    fresh_ref,
    mixed_ref,
    gated_ref,
):
    step = pl.program_id(0)
    pack = prefix_ref.shape[1]
    width = LANES
    offset = offset_ref[0]
    chains = [(pos, head) for pos in range(pack) for head in range(heads)]
    states = [
        dot3(prefix_ref[head, pos, :, :width], incoming_ref[head], NN)
        + prefix_ref[head, pos, :, width:]
        for pos, head in chains
    ]
    freshes = [
        u_ref[head, pos] - dot3(w_ref[head, pos], state, NN)
        for (pos, head), state in zip(chains, states)
    ]
    outs = []
    for (pos, head), state, fresh in zip(chains, states, freshes):
        carried, _ = decay_parts(cumul_ref[head, pos], (step * pack + pos) * SPAN, offset)
        outs.append(
            dot3(
                jnp.concatenate([carried * q_ref[head, pos], score_ref[head, pos]], 1),
                jnp.concatenate([state, fresh], 0),
                NN,
            )
        )
    for (pos, head), state, fresh, mixed in zip(chains, states, freshes, outs):
        here = slice(pos * SPAN, (pos + 1) * SPAN)
        cols = slice(head * width, (head + 1) * width)
        state_ref[head, pos] = state.astype(BF16)
        fresh_ref[head, pos] = fresh.astype(BF16)
        mixed_ref[here, cols] = mixed
        scale = lax.rsqrt(jnp.mean(mixed * mixed, -1, keepdims=True) + EPSILON)
        outgate = outgate_ref[here, cols]
        gated = mixed * scale * gain_ref[...] * (outgate * jax.nn.sigmoid(outgate))
        gated_ref[here, cols] = gated.astype(BF16).astype(gated_ref.dtype)


def outputs_of(offset, incoming, saved, outgate, gain, gated_type):
    prefix, u, w, scores, q, cumul = saved
    heads, blocks = prefix.shape[:2]
    width = LANES
    virt = STEPS * SPAN
    tile = PACK * SPAN
    rows = outgate.shape[0]
    per_block = specs_of(heads, PACK)
    flat = pl.BlockSpec((tile, heads * width), lambda g: (g, 0))
    return pl.pallas_call(
        partial(output_kernel, heads),
        grid=(blocks // PACK,),
        in_specs=[
            SCALARS,
            whole((heads, width, width)),
            per_block(width, 2 * width),
            per_block(virt, width),
            per_block(virt, width),
            per_block(SPAN, virt),
            per_block(SPAN, width),
            per_block(SPAN, width),
            flat,
            whole((1, width)),
        ],
        out_specs=[per_block(width, width), per_block(virt, width), flat, flat],
        out_shape=[
            jax.ShapeDtypeStruct((heads, blocks, width, width), BF16),
            jax.ShapeDtypeStruct((heads, blocks, virt, width), BF16),
            jax.ShapeDtypeStruct((rows, heads * width), F32),
            jax.ShapeDtypeStruct((rows, heads * width), gated_type),
        ],
        compiler_params=params(),
        cost_estimate=LIGHT,
        name="mixer_outputs",
    )(offset, incoming, prefix, u, w, scores, q, cumul, outgate, gain)


def gate_back_kernel(
    heads,
    parts,
    place_ref,
    *refs,
):
    piece_refs = refs[:parts]
    (
        weight_ref,
        mixed_ref,
        outgate_ref,
        gain_ref,
        query_ref,
        prefix_ref,
        branch_ref,
        grad_mixed_ref,
        grad_outgate_ref,
        grad_gain_ref,
        term_ref,
        total_ref,
        sum_ref,
    ) = refs[parts:]
    step = pl.program_id(0)
    pack = prefix_ref.shape[1]
    width = LANES
    rows = branch_ref.shape[0]

    @pl.when(step == 0)
    def _():
        sum_ref[...] = sum(ref[rows:] for ref in piece_refs)
        grad_gain_ref[...] = jnp.zeros_like(grad_gain_ref)
        total_ref[...] = jnp.zeros_like(total_ref)

    for near in range(parts):

        @pl.when(step == near)
        def _():
            branch_ref[...] = piece_refs[near][:rows].astype(BF16)

    grad_all = dot1(branch_ref[...], weight_ref[...], NT)
    gain = gain_ref[...]
    grads_mixed = []
    for head in range(heads):
        cols = slice(head * width, (head + 1) * width)
        mixed = mixed_ref[:, cols]
        outgate = outgate_ref[:, cols]
        grad = grad_all[:, cols]
        scale = lax.rsqrt(jnp.mean(mixed * mixed, -1, keepdims=True) + EPSILON)
        normed = mixed * scale
        sigma = jax.nn.sigmoid(outgate)
        silu = outgate * sigma
        grad_outgate = grad * normed * gain * (sigma * (1.0 + outgate * (1.0 - sigma)))
        grad_outgate_ref[:, cols] = grad_outgate.astype(BF16)
        through = grad * silu
        product = through * normed
        grad_gain_ref[...] += jnp.sum(product.reshape(-1, 8, width), 0)
        grad_normed = through * gain
        grad_mixed = scale * (
            grad_normed - normed * jnp.mean(grad_normed * normed, -1, keepdims=True)
        )
        grad_mixed_ref[:, cols] = grad_mixed.astype(BF16)
        grads_mixed.append(grad_mixed)
    chains = [(pos, head) for pos in range(pack) for head in range(heads)]
    terms = [
        dot3(query_ref[head, pos], grads_mixed[head][pos * SPAN : (pos + 1) * SPAN], TN)
        for pos, head in chains
    ]
    moved = [dot3(prefix_ref[head, pos], term, TN) for (pos, head), term in zip(chains, terms)]
    totals = [total_ref[head] for head in range(heads)]
    for (pos, head), term, part in zip(chains, terms, moved):
        term_ref[head, pos] = term
        totals[head] = totals[head] + part
    for head in range(heads):
        total_ref[head] = totals[head]


def gate_back(place, pieces, weight, mixed, outgate, gain, query, prefix):
    heads, blocks = prefix.shape[:2]
    width = LANES
    parts = len(pieces)
    model = pieces[0].shape[1]
    rows = mixed.shape[0]
    tile = rows // parts
    pack = tile // SPAN

    def fixed(*shape):
        return pl.BlockSpec(shape, lambda g, at: (0,) * len(shape))

    def per_block(*dims):
        return pl.BlockSpec((heads, pack) + dims, lambda g, at: (0, at[g]) + (0,) * len(dims))

    def flat(size):
        return pl.BlockSpec((tile, size), lambda g, at: (at[g], 0))

    return pl.pallas_call(
        partial(gate_back_kernel, heads, parts),
        grid_spec=pltpu.PrefetchScalarGridSpec(
            num_scalar_prefetch=1,
            grid=(parts,),
            in_specs=[fixed(tile + EDGE, model)] * parts
            + [
                fixed(*weight.shape),
                flat(heads * width),
                flat(heads * width),
                fixed(1, width),
                per_block(SPAN, width),
                per_block(width, width),
            ],
            out_specs=[
                flat(model),
                flat(heads * width),
                flat(heads * width),
                fixed(8, width),
                per_block(width, width),
                fixed(heads, width, width),
                fixed(EDGE, model),
            ],
        ),
        out_shape=[
            jax.ShapeDtypeStruct((rows, model), BF16),
            jax.ShapeDtypeStruct((rows, heads * width), BF16),
            jax.ShapeDtypeStruct((rows, heads * width), BF16),
            jax.ShapeDtypeStruct((8, width), F32),
            jax.ShapeDtypeStruct((heads, blocks, width, width), F32),
            jax.ShapeDtypeStruct((heads, width, width), F32),
            jax.ShapeDtypeStruct((EDGE, model), F32),
        ],
        compiler_params=params(),
        cost_estimate=LIGHT,
        name="gate_back",
    )(place, *pieces, weight, mixed, outgate, gain, query, prefix)


def place_kernel(parts, place_ref, *refs):
    out_ref, sum_ref = refs[parts:]
    rows = refs[0].shape[0] - EDGE
    for near in range(parts):
        here = pl.ds(pl.multiple_of(place_ref[near] * rows, rows), rows)
        out_ref[here] = refs[near][:rows].astype(out_ref.dtype)
    sum_ref[...] = sum(ref[rows:] for ref in refs[:parts])


def place_rows(place, pieces, kind):
    parts = len(pieces)
    rows, columns = pieces[0].shape
    return pl.pallas_call(
        partial(place_kernel, parts),
        in_specs=[SCALARS] + [IN_VMEM] * parts,
        out_specs=[IN_VMEM, IN_VMEM],
        out_shape=[
            jax.ShapeDtypeStruct((parts * (rows - EDGE), columns), kind),
            jax.ShapeDtypeStruct((EDGE, columns), F32),
        ],
        compiler_params=params(),
        cost_estimate=LIGHT,
        name="place_rows",
    )(place, *pieces)


def low_weight_kernel(*refs):
    refs[-2][...] = jnp.concatenate([ref[...].astype(BF16) for ref in refs[:-3]], 0)


def low_weight(pieces, passed):
    depth, columns = pieces[0].shape
    steps = 2
    return pl.pallas_call(
        low_weight_kernel,
        grid=(steps,),
        in_specs=[pl.BlockSpec((depth, columns // steps), lambda g: (0, g))] * len(pieces)
        + [pl.BlockSpec(memory_space=pl.ANY)],
        out_specs=[
            pl.BlockSpec((depth * len(pieces), columns // steps), lambda g: (0, g)),
            pl.BlockSpec(memory_space=pl.ANY),
        ],
        out_shape=[
            jax.ShapeDtypeStruct((depth * len(pieces), columns), BF16),
            jax.ShapeDtypeStruct(passed.shape, passed.dtype),
        ],
        input_output_aliases={len(pieces): 1},
        compiler_params=params(),
        cost_estimate=LIGHT,
        name="low_weight",
    )(*pieces, passed)


def first_kernel(
    input_ref,
    gain_ref,
    mix_ref,
    rates_ref,
    outgate_ref,
    normed_ref,
    mixing_ref,
    rates_out_ref,
    outgate_out_ref,
):
    values = input_ref[...].astype(F32)
    scale = lax.rsqrt(jnp.mean(values * values, -1, keepdims=True) + EPSILON)
    normed = (values * scale * gain_ref[...]).astype(BF16)
    normed_ref[...] = normed
    mixing_ref[...] = dot1(normed, mix_ref[...], NN)
    rates_out_ref[...] = dot1(normed, rates_ref[...], NN)
    outgate_out_ref[...] = dot1(normed, outgate_ref[...], NN)


def first_projections(block_input, gain, w_mix, w_rates, w_outgate):
    rows, model = block_input.shape
    steps = 4
    tile = rows // steps
    flat = lambda size: pl.BlockSpec((tile, size), lambda g: (g, 0))
    weights = (w_mix, w_rates, w_outgate)
    return pl.pallas_call(
        first_kernel,
        grid=(steps,),
        in_specs=[flat(model), whole((1, model))] + [whole(weight.shape) for weight in weights],
        out_specs=[flat(model)] + [flat(weight.shape[1]) for weight in weights],
        out_shape=[jax.ShapeDtypeStruct((rows, model), BF16)]
        + [jax.ShapeDtypeStruct((rows, weight.shape[1]), F32) for weight in weights],
        compiler_params=params(),
        cost_estimate=LIGHT,
        name="first_projections",
    )(block_input, gain, *weights)


def dense_kernel(parts, *refs):
    gated_refs = refs[1 : 1 + parts]
    (
        weight_ref,
        input_ref,
        gain_ref,
        ffn_ref,
        down_ref,
        grad_ref,
    ) = refs[1 + parts : 7 + parts]
    (
        middle_ref,
        normed_ref,
        activ_ref,
        *some_refs,
        back_ref,
        fore_ref,
    ) = refs[-6 - len(CUTS) :]
    hidden = down_ref.shape[0]
    gated = jnp.concatenate([ref[...].astype(BF16) for ref in gated_refs], 1)
    middle = input_ref[...].astype(F32) + dot1(gated, weight_ref[...], NN)
    middle_ref[...] = middle
    scale = lax.rsqrt(jnp.mean(middle * middle, -1, keepdims=True) + EPSILON)
    normed = (middle * scale * gain_ref[...]).astype(BF16)
    normed_ref[...] = normed
    both = dot1(normed, ffn_ref[...], NN)
    gate, up = both[:, :hidden], both[:, hidden:]
    grad_activ = dot1(grad_ref[...], down_ref[...], NT)
    sigma = jax.nn.sigmoid(gate)
    silu = gate * sigma
    activ = (silu * up).astype(BF16)
    activ_ref[:, :hidden] = activ
    activ_ref[:, hidden:] = jnp.zeros_like(activ_ref[:, hidden:])
    grad_gate = grad_activ * up * (sigma * (1.0 + gate * (1.0 - sigma)))
    grad_both = jnp.concatenate([grad_gate, grad_activ * silu], 1).astype(BF16)
    for ref, low, high in zip(some_refs, (0,) + CUTS, CUTS + (2 * hidden,)):
        ref[...] = grad_both[:, low:high]
    back_ref[...] = dot1(grad_both, ffn_ref[...], NT)
    fore_ref[...] = dot1(activ, down_ref[...], NN)


DENSE_STEPS = 2
CUTS = (384, 768)


def dense_half(half, gated_near, weight, block_input, gain, ffn, w_down, grad, filled):
    parts = len(gated_near)
    rows, model = block_input.shape
    steps = DENSE_STEPS
    tile = rows // (2 * steps)
    depth = gated_near[0].shape[1]
    hidden = w_down.shape[0]

    def fixed(*shape):
        return pl.BlockSpec(shape, lambda g, at: (0,) * len(shape))

    def flat(size):
        return pl.BlockSpec((tile, size), lambda g, at: (at[0] * steps + g, 0))

    sizes = [
        (model, F32),
        (model, BF16),
        (hidden + -hidden % LANES, BF16),
    ] + [(high - low, BF16) for low, high in zip((0,) + CUTS, CUTS + (2 * hidden,))]
    operands = [half, *gated_near, weight, block_input, gain, ffn, w_down, grad]
    in_specs = [flat(depth)] * parts + [
        fixed(parts * depth, model),
        flat(model),
        fixed(1, model),
        fixed(model, 2 * hidden),
        fixed(hidden, model),
        flat(model),
    ]
    aliases = {}
    if filled is not None:
        aliases = {len(operands) + index: index for index in range(len(filled))}
        in_specs = in_specs + [pl.BlockSpec(memory_space=pl.ANY)] * len(filled)
        operands = operands + list(filled)
    return pl.pallas_call(
        partial(dense_kernel, parts),
        grid_spec=pltpu.PrefetchScalarGridSpec(
            num_scalar_prefetch=1,
            grid=(steps,),
            in_specs=in_specs,
            out_specs=[flat(size) for size, _ in sizes]
            + [pl.BlockSpec((tile, model), lambda g, at: (g, 0))] * 2,
        ),
        out_shape=[jax.ShapeDtypeStruct((rows, size), kind) for size, kind in sizes]
        + [jax.ShapeDtypeStruct((rows // 2, model), F32)] * 2,
        input_output_aliases=aliases,
        compiler_params=params(),
        cost_estimate=LIGHT,
        name="dense_half",
    )(*operands)


def first_back_kernel(count, place_ref, *refs):
    grad_refs, weight_refs = refs[:count], refs[count : 2 * count]
    sent_ref, kept_ref = refs[2 * count :]
    result = sum(
        dot1(grad_ref[...], weight_ref[...], NT)
        for grad_ref, weight_ref in zip(grad_refs, weight_refs)
    )
    half = pl.num_programs(0) // 2

    @pl.when(pl.program_id(0) < half)
    def _():
        sent_ref[...] = result

    @pl.when(pl.program_id(0) >= half)
    def _():
        kept_ref[...] = result


def first_back(half, grads, weights):
    rows = grads[0].shape[0]
    model = weights[0].shape[0]
    steps = 4
    tile = rows // steps
    side = steps // 2

    def rows_at(g, at):
        kept = (g >= side).astype(jnp.int32)
        return (kept * at[0] + (1 - kept) * (1 - at[0])) * side + g - kept * side

    def spec_of(grad):
        return pl.BlockSpec((tile, grad.shape[1]), lambda g, at: (rows_at(g, at), 0))

    return pl.pallas_call(
        partial(first_back_kernel, len(grads)),
        grid_spec=pltpu.PrefetchScalarGridSpec(
            num_scalar_prefetch=1,
            grid=(steps,),
            in_specs=[spec_of(grad) for grad in grads]
            + [pl.BlockSpec(weight.shape, lambda g, at: (0, 0)) for weight in weights],
            out_specs=[
                pl.BlockSpec((tile, model), lambda g, at: (jnp.minimum(g, side - 1), 0)),
                pl.BlockSpec((tile, model), lambda g, at: (jnp.maximum(g - side, 0), 0)),
            ],
        ),
        out_shape=[jax.ShapeDtypeStruct((rows // 2, model), F32)] * 2,
        compiler_params=params(),
        cost_estimate=LIGHT,
        name="first_back",
    )(half, *grads, *weights)


def back_kernel(
    heads,
    offset_ref,
    leaving_ref,
    term_ref,
    phi_ref,
    state_ref,
    fresh_ref,
    grad_ref,
    score_ref,
    x_ref,
    n_ref,
    cumul_ref,
    q_ref,
    k_ref,
    rates_ref,
    rate_row_ref,
    bias_row_ref,
    conv_ref,
    edge_ref,
    halo_ref,
    mix_ref,
    taps_ref,
    grad_mix_ref,
    last_ref,
    before_ref,
    grad_rates_ref,
    decay_sum_ref,
    grad_taps_ref,
    run_ref,
    next_ref,
    act_ref,
):
    step = pl.program_id(0)
    steps = pl.num_programs(0)
    group = steps - 1 - step
    rows = mix_ref.shape[0]
    offset = offset_ref[0]
    width = LANES
    virt = STEPS * SPAN
    strict, _, _ = strict_mask()
    lane = iota((SPAN, width), 1)

    @pl.when(step == 0)
    def _():
        run_ref[...] = leaving_ref[...]
        next_ref[...] = jnp.zeros_like(next_ref)
        decay_sum_ref[...] = jnp.zeros_like(decay_sum_ref)
        grad_taps_ref[...] = jnp.zeros_like(grad_taps_ref)

    tok_row, tok_col = iota((SPAN, SPAN), 0), iota((SPAN, SPAN), 1)
    later = (tok_col >= tok_row).astype(BF16)
    earlier = tok_col < tok_row
    sums = jnp.concatenate([later, earlier.astype(BF16)], 1)
    beta_all, decay_all, slope_all = rate_parts(
        rates_ref[...], rate_row_ref[...], bias_row_ref[...]
    )
    chains = [(pos, head) for pos in reversed(range(rows // SPAN)) for head in range(heads)]
    leavings = []
    for pos, head in chains:
        leaving = run_ref[head]
        leavings.append(leaving)
        run_ref[head] = dot3(phi_ref[head, pos], leaving, TN) + term_ref[head, pos]
    betas, parts_of, ratios, masked = [], [], [], []
    for pos, head in chains:
        here = slice(pos * SPAN, (pos + 1) * SPAN)
        begin = group * rows + pos * SPAN
        first_lane = head * (STEPS + 1)
        beta = jnp.concatenate(
            [
                spread(beta_all[here, first_lane + sub : first_lane + sub + 1])
                for sub in range(STEPS)
            ],
            0,
        )
        cumul = cumul_ref[head, pos]
        betas.append(beta)
        parts_of.append(decay_parts(cumul, begin, offset))
        ratio = decay_ratio(cumul, begin, offset)
        ratios.append(ratio)
        masked.append(jnp.where(strict, beta * twice(ratio), 0.0))
    lows = [leaving.astype(BF16) for leaving in leavings]
    grads = [
        grad_ref[pos * SPAN : (pos + 1) * SPAN, head * width : (head + 1) * width]
        for pos, head in chains
    ]
    scores_low = [score_ref[head, pos].astype(BF16) for pos, head in chains]
    states = [state_ref[head, pos] for pos, head in chains]
    freshes = [fresh_ref[head, pos] for pos, head in chains]
    queries = [q_ref[head, pos] for pos, head in chains]
    keys = [k_ref[head, pos] for pos, head in chains]
    key_leavings = [
        twice(tail) * dot1(key, low, NN) for key, low, (_, tail) in zip(keys, lows, parts_of)
    ]
    grad_freshes = [
        dot1(scores, grad, TN) + key_leaving
        for scores, grad, key_leaving in zip(scores_low, grads, key_leavings)
    ]
    solveds = [
        dot1(x_ref[head, pos], grad_fresh, TN)
        for (pos, head), grad_fresh in zip(chains, grad_freshes)
    ]
    scaleds = [beta * solved for beta, solved in zip(betas, solveds)]
    grad_scores = [dot1(grad, fresh, NT) for grad, fresh in zip(grads, freshes)]
    grad_systems = [-dot1(solved, fresh, NT) for solved, fresh in zip(solveds, freshes)]
    grad_states = [
        carried * dot1(grad, state, NT)
        for grad, state, (carried, _) in zip(grads, states, parts_of)
    ]
    scaled_states = [
        twice(carried) * dot1(scaled, state, NT)
        for scaled, state, (carried, _) in zip(scaleds, states, parts_of)
    ]
    boths = [
        jnp.concatenate([grad_score * ratio, grad_system * mask], 0).astype(BF16)
        for grad_score, ratio, grad_system, mask in zip(grad_scores, ratios, grad_systems, masked)
    ]
    from_keys = [dot1(both, key, NN) for both, key in zip(boths, keys)]
    to_keys = [
        dot1(both, jnp.concatenate([query.astype(BF16), key], 0), TN)
        for both, query, key in zip(boths, queries, keys)
    ]
    from_leavings = [
        twice(tail) * dot1(fresh, low, NT) for fresh, low, (_, tail) in zip(freshes, lows, parts_of)
    ]
    all_pairs = []
    for index, (pos, head) in enumerate(chains):
        system_pairs = grad_systems[index] * n_ref[head, pos].astype(F32)
        pairs = grad_scores[index] * score_ref[head, pos]
        pairs = pairs + system_pairs[:SPAN] + system_pairs[SPAN:]
        all_pairs.append(pairs[:, :SPAN] + pairs[:, SPAN:])
    crossed = [jnp.where(earlier, dot1(later, pairs, NN), 0.0) for pairs in all_pairs]
    all_ends = []
    for index, (pos, head) in enumerate(chains):
        read = scaled_states[index] * keys[index].astype(F32)
        arriving = grad_states[index] * queries[index] - read[:SPAN] - read[SPAN:]
        written = key_leavings[index] * freshes[index].astype(F32)
        written = written[:SPAN] + written[SPAN:]
        all_ends.append(dot1(sums, jnp.concatenate([arriving, written], 0), NN))
    rates_of = [jnp.zeros((SPAN, width), F32) for _ in range(rows // SPAN)]
    for index, (pos, head) in enumerate(chains):
        here = slice(pos * SPAN, (pos + 1) * SPAN)
        first_lane = head * (STEPS + 1)
        grad_query = from_keys[index][:SPAN] + grad_states[index]
        grad_key = (
            from_keys[index][SPAN:]
            - scaled_states[index]
            + to_keys[index]
            + from_leavings[index]
        )
        scaled = scaleds[index]
        for place_of, part in enumerate(
            (grad_query, grad_key[:SPAN], grad_key[SPAN:], scaled[:SPAN], scaled[SPAN:])
        ):
            at = (head * GROUPS + place_of) * width
            act_ref[here, at : at + width] = part
        fresh = freshes[index].astype(F32)
        step_part = (1.0 - betas[index]) * jnp.sum(solveds[index] * fresh, -1, keepdims=True)
        kept = parts_of[index][0][SPAN - 1 :] * jnp.sum(
            leavings[index] * states[index].astype(F32), 0, keepdims=True
        )
        grad_decay = jnp.sum(crossed[index], -1, keepdims=True) + jnp.sum(
            all_ends[index] + kept, -1, keepdims=True
        )
        for sub in range(STEPS):
            rates_of[pos] = jnp.where(
                lane == first_lane + sub,
                step_part[sub * SPAN : (sub + 1) * SPAN],
                rates_of[pos],
            )
        rates_of[pos] = jnp.where(lane == first_lane + STEPS, spread(grad_decay), rates_of[pos])
    is_decay = lane % (STEPS + 1) == STEPS
    for pos, grad_rates in enumerate(rates_of):
        here = slice(pos * SPAN, (pos + 1) * SPAN)
        decay_part = jnp.where(is_decay, grad_rates * decay_all[here], 0.0)
        grad_rates = jnp.where(is_decay, grad_rates * slope_all[here], grad_rates)
        grad_rates_ref[here] = grad_rates.astype(BF16)
        decay_sum_ref[0:1] += jnp.sum(decay_part, 0, keepdims=True)
        decay_sum_ref[1:2] += jnp.sum(jnp.where(is_decay, grad_rates, 0.0), 0, keepdims=True)

    place = group * rows + iota((rows, width), 0)
    keep_back = [1.0 - crossing(place - back, back, offset).astype(F32) for back in range(CONV)]
    keep_fore = [1.0 - crossing(place, fore, offset).astype(F32) for fore in range(CONV)]
    edge_place = iota((EDGE, width), 0) - EDGE
    keep_edge = [1.0 - crossing(edge_place, fore, offset).astype(F32) for fore in range(CONV)]
    for part in range(heads * GROUPS):
        cols = slice(part * width, (part + 1) * width)
        conv = conv_ref[:, cols]
        grad = act_ref[:, cols]
        sigma = jax.nn.sigmoid(conv)
        if 1 <= part % GROUPS < 1 + STEPS:
            act = conv * sigma
            scale = lax.rsqrt(jnp.sum(act * act, -1, keepdims=True) + EPSILON)
            unit = act * scale
            grad = scale * (grad - unit * jnp.sum(unit * grad, -1, keepdims=True))
        grad_conv = grad * (sigma * (1.0 + conv * (1.0 - sigma)))
        wide = jnp.concatenate([grad_conv, next_ref[:, cols]], 0)
        before = jnp.concatenate([jnp.zeros((EDGE, width), F32), grad_conv[:EDGE]], 0)
        above = jnp.where(group == 0, edge_ref[:, cols], halo_ref[:, cols])
        mix_wide = jnp.concatenate([above, mix_ref[:, cols]], 0)
        tap = taps_ref[CONV - 1 : CONV, cols]
        grad_mix = tap * grad_conv
        grad_before = jnp.zeros((EDGE, width), F32)
        sums_of = jnp.sum(grad_conv * mix_wide[EDGE:], 0, keepdims=True)
        grad_taps_ref[CONV - 1 : CONV, cols] += sums_of
        for shift in range(1, CONV):
            tap = taps_ref[CONV - 1 - shift : CONV - shift, cols]
            moved = pltpu.roll(wide, rows + EDGE - shift, 0)[:rows]
            grad_mix = grad_mix + tap * (moved * keep_fore[shift])
            moved = pltpu.roll(before, 2 * EDGE - shift, 0)[:EDGE]
            grad_before = grad_before + tap * (moved * keep_edge[shift])
            moved = pltpu.roll(mix_wide, shift, 0)[EDGE:] * keep_back[shift]
            grad_taps_ref[CONV - 1 - shift : CONV - shift, cols] += jnp.sum(
                grad_conv * moved, 0, keepdims=True
            )
        next_ref[:, cols] = grad_conv[:EDGE]
        grad_mix_ref[:, cols] = grad_mix.astype(BF16)
        before_ref[:, cols] = grad_before

        @pl.when(step == 0)
        def _():
            last_ref[:, cols] = grad_mix[rows - 2 * EDGE :]


def recurrence_back(offset, leaving, saved, rates, rate_row, bias_row, conv, edge, mixing, taps):
    term, phi, state, fresh, grad, scores, x, n, cumul, q, k = saved
    rows, columns = mixing.shape
    heads, blocks = term.shape[:2]
    width = LANES
    virt = STEPS * SPAN
    tile = PACK * SPAN
    steps = blocks // PACK

    def per_block(*dims):
        return pl.BlockSpec(
            (heads, PACK) + dims, lambda g: (0, steps - 1 - g) + (0,) * len(dims)
        )

    def flat(size):
        return pl.BlockSpec((tile, size), lambda g: (steps - 1 - g, 0))

    return pl.pallas_call(
        partial(back_kernel, heads),
        grid=(steps,),
        in_specs=[
            SCALARS,
            whole((heads, width, width)),
            per_block(width, width),
            per_block(width, width),
            per_block(width, width),
            per_block(virt, width),
            flat(heads * width),
            per_block(SPAN, virt),
            per_block(virt, virt),
            per_block(virt, virt),
            per_block(SPAN, width),
            per_block(SPAN, width),
            per_block(virt, width),
            flat(LANES),
            whole((1, LANES)),
            whole((1, LANES)),
            flat(columns),
            whole((EDGE, columns)),
            pl.BlockSpec(
                (EDGE, columns),
                lambda g: (jnp.maximum((steps - 1 - g) * (tile // EDGE) - 1, 0), 0),
            ),
            flat(columns),
            whole(taps.shape),
        ],
        out_specs=[
            flat(columns),
            whole((2 * EDGE, columns)),
            whole((EDGE, columns)),
            flat(LANES),
            whole((8, LANES)),
            whole((8, columns)),
        ],
        out_shape=[
            jax.ShapeDtypeStruct((rows, columns), BF16),
            jax.ShapeDtypeStruct((2 * EDGE, columns), F32),
            jax.ShapeDtypeStruct((EDGE, columns), F32),
            jax.ShapeDtypeStruct((rows, LANES), BF16),
            jax.ShapeDtypeStruct((8, LANES), F32),
            jax.ShapeDtypeStruct((8, columns), F32),
        ],
        scratch_shapes=[
            pltpu.VMEM((heads, width, width), F32),
            pltpu.VMEM((EDGE, columns), F32),
            pltpu.VMEM((tile, columns), F32),
        ],
        compiler_params=params(),
        cost_estimate=LIGHT,
        name="recurrence_back",
    )(
        offset, leaving, term, phi, state, fresh, grad, scores, x, n, cumul, q, k,
        rates, rate_row, bias_row, conv, edge, mixing, mixing, taps,
    )


def piece_at(index, total, low, mine, bit):
    half = total // 2
    later = (index >= half).astype(jnp.int32)
    rest = index - later * half
    side = (mine // bit) % 2
    picked = later * side + (1 - later) * (1 - side)
    return ((rest >> low) << (low + 1)) | (picked << low) | (rest & ((1 << low) - 1))


def sent_at(index, total):
    return jnp.minimum(index, total // 2 - 1)


def kept_at(index, total):
    return jnp.maximum(index - total // 2, 0)


def grad_kernel(half, pairs, *refs):
    sent_ref, kept_ref = refs[-2:]
    depth = sent_ref.shape[1]

    def put(out_ref):
        place = 0
        for index in range(pairs):
            first = 1 + index * (half + 1)
            left = jnp.concatenate([ref[...] for ref in refs[first : first + half]], 1)
            right_ref = refs[first + half]
            size = right_ref.shape[1]
            result = dot1(left, right_ref[...], TN)
            for piece in range(half):
                out_ref[piece, :, place : place + size] = result[piece * depth : (piece + 1) * depth]
            place += size

    @pl.when(pl.program_id(0) == 0)
    def _():
        put(sent_ref)

    @pl.when(pl.program_id(0) == 1)
    def _():
        put(kept_ref)


def weight_grad(mine, bit, total, pairs):
    low = bit.bit_length() - 1
    half = total // 2
    rows = pairs[0][0].shape[0]
    depth = pairs[0][0].shape[1] // total

    def pick(piece):
        return lambda g, at: (0, piece_at(g * half + piece, total, low, at[0], bit))

    def fixed(place):
        return lambda g, at: (0, place)

    in_specs, operands, width = [], [], 0
    for left, right, place, size in pairs:
        in_specs += [pl.BlockSpec((rows, depth), pick(piece)) for piece in range(half)]
        in_specs.append(pl.BlockSpec((rows, size), fixed(place)))
        operands += [left] * half + [right]
        width += size
    out = (half, depth, width)
    return pl.pallas_call(
        partial(grad_kernel, half, len(pairs)),
        grid_spec=pltpu.PrefetchScalarGridSpec(
            num_scalar_prefetch=1,
            grid=(2,),
            in_specs=in_specs,
            out_specs=[pl.BlockSpec(out, lambda g, at: (0, 0, 0))] * 2,
        ),
        out_shape=[jax.ShapeDtypeStruct(out, F32)] * 2,
        compiler_params=params(),
        cost_estimate=LIGHT,
        name="weight_grad",
    )(mine, *operands)


def down_grad_kernel(grad_ref, activ_ref, out_ref):
    out_ref[...] = dot1(grad_ref[...], activ_ref[...], TN)


def down_grad(grad, activ):
    rows, model = grad.shape
    steps = 4
    tile = model // steps
    return pl.pallas_call(
        down_grad_kernel,
        grid=(steps,),
        in_specs=[pl.BlockSpec((rows, tile), lambda g: (0, g)), whole(activ.shape)],
        out_specs=pl.BlockSpec((tile, activ.shape[1]), lambda g: (g, 0)),
        out_shape=jax.ShapeDtypeStruct((model, activ.shape[1]), F32),
        compiler_params=params(),
        cost_estimate=LIGHT,
        name="down_grad",
    )(grad, activ)


def combine_kernel(bit, mine_ref, kept_ref, arrived_ref, sent_ref, next_ref):
    side = (mine_ref[0] // bit) % 2
    sent_ref[...] = (kept_ref[:, 1 - side] + arrived_ref[:, 1 - side]).reshape(sent_ref.shape)
    next_ref[...] = (kept_ref[:, side] + arrived_ref[:, side]).reshape(next_ref.shape)


IN_VMEM = pl.BlockSpec(memory_space=pltpu.VMEM)


def combine(mine, bit, low, kept, arrived):
    total, rows, columns = kept.shape
    half = total // 2
    view = lambda array: array.reshape((half >> low, 2, 1 << low, rows, columns))
    return pl.pallas_call(
        partial(combine_kernel, bit),
        in_specs=[SCALARS, IN_VMEM, IN_VMEM],
        out_specs=[IN_VMEM, IN_VMEM],
        out_shape=[jax.ShapeDtypeStruct((half, rows, columns), F32)] * 2,
        compiler_params=params(),
        cost_estimate=LIGHT,
        name="combine",
    )(mine, view(kept), view(arrived))


def norm_back_kernel(
    place_ref, kept_ref, arrived_ref, value_ref, gain_ref, residual_ref, out_ref
):
    step = pl.program_id(0)
    tile = kept_ref.shape[0]
    rows = out_ref.shape[0] - EDGE
    values = value_ref[...].astype(F32)
    grad = kept_ref[...] + arrived_ref[...]
    scale = lax.rsqrt(jnp.mean(values * values, -1, keepdims=True) + EPSILON)
    normed = values * scale
    through = grad * gain_ref[...]
    back = scale * (through - normed * jnp.mean(through * normed, -1, keepdims=True))
    out_ref[pl.ds(pl.multiple_of(step * tile, tile), tile)] = back + residual_ref[...].astype(F32)
    sums = jnp.sum((grad * normed).reshape(-1, EDGE, grad.shape[1]), 0)

    @pl.when(step == 0)
    def _():
        out_ref[rows:] = sums

    @pl.when(step != 0)
    def _():
        out_ref[rows:] += sums


def norm_back(place, kept, arrived, values, gain, residual):
    rows, model = kept.shape
    steps = 2
    tile = rows // steps
    local = pl.BlockSpec((tile, model), lambda g, at: (g, 0))

    def spec_of(array):
        if array.shape[0] == rows + EDGE:
            return local
        return pl.BlockSpec((tile, model), lambda g, at: (at[0] * steps + g, 0))

    return pl.pallas_call(
        norm_back_kernel,
        grid_spec=pltpu.PrefetchScalarGridSpec(
            num_scalar_prefetch=1,
            grid=(steps,),
            in_specs=[
                local,
                local,
                spec_of(values),
                pl.BlockSpec((1, model), lambda g, at: (0, 0)),
                spec_of(residual),
            ],
            out_specs=pl.BlockSpec((rows + EDGE, model), lambda g, at: (0, 0)),
        ),
        out_shape=jax.ShapeDtypeStruct((rows + EDGE, model), F32),
        compiler_params=params(),
        cost_estimate=LIGHT,
        name="norm_back",
    )(place, kept, arrived, values, gain, residual)


def own_output_kernel(kept_ref, arrived_ref, middle_ref, gain_ref, out_ref):
    rows, model = kept_ref.shape
    width = gain_ref.shape[1]
    out_ref[:rows] = kept_ref[...] + arrived_ref[...] + middle_ref[...]
    out_ref[rows:] = jnp.concatenate(
        [gain_ref[...], jnp.zeros((EDGE, model - width), F32)], 1
    )


def own_output(place, kept, arrived, middle, grad_gain):
    rows, model = kept.shape
    return pl.pallas_call(
        lambda place_ref, *refs: own_output_kernel(*refs),
        grid_spec=pltpu.PrefetchScalarGridSpec(
            num_scalar_prefetch=1,
            grid=(1,),
            in_specs=[
                pl.BlockSpec((rows, model), lambda g, at: (0, 0)),
                pl.BlockSpec((rows, model), lambda g, at: (0, 0)),
                pl.BlockSpec((rows, model), lambda g, at: (at[0], 0)),
                pl.BlockSpec(grad_gain.shape, lambda g, at: (0, 0)),
            ],
            out_specs=pl.BlockSpec((rows + EDGE, model), lambda g, at: (0, 0)),
        ),
        out_shape=jax.ShapeDtypeStruct((rows + EDGE, model), F32),
        compiler_params=params(),
        cost_estimate=LIGHT,
        name="own_output",
    )(place, kept, arrived, middle, grad_gain)


def pack_kernel(heads, first_ref, second_ref, gain_ref, *refs):
    decay_refs, taps_refs, out_ref = refs[:heads], refs[heads : 2 * heads], refs[-1]
    place = 0
    for ref in (first_ref, second_ref):
        for start in range(0, ref.shape[1], LANES):
            out_ref[place : place + 1] = jnp.sum(ref[:, start : start + LANES], 0, keepdims=True)
            place += 1
    for ref in taps_refs:
        for start in range(0, ref.shape[1], LANES):
            out_ref[place : place + EDGE] = ref[:, start : start + LANES]
            place += EDGE
    out_ref[place : place + EDGE] = gain_ref[:, :LANES]
    out_ref[place + EDGE : place + 2 * EDGE] = sum(ref[...] for ref in decay_refs)


def pack_small(first, second, gain, decays, taps):
    columns = sum(part.shape[1] for part in taps)
    rows = 2 * (first.shape[1] // LANES) + EDGE * (columns // LANES) + 2 * EDGE
    return pl.pallas_call(
        partial(pack_kernel, len(taps)),
        out_shape=jax.ShapeDtypeStruct((rows, LANES), F32),
        compiler_params=params(),
        cost_estimate=LIGHT,
        name="pack_small",
    )(first, second, gain, *decays, *taps)


def unpack_kernel(
    mine_ref, small_ref, first_ref, second_ref, gain_ref, decay_ref, taps_ref, *, count, model
):
    blocks = model // LANES
    size = model // count
    index = mine_ref[0]
    for base, ref in ((0, first_ref), (blocks, second_ref)):
        row = small_ref[pl.ds(base + index * size // LANES, 1)]
        if size < LANES:
            row = pltpu.roll(row, (LANES - index * size % LANES) % LANES, 1)
        ref[...] = row[:, :size]
    place = 2 * blocks
    for start in range(0, taps_ref.shape[1], LANES):
        taps_ref[:, start : start + LANES] = small_ref[place : place + CONV]
        place += EDGE
    gain_ref[...] = jnp.sum(small_ref[place : place + EDGE], 0, keepdims=True)
    decay_ref[...] = small_ref[place + EDGE : place + 2 * EDGE]


def unpack_small(mine, small, count, model, columns):
    size = model // count
    shapes = [(1, size), (1, size), (1, LANES), (EDGE, LANES), (CONV, columns)]
    return pl.pallas_call(
        partial(unpack_kernel, count=count, model=model),
        in_specs=[SCALARS, IN_VMEM],
        out_shape=[jax.ShapeDtypeStruct(shape, F32) for shape in shapes],
        compiler_params=params(),
        cost_estimate=LIGHT,
        name="unpack_small",
    )(mine, small)


def exchange(value, axis, bit):
    count = lax.axis_size(axis)
    return lax.ppermute(value, axis, [(place, place ^ bit) for place in range(count)])


def shifted(value, axis, steps):
    count = lax.axis_size(axis)
    first, last = (max(0, -steps), min(count, count - steps))
    return lax.ppermute(value, axis, [(source, source + steps) for source in range(first, last)])


def bits_of(axis):
    count = lax.axis_size(axis)
    return [1 << power for power in range(count.bit_length() - 1)]


class GatherNear:
    def __init__(self, value, axis):
        self.axis = axis
        self.bits = bits_of(axis)
        self.found = {0: value}
        for bit in self.bits[::-1]:
            self.found[bit] = exchange(value, axis, bit)

    def finish(self, *others):
        for bit in self.bits[::-1]:
            if others and bit == self.bits[-1]:
                self.found[bit] = after(self.found[bit], *others)
            for near in sorted(self.found):
                if near > bit and not near & bit and near | bit not in self.found:
                    self.found[near | bit] = exchange(self.found[near], self.axis, bit)
        return [self.found[near] for near in sorted(self.found)]


def gather_near(value, axis, *others):
    start = GatherNear(value, axis)
    others = sum([list(one()) if callable(one) else [one] for one in others], [])
    return start.finish(*others)


def after(value, *others):
    return lax.optimization_barrier((value,) + others)[0]


def join(*values):
    return lax.optimization_barrier(values)


class Scatter:
    def __init__(self, mine, axis, order, kept, sent):
        self.mine = mine
        self.axis = axis
        self.bits = sorted(order)
        self.order = list(order)
        self.kept = kept
        self.sent = sent

    def send(self):
        bit = self.order.pop(0)
        self.bits.remove(bit)
        self.arrived = exchange(self.sent, self.axis, bit)
        self.sent = None
        return self

    def add(self):
        if self.order:
            bit = self.order[0]
            self.sent, self.kept = combine(
                self.mine, bit, self.bits.index(bit), self.kept, self.arrived
            )
        else:
            self.total = self.kept[0] + self.arrived[0]
        return self

    def step(self):
        self.add()
        return self.send() if self.order else self


class WholeSum:
    def __init__(self, pairs):
        self.kept = self.sent = jnp.concatenate(
            [
                contract(left, lax.slice_in_dim(right, place * size, (place + 1) * size, axis=1), 0, 0)
                for left, right, place, size in pairs
            ],
            1,
        )
        self.order = []

    def send(self):
        self.arrived = lax.psum_scatter(self.sent, "seq", scatter_dimension=0, tiled=True)
        return self

    def add(self):
        self.total = self.kept = self.arrived
        return self

    def step(self):
        return self.add()


def arrive(*scatters, also=()):
    found = join(*[one.arrived for one in scatters], *also)
    for one, value in zip(scatters, found):
        one.arrived = value
    return found[len(scatters) :]


def contract(left, right, left_dim, right_dim):
    return lax.dot_general(
        left, right, (((left_dim,), (right_dim,)), ((), ())), preferred_element_type=F32
    )


def carried_in(total, own, axis, backward, maps=None):
    count = lax.axis_size(axis)
    sign = -1 if backward else 1
    reach = count - DOCS - 1
    if reach > DOCS - 1:
        reach = count - 1
    dims = (1, 1) if backward else (2, 1)
    width = LANES

    def move(map_of, state):
        return lax.dot_general(
            map_of, state, (((dims[0],), (1,)), ((0,), (0,))), precision=lax.Precision.HIGHEST
        )

    if reach < count - 1:
        if own is None:
            both = [shifted(total, axis, sign * step) for step in range(1, reach)]
            maps = [pair[..., :width] for pair in both]
            terms = [pair[..., width:] for pair in both]
            terms.append(shifted(total[..., width:], axis, sign * reach))
        else:
            terms = [shifted(own, axis, sign * step) for step in range(1, reach + 1)]
    else:
        every_map = lax.all_gather(total[..., :width], axis)
        every_term = lax.all_gather(total[..., width:] if own is None else own, axis)
        mine = lax.axis_index(axis)

        def at(array, step):
            place = mine - sign * step
            picked = lax.dynamic_index_in_dim(array, jnp.clip(place, 0, count - 1), 0, False)
            return jnp.where((place >= 0) & (place < count), picked, 0.0)

        maps = [at(every_map, step) for step in range(1, reach)]
        terms = [at(every_term, step) for step in range(1, reach + 1)]
    state = terms[-1]
    for map_of, term in zip(reversed(maps), reversed(terms[:-1])):
        state = move(map_of, state) + term
    return state


def maps_between(total, axis):
    count = lax.axis_size(axis)
    reach = count - DOCS - 1
    if reach > DOCS - 1:
        return None
    return [shifted(total[..., :LANES], axis, -step) for step in range(1, reach)]


def normalize(values):
    return values * lax.rsqrt(jnp.mean(values * values, -1, keepdims=True) + EPSILON)


def lanes_of(per_head):
    row = jnp.repeat(per_head, STEPS + 1)
    return jnp.pad(row, (0, LANES - row.shape[0]))[None]


def body(
    block_input,
    first_gain,
    w_mix,
    conv_taps,
    w_rates,
    log_rate,
    rate_bias,
    w_outgate,
    head_gain,
    w_out,
    second_gain,
    w_ffn,
    w_down,
    grad_output,
    seq_starts,
):
    rows, model = block_input.shape
    heads = log_rate.shape[0]
    parts = lax.axis_size("head")
    quarter = rows // parts
    head_index = lax.axis_index("head")
    seq, seq_index = lax.axis_size("seq"), lax.axis_index("seq")
    gain1, gain2 = first_gain.astype(F32), second_gain.astype(F32)
    head_gain_row = head_gain.astype(F32)[None]
    taps = conv_taps.astype(F32)
    rate_row, bias_row = lanes_of(log_rate), lanes_of(rate_bias)
    rate_lanes = w_rates.shape[1]
    w_rates_wide = jnp.pad(w_rates, ((0, 0), (0, LANES - rate_lanes)))
    ffn_flat = w_ffn.reshape(model, -1)

    head_bits = bits_of("head")
    core = head_index % 2
    kept_half, sent_half = core[None], (1 - core)[None]

    def block_of(index):
        return sum(
            ((index // bit) % 2) * (parts // (2 * bit)) for bit in head_bits
        )

    places = jnp.stack([block_of(head_index ^ near) for near in range(parts)]).astype(jnp.int32)
    own_block = places[0]
    own_rows = lambda array: lax.dynamic_slice_in_dim(array, own_block * quarter, quarter, 0)

    head_mine, seq_mine = head_index[None], seq_index[None]
    head_order, seq_bits = head_bits, bits_of("seq")

    raw_edge = shifted(block_input[rows - EDGE :].astype(F32), "seq", 1)
    normed1_low, mixing, rates, outgate = first_projections(
        block_input, gain1[None], w_mix, w_rates_wide, w_outgate
    )
    w_out_near = gather_near(w_out.astype(F32), "head")
    edge, conv, q, k, x, system, cumul, u, w, scores, query_map, prefix, phi, total = local_maps(
        seq_starts, raw_edge, gain1[None], w_mix, mixing, taps, rates, rate_row, bias_row
    )
    width = LANES
    incoming = carried_in(total, None, "seq", False)
    state, fresh, mixed, gated = outputs_of(
        seq_starts, incoming, (prefix, u, w, scores, q, cumul), outgate, head_gain_row, F32
    )
    gated_start = GatherNear(gated, "head")
    w_out_low, ffn_flat = low_weight([after(piece, gated) for piece in w_out_near], ffn_flat)
    maps = maps_between(after(total, gated), "seq") or ()
    ffn_flat, w_out_low, *maps = join(ffn_flat, w_out_low, *maps)
    gated_near = gated_start.finish(ffn_flat, w_out_low)

    dense = lambda half, filled: dense_half(
        half, gated_near, w_out_low, block_input, gain2[None], ffn_flat, w_down, grad_output, filled
    )
    *filled, back_sent, fore_sent = dense(sent_half, None)
    split = lambda half: half.reshape(parts // 2, quarter, model)
    back = Scatter(head_mine, "head", head_order, None, split(back_sent)).send()
    *filled, back_kept, fore_kept = dense(kept_half, filled)
    middle, normed2_low, activ_low, *grads_both = filled
    back.kept = split(back_kept)
    back.step()

    near_first, far_first = seq_bits, seq_bits[1:] + seq_bits[:1]
    tiled = model // seq % LANES == 0

    def grad_sum(order, *pairs, tie=()):
        (left, *rest), *others = pairs
        pairs = [(after(left, *tie), *rest)] + others
        if not tiled:
            return WholeSum(pairs)
        sent, kept = weight_grad(seq_mine, order[0], seq, pairs)
        return Scatter(seq_mine, "seq", order, kept, sent)

    ffn_sums, tie = [], back.kept
    for order, right in zip((near_first, far_first, near_first), grads_both):
        ffn_sums.append(grad_sum(order, (normed2_low, right, 0, right.shape[1]), tie=(tie,)))
        tie = ffn_sums[-1].kept
    ffn_one, ffn_two, ffn_three = ffn_sums
    ffn_one.send()
    ffn_two.send()
    fore = Scatter(
        head_mine, "head", head_order, split(fore_kept), after(split(fore_sent), back.kept)
    ).send()
    down_sum = grad_sum(
        near_first, (grad_output, activ_low, 0, activ_low.shape[1]), tie=(ffn_three.kept,)
    )
    ffn_three.sent, down_sum.sent = arrive(
        back, fore, ffn_one, ffn_two, also=(ffn_three.sent, down_sum.sent)
    )
    grad_middle_own = norm_back(
        places[:1], back.kept[0], back.arrived[0], middle, gain2[None], grad_output
    )

    middle_start = GatherNear(grad_middle_own, "head")
    ffn_three.sent = after(ffn_three.sent, grad_middle_own)
    ffn_three.send()
    tie = grad_middle_own
    for one in (ffn_one, ffn_two):
        one.arrived = after(one.arrived, tie)
        one.step()
        tie = one.kept
    fore.arrived = after(fore.arrived, tie)
    fore.add()
    middle_start.found[2], fore.sent = arrive(
        *ffn_sums, also=(middle_start.found[2], fore.sent)
    )

    fore.send()
    grad_branch, grad_mixed, outgate_low, grad_gain, term, grad_total, grad_second_gain = gate_back(
        places, middle_start.finish(), w_out, mixed, outgate, head_gain_row, query_map, prefix
    )
    leaving = carried_in(total, grad_total, "seq", True, maps)
    out_width, outgate_width = gated.shape[1], outgate_low.shape[1]
    side_sum = grad_sum(
        near_first,
        (grad_branch, gated.astype(BF16), 0, out_width),
        (normed1_low, outgate_low, 0, outgate_width),
        tie=(grad_total,),
    )
    tie = side_sum.kept
    for one in (ffn_three, ffn_one):
        one.arrived = after(one.arrived, tie)
        one.add()
        tie = one.kept
    leaving, side_sum.sent, ffn_three.sent, ffn_one.sent, down_sum.sent = arrive(
        fore, also=(leaving, side_sum.sent, ffn_three.sent, ffn_one.sent, down_sum.sent)
    )
    output_own = own_output(places[:1], fore.kept[0], fore.arrived[0], middle, grad_gain)

    output_start = GatherNear(output_own, "head")
    down_sum.send()
    ffn_three.send()
    ffn_one.send()
    leaving, output_start.found[1] = join(after(leaving, output_own), output_start.found[1])
    grad_mix_rows, last_rows, before_rows, rate_low, decay_sums, grad_taps = recurrence_back(
        seq_starts,
        leaving,
        (term, phi, state, fresh, grad_mixed, scores, x, system, cumul, q, k),
        rates,
        rate_row,
        bias_row,
        conv,
        edge,
        mixing,
        taps,
    )
    before_rows, output_start.found[2] = arrive(
        ffn_one, ffn_three, down_sum, also=(before_rows, output_start.found[2])
    )

    returned = shifted(before_rows, "seq", -1)
    down_sum.add()
    ffn_three.arrived = after(ffn_three.arrived, down_sum.kept)
    ffn_three.add()
    returned, side_sum.sent, down_sum.sent, ffn_three.sent = join(
        returned, side_sum.sent, down_sum.sent, ffn_three.sent
    )
    for one in (side_sum, down_sum, ffn_three):
        one.send()
    last_rows = last_rows + jnp.pad(returned, ((EDGE, 0), (0, 0)))
    mixing_low = lax.dynamic_update_slice_in_dim(
        grad_mix_rows, last_rows.astype(BF16), rows - 2 * EDGE, 0
    )
    columns = mixing_low.shape[1]
    half_columns, narrow = columns // 2, columns // 10
    mix_one = grad_sum(near_first, (normed1_low, mixing_low, 0, half_columns))
    part_sent, part_kept = first_back(
        kept_half,
        (after(mixing_low, mix_one.kept), outgate_low, rate_low),
        (w_mix, w_outgate, w_rates_wide),
    )
    output_near = output_start.finish()
    part_sent, part_kept, mix_one.sent, *output_near = arrive(
        side_sum, down_sum, ffn_three,
        also=(part_sent, part_kept, mix_one.sent, *output_near),
    )
    part = Scatter(head_mine, "head", head_order, split(part_kept), split(part_sent)).send()
    part.step()
    mix_one.send()
    tie = part.kept
    for one in (side_sum, down_sum):
        one.arrived = after(one.arrived, tie)
        one.step()
        tie = one.kept

    mix_two = grad_sum(
        near_first,
        *[(normed1_low, mixing_low, 5 + piece, narrow) for piece in range(3)],
        tie=(tie,),
    ).send()
    output, grad_head_gain = place_rows(
        places, [after(piece, mix_two.kept) for piece in output_near], BF16
    )
    mix_three = grad_sum(
        near_first,
        *[(normed1_low, mixing_low, 8 + piece, narrow) for piece in range(2)],
        (normed1_low, rate_low, 0, LANES),
        tie=(output,),
    )
    mix_one.arrived = after(mix_one.arrived, mix_three.kept)
    mix_one.step()
    mix_three.sent, _ = arrive(
        part, side_sum, down_sum, also=(mix_three.sent, mix_one.kept)
    )
    grad_input_own = norm_back(
        places[:1], part.kept[0], part.arrived[0], block_input, gain1[None], grad_middle_own
    )

    input_start = GatherNear(grad_input_own, "head")
    mix_three.sent, side_sum.arrived, _ = join(mix_three.sent, side_sum.arrived, grad_input_own)
    mix_three.send()
    tie = grad_input_own
    for one in (side_sum, mix_two):
        one.arrived = after(one.arrived, tie)
        one.step()
        tie = one.kept
    mix_one.arrived, side_sum.arrived, _ = join(mix_one.arrived, side_sum.arrived, tie)
    mix_one.step()
    input_start.found[2], tie = arrive(
        mix_two, mix_three, also=(input_start.found[2], mix_one.kept)
    )
    for one in (mix_three, mix_two):
        one.step()
    grad_input, grad_first_gain = place_rows(places, input_start.finish(), F32)
    ffn_two.arrived, mix_three.arrived, _ = join(ffn_two.arrived, mix_three.arrived, grad_input)
    ffn_two.step()
    small = pack_small(
        grad_first_gain,
        grad_second_gain,
        grad_head_gain,
        [decay_sums],
        [grad_taps],
    )
    for bit in seq_bits:
        small = small + exchange(small, "seq", bit)
    gain1_own, gain2_own, gain_sum, decay_sum, taps_sum = unpack_small(
        seq_mine, small, seq, model, mixing.shape[1]
    )
    decay_lanes = decay_sum[:, STEPS : heads * (STEPS + 1) : STEPS + 1]

    def total_of(one):
        while one.order:
            one.step()
        return one.add().total

    side_total = total_of(side_sum)
    ffn_total = jnp.concatenate([total_of(one) for one in ffn_sums], 1)
    mix_total = jnp.concatenate([total_of(one) for one in (mix_one, mix_two, mix_three)], 1)
    return (
        output,
        grad_input,
        gain1_own[0],
        mix_total[:, :columns],
        taps_sum,
        mix_total[:, columns : columns + rate_lanes],
        decay_lanes[0],
        decay_lanes[1],
        side_total[:, out_width:],
        gain_sum[0],
        side_total[:, :out_width].T,
        gain2_own[0],
        ffn_total.reshape((-1,) + w_ffn.shape[1:]),
        total_of(down_sum)[:, : w_down.shape[0]].T,
    )


def solution(mesh):
    return jax.shard_map(
        body,
        mesh=mesh,
        in_specs=(
            P("seq", None),
            P(),
            P(None, "head"),
            P(None, "head"),
            P(None, "head"),
            P("head"),
            P("head"),
            P(None, "head"),
            P(),
            P("head", None),
            P(),
            P(None, None, "head"),
            P("head", None),
            P("seq", None),
            P("seq"),
        ),
        out_specs=(
            P("seq", None),
            P("seq", None),
            P("seq"),
            P("seq", "head"),
            P(None, "head"),
            P("seq", "head"),
            P("head"),
            P("head"),
            P("seq", "head"),
            P(),
            P("head", "seq"),
            P("seq"),
            P("seq", None, "head"),
            P("head", "seq"),
        ),
        check_vma=False,
    )
```

```python
from functools import partial

import jax
import jax.numpy as jnp
from jax import lax
from jax.experimental import pallas as pl
from jax.experimental.pallas import tpu as pltpu
from jax.sharding import PartitionSpec as P

STEPS = 2
CONV = 4
SPAN = 64
EDGE = 8
LANES = 128
GROUPS = 1 + 2 * STEPS
PACK = 4
DOCS = 4
EPSILON = 1e-06
VMEM_LIMIT = 56 * 1024 * 1024

F32 = jnp.float32
BF16 = jnp.bfloat16
NN = (1, 0)
NT = (1, 1)
TN = (0, 0)


def dot1(left, right, dims):
    return lax.dot_general(
        left.astype(BF16),
        right.astype(BF16),
        (((dims[0],), (dims[1],)), ((), ())),
        preferred_element_type=F32,
    )


def halves(value):
    high = value.astype(BF16)
    return high, (value - high.astype(F32)).astype(BF16)


def dot3(left, right, dims):
    left_high, left_low = halves(left)
    right_high, right_low = halves(right)
    return dot1(
        jnp.concatenate([left_high, left_low, left_high], dims[0]),
        jnp.concatenate([right_high, right_high, right_low], dims[1]),
        dims,
    )


def iota(shape, dim):
    return lax.broadcasted_iota(jnp.int32, shape, dim)


def twice(value):
    return jnp.concatenate([value, value], 0)


def spread(column):
    return jnp.broadcast_to(column, (column.shape[0], LANES))


def crossing(place, reach, offset):
    return (place < offset) & (offset <= place + reach)


def lane_row(ref, heads):
    lane = iota((1, LANES), 1)
    row = jnp.zeros((1, LANES), F32)
    for head in range(heads):
        here = (lane >= head * (STEPS + 1)) & (lane < (head + 1) * (STEPS + 1))
        row = jnp.where(here, ref[head], row)
    return row


def rate_parts(raw, rate_row, bias_row):
    shifted_raw = raw + bias_row
    soft = jnp.maximum(shifted_raw, 0.0) + jnp.log1p(jnp.exp(-jnp.abs(shifted_raw)))
    slope = -jnp.exp(rate_row)
    return jax.nn.sigmoid(raw), slope * soft, slope * jax.nn.sigmoid(shifted_raw)


def decay_parts(cumul, begin, offset):
    place = begin + iota(cumul.shape, 0)
    inside = offset >= begin
    carried = jnp.where(inside & (place >= offset), 0.0, jnp.exp(cumul))
    cut = (place < offset) & (offset <= begin + (SPAN - 1))
    tail = jnp.exp(jnp.where(cut, -1e30, cumul[SPAN - 1 :] - cumul))
    return carried, tail


def decay_ratio(cumul, begin, offset):
    across = jnp.transpose(twice(cumul))[:SPAN]
    row = iota(across.shape, 0)
    col = iota(across.shape, 1) & (SPAN - 1)
    cut = (begin + col < offset) & (offset <= begin + row)
    return jnp.exp(jnp.where((col <= row) & jnp.logical_not(cut), cumul - across, -1e30))


def strict_mask():
    shape = (STEPS * SPAN, STEPS * SPAN)
    row, col = iota(shape, 0), iota(shape, 1)
    row_tok, col_tok = row & (SPAN - 1), col & (SPAN - 1)
    strict = (col_tok < row_tok) | ((col_tok == row_tok) & (col < row))
    return strict, row_tok ^ col_tok, (row == col).astype(F32)


def local_kernel(
    heads,
    offset_ref,
    log_rate_ref,
    rate_bias_ref,
    edge_ref,
    halo_ref,
    mix_ref,
    taps_ref,
    rates_ref,
    conv_ref,
    q_ref,
    k_ref,
    x_ref,
    n_ref,
    cumul_ref,
    u_ref,
    w_ref,
    score_ref,
    query_ref,
    prefix_ref,
    phi_ref,
    total_ref,
    run_ref,
):
    step = pl.program_id(0)
    rows = mix_ref.shape[0]
    offset = offset_ref[0]
    width = LANES
    strict, apart, eye = strict_mask()

    @pl.when(step == 0)
    def _():
        run_ref[...] = jnp.concatenate([jnp.broadcast_to(eye, run_ref.shape[:2] + (width,)), jnp.zeros(run_ref.shape[:2] + (width,), F32)], 2)

    place = step * rows + iota((rows, width), 0)
    keep = [1.0 - crossing(place - back, back, offset).astype(F32) for back in range(CONV)]
    acts = []
    for part in range(heads * GROUPS):
        cols = slice(part * width, (part + 1) * width)
        before = jnp.where(step == 0, edge_ref[:, cols], halo_ref[:, cols])
        wide = jnp.concatenate([before, mix_ref[:, cols]], 0)
        taps = taps_ref[:, cols].astype(F32)
        conv = taps[CONV - 1 : CONV] * wide[EDGE:]
        for back in range(1, CONV):
            moved = pltpu.roll(wide, back, 0)[EDGE:]
            conv = conv + taps[CONV - 1 - back : CONV - back] * (moved * keep[back])
        conv_ref[:, cols] = conv
        act = conv * jax.nn.sigmoid(conv)
        if 1 <= part % GROUPS < 1 + STEPS:
            act = act * lax.rsqrt(jnp.sum(act * act, -1, keepdims=True) + EPSILON)
        acts.append(act)

    beta_all, decay_all, _ = rate_parts(
        rates_ref[...], lane_row(log_rate_ref, heads), lane_row(rate_bias_ref, heads)
    )
    lower = (iota((SPAN, SPAN), 1) <= iota((SPAN, SPAN), 0)).astype(F32)
    chains = [(pos, head) for pos in range(rows // SPAN) for head in range(heads)]
    cumuls = [
        jnp.dot(
            lower,
            decay_all[pos * SPAN : (pos + 1) * SPAN],
            precision=lax.Precision.HIGHEST,
            preferred_element_type=F32,
        )
        for pos in range(rows // SPAN)
    ]
    queries, keys, scaleds, tails, carries, ratios, systems = [], [], [], [], [], [], []
    for pos, head in chains:
        here = slice(pos * SPAN, (pos + 1) * SPAN)
        begin = step * rows + pos * SPAN
        query, key1, key2, value1, value2 = (
            act[here] for act in acts[head * GROUPS : (head + 1) * GROUPS]
        )
        key = jnp.concatenate([key1, key2], 0)
        value = jnp.concatenate([value1, value2], 0)
        lane = head * (STEPS + 1)
        beta = jnp.concatenate(
            [spread(beta_all[here, lane + sub : lane + sub + 1]) for sub in range(STEPS)], 0
        )
        cumul = spread(cumuls[pos][:, lane + STEPS : lane + STEPS + 1])
        cumul_ref[head, pos] = cumul
        carried, tail = decay_parts(cumul, begin, offset)
        ratio = decay_ratio(cumul, begin, offset)
        key_low = key.astype(BF16)
        q_ref[head, pos] = query
        k_ref[head, pos] = key_low
        queries.append(query)
        keys.append(key)
        tails.append(twice(tail))
        carries.append(carried)
        ratios.append(ratio)
        scaleds.append(jnp.concatenate([beta * value, beta * twice(carried) * key], 1))
        systems.append(jnp.where(strict, beta * twice(ratio), 0.0) * dot3(key, key, NT))
    inverses = [eye - jnp.where(apart == 0, system, 0.0) for system in systems]
    for level in range(SPAN.bit_length() - 1):
        off_blocks = [jnp.where((apart >> level) == 1, system, 0.0) for system in systems]
        lows = [inverse.astype(BF16) for inverse in inverses]
        halfway = [dot1(low, off, NN) for low, off in zip(lows, off_blocks)]
        inverses = [
            inverse - dot1(half, low, NN) for inverse, half, low in zip(inverses, halfway, lows)
        ]
    residues = [
        (eye - inverse) - dot3(system, inverse, NN) for inverse, system in zip(inverses, systems)
    ]
    inverses = [
        inverse + dot1(inverse, residue, NN) for inverse, residue in zip(inverses, residues)
    ]
    solveds = [dot3(inverse, scaled, NN) for inverse, scaled in zip(inverses, scaleds)]
    all_scores = [ratio * dot3(query, key, NT) for ratio, query, key in zip(ratios, queries, keys)]
    all_maps = [
        dot3(
            key,
            jnp.concatenate([tail * solved[:, width:], tail * solved[:, :width]], 1),
            TN,
        )
        for key, tail, solved in zip(keys, tails, solveds)
    ]
    inner = [dot1(scores, solved[:, width:], NN) for scores, solved in zip(all_scores, solveds)]
    for index, (pos, head) in enumerate(chains):
        solved, maps, carried = solveds[index], all_maps[index], carries[index]
        phi = carried[SPAN - 1 :] * eye - maps[:, :width]
        x_ref[head, pos] = inverses[index].astype(BF16)
        n_ref[head, pos] = systems[index].astype(BF16)
        u_ref[head, pos] = solved[:, :width]
        w_ref[head, pos] = solved[:, width:]
        score_ref[head, pos] = all_scores[index]
        query_ref[head, pos] = carried * queries[index] - inner[index]
        phi_ref[head, pos] = phi
        run = run_ref[head]
        prefix_ref[head, pos] = run
        moved_run = dot3(phi, run, NN)
        run_ref[head] = jnp.concatenate(
            [moved_run[:, :width], moved_run[:, width:] + maps[:, width:]], 1
        )
    total_ref[...] = run_ref[...]


def specs_of(heads, pack):
    def per_block(*dims):
        return pl.BlockSpec((heads, pack) + dims, lambda g: (0, g) + (0,) * len(dims))

    return per_block


def whole(shape):
    return pl.BlockSpec(shape, lambda g: (0,) * len(shape))


SCALARS = pl.BlockSpec(memory_space=pltpu.SMEM)


def params():
    return pltpu.CompilerParams(vmem_limit_bytes=VMEM_LIMIT)


LIGHT = pl.CostEstimate(flops=1, bytes_accessed=1, transcendentals=0)


def local_maps(offset, log_rate, rate_bias, edge, mixing, taps, rates):
    rows, columns = mixing.shape
    width = LANES
    heads = columns // (GROUPS * width)
    blocks = rows // SPAN
    virt = STEPS * SPAN
    tile = PACK * SPAN
    per_block = specs_of(heads, PACK)
    saved = [
        (per_block(SPAN, width), (SPAN, width), F32),
        (per_block(virt, width), (virt, width), BF16),
        (per_block(virt, virt), (virt, virt), BF16),
        (per_block(virt, virt), (virt, virt), BF16),
        (per_block(SPAN, width), (SPAN, width), F32),
        (per_block(virt, width), (virt, width), F32),
        (per_block(virt, width), (virt, width), F32),
        (per_block(SPAN, virt), (SPAN, virt), F32),
        (per_block(SPAN, width), (SPAN, width), F32),
        (per_block(width, 2 * width), (width, 2 * width), F32),
        (per_block(width, width), (width, width), F32),
    ]
    return pl.pallas_call(
        partial(local_kernel, heads),
        grid=(blocks // PACK,),
        in_specs=[
            SCALARS,
            SCALARS,
            SCALARS,
            whole((EDGE, columns)),
            pl.BlockSpec((EDGE, columns), lambda g: (jnp.maximum(g * (tile // EDGE) - 1, 0), 0)),
            pl.BlockSpec((tile, columns), lambda g: (g, 0)),
            whole(taps.shape),
            pl.BlockSpec((tile, LANES), lambda g: (g, 0)),
        ],
        out_specs=[pl.BlockSpec((tile, columns), lambda g: (g, 0))]
        + [spec for spec, _, _ in saved]
        + [whole((heads, width, 2 * width))],
        out_shape=[jax.ShapeDtypeStruct((rows, columns), F32)]
        + [jax.ShapeDtypeStruct((heads, blocks) + dims, kind) for _, dims, kind in saved]
        + [jax.ShapeDtypeStruct((heads, width, 2 * width), F32)],
        scratch_shapes=[pltpu.VMEM((heads, width, 2 * width), F32)],
        compiler_params=params(),
        cost_estimate=LIGHT,
        name="local_maps",
    )(offset, log_rate, rate_bias, edge, mixing, mixing, taps, rates)


def output_kernel(
    heads,
    offset_ref,
    incoming_ref,
    prefix_ref,
    u_ref,
    w_ref,
    score_ref,
    q_ref,
    cumul_ref,
    outgate_ref,
    gain_ref,
    state_ref,
    fresh_ref,
    mixed_ref,
    gated_ref,
):
    step = pl.program_id(0)
    pack = prefix_ref.shape[1]
    width = LANES
    offset = offset_ref[0]
    chains = [(pos, head) for pos in range(pack) for head in range(heads)]
    states = [
        dot3(prefix_ref[head, pos, :, :width], incoming_ref[head], NN)
        + prefix_ref[head, pos, :, width:]
        for pos, head in chains
    ]
    freshes = [
        u_ref[head, pos] - dot3(w_ref[head, pos], state, NN)
        for (pos, head), state in zip(chains, states)
    ]
    outs = []
    for (pos, head), state, fresh in zip(chains, states, freshes):
        carried, _ = decay_parts(cumul_ref[head, pos], (step * pack + pos) * SPAN, offset)
        outs.append(
            dot3(
                jnp.concatenate([carried * q_ref[head, pos], score_ref[head, pos]], 1),
                jnp.concatenate([state, fresh], 0),
                NN,
            )
        )
    for (pos, head), state, fresh, mixed in zip(chains, states, freshes, outs):
        here = slice(pos * SPAN, (pos + 1) * SPAN)
        cols = slice(head * width, (head + 1) * width)
        state_ref[head, pos] = state
        fresh_ref[head, pos] = fresh
        mixed_ref[here, cols] = mixed
        scale = lax.rsqrt(jnp.mean(mixed * mixed, -1, keepdims=True) + EPSILON)
        outgate = outgate_ref[here, cols]
        gated = mixed * scale * gain_ref[...].astype(F32) * (outgate * jax.nn.sigmoid(outgate))
        gated_ref[here, cols] = gated.astype(BF16).astype(gated_ref.dtype)


def outputs_of(offset, incoming, saved, outgate, gain, gated_type):
    prefix, u, w, scores, q, cumul = saved
    heads, blocks = prefix.shape[:2]
    width = LANES
    virt = STEPS * SPAN
    tile = PACK * SPAN
    rows = outgate.shape[0]
    per_block = specs_of(heads, PACK)
    flat = pl.BlockSpec((tile, heads * width), lambda g: (g, 0))
    return pl.pallas_call(
        partial(output_kernel, heads),
        grid=(blocks // PACK,),
        in_specs=[
            SCALARS,
            whole((heads, width, width)),
            per_block(width, 2 * width),
            per_block(virt, width),
            per_block(virt, width),
            per_block(SPAN, virt),
            per_block(SPAN, width),
            per_block(SPAN, width),
            flat,
            whole((1, width)),
        ],
        out_specs=[per_block(width, width), per_block(virt, width), flat, flat],
        out_shape=[
            jax.ShapeDtypeStruct((heads, blocks, width, width), F32),
            jax.ShapeDtypeStruct((heads, blocks, virt, width), F32),
            jax.ShapeDtypeStruct((rows, heads * width), F32),
            jax.ShapeDtypeStruct((rows, heads * width), gated_type),
        ],
        compiler_params=params(),
        cost_estimate=LIGHT,
        name="mixer_outputs",
    )(offset, incoming, prefix, u, w, scores, q, cumul, outgate, gain)


def gate_back_kernel(
    heads,
    parts,
    place_ref,
    *refs,
):
    piece_refs = refs[:parts]
    (
        weight_ref,
        mixed_ref,
        outgate_ref,
        gain_ref,
        query_ref,
        prefix_ref,
    ) = refs[parts : parts + 6]
    before = refs[parts + 6 : -7]
    (
        grad_gain_ref,
        total_ref,
        sum_ref,
        branch_ref,
        grad_mixed_ref,
        grad_outgate_ref,
        term_ref,
    ) = refs[-7:]
    step = pl.program_id(0)
    pack = prefix_ref.shape[1]
    width = LANES
    rows = branch_ref.shape[0]

    @pl.when(step == 0)
    def _():
        sum_ref[...] = sum(ref[rows:] for ref in piece_refs)
        grad_gain_ref[...] = jnp.zeros_like(grad_gain_ref)
        total_ref[...] = jnp.zeros_like(total_ref)
        if before:
            grad_gain_ref[...] = before[0][...]
            total_ref[...] = before[1][...]
            sum_ref[...] += before[2][...]

    for near in range(parts):

        @pl.when(step == near)
        def _():
            branch_ref[...] = piece_refs[near][:rows].astype(BF16)

    grad_all = dot1(branch_ref[...], weight_ref[...], NT)
    gain = gain_ref[...].astype(F32)
    grads_mixed = []
    for head in range(heads):
        cols = slice(head * width, (head + 1) * width)
        mixed = mixed_ref[:, cols]
        outgate = outgate_ref[:, cols]
        grad = grad_all[:, cols]
        scale = lax.rsqrt(jnp.mean(mixed * mixed, -1, keepdims=True) + EPSILON)
        normed = mixed * scale
        sigma = jax.nn.sigmoid(outgate)
        silu = outgate * sigma
        grad_outgate = grad * normed * gain * (sigma * (1.0 + outgate * (1.0 - sigma)))
        grad_outgate_ref[:, cols] = grad_outgate.astype(BF16)
        through = grad * silu
        product = through * normed
        grad_gain_ref[...] += jnp.sum(product.reshape(-1, 8, width), 0)
        grad_normed = through * gain
        grad_mixed = scale * (
            grad_normed - normed * jnp.mean(grad_normed * normed, -1, keepdims=True)
        )
        grad_mixed_ref[:, cols] = grad_mixed.astype(BF16)
        grads_mixed.append(grad_mixed)
    chains = [(pos, head) for pos in range(pack) for head in range(heads)]
    terms = [
        dot3(query_ref[head, pos], grads_mixed[head][pos * SPAN : (pos + 1) * SPAN], TN)
        for pos, head in chains
    ]
    moved = [dot3(prefix_ref[head, pos], term, TN) for (pos, head), term in zip(chains, terms)]
    totals = [total_ref[head] for head in range(heads)]
    for (pos, head), term, part in zip(chains, terms, moved):
        term_ref[head, pos] = term
        totals[head] = totals[head] + part
    for head in range(heads):
        total_ref[head] = totals[head]


def gate_back(place, pieces, weight, mixed, outgate, gain, query, prefix, before):
    heads, blocks = prefix.shape[:2]
    width = LANES
    parts = len(pieces)
    model = pieces[0].shape[1]
    rows = mixed.shape[0]
    tile = pieces[0].shape[0] - EDGE
    pack = tile // SPAN

    def fixed(*shape):
        return pl.BlockSpec(shape, lambda g, at: (0,) * len(shape))

    def per_block(*dims):
        return pl.BlockSpec((heads, pack) + dims, lambda g, at: (0, at[g]) + (0,) * len(dims))

    def flat(size):
        return pl.BlockSpec((tile, size), lambda g, at: (at[g], 0))

    in_specs = [fixed(tile + EDGE, model)] * parts + [
        fixed(*weight.shape),
        flat(heads * width),
        flat(heads * width),
        fixed(1, width),
        per_block(SPAN, width),
        per_block(width, width),
    ]
    operands = [place, *pieces, weight, mixed, outgate, gain, query, prefix]
    totals = [(8, width), (heads, width, width), (EDGE, model)]
    aliases = {}
    if before is not None:
        aliases = {len(operands) + 3 + index: 3 + index for index in range(4)}
        in_specs += [fixed(*shape) for shape in totals]
        in_specs += [pl.BlockSpec(memory_space=pl.ANY)] * 4
        operands += list(before)
    return pl.pallas_call(
        partial(gate_back_kernel, heads, parts),
        grid_spec=pltpu.PrefetchScalarGridSpec(
            num_scalar_prefetch=1,
            grid=(parts,),
            in_specs=in_specs,
            out_specs=[fixed(*shape) for shape in totals]
            + [flat(model), flat(heads * width), flat(heads * width), per_block(width, width)],
        ),
        out_shape=[jax.ShapeDtypeStruct(shape, F32) for shape in totals]
        + [
            jax.ShapeDtypeStruct((rows, model), BF16),
            jax.ShapeDtypeStruct((rows, heads * width), BF16),
            jax.ShapeDtypeStruct((rows, heads * width), BF16),
            jax.ShapeDtypeStruct((heads, blocks, width, width), F32),
        ],
        input_output_aliases=aliases,
        compiler_params=params(),
        cost_estimate=LIGHT,
        name="gate_back",
    )(*operands)


def place_kernel(parts, place_ref, *refs):
    out_ref, sum_ref = refs[parts:]
    rows = refs[0].shape[0] - EDGE
    for near in range(parts):
        here = pl.ds(pl.multiple_of(place_ref[near] * rows, rows), rows)
        out_ref[here] = refs[near][:rows].astype(out_ref.dtype)
    sum_ref[...] = sum(ref[rows:] for ref in refs[:parts])


def place_rows(place, pieces, kind):
    parts = len(pieces)
    rows, columns = pieces[0].shape
    return pl.pallas_call(
        partial(place_kernel, parts),
        in_specs=[SCALARS] + [IN_VMEM] * parts,
        out_specs=[IN_VMEM, IN_VMEM],
        out_shape=[
            jax.ShapeDtypeStruct((parts * (rows - EDGE), columns), kind),
            jax.ShapeDtypeStruct((EDGE, columns), F32),
        ],
        compiler_params=params(),
        cost_estimate=LIGHT,
        name="place_rows",
    )(place, *pieces)


def low_weight_kernel(*refs):
    refs[-2][...] = jnp.concatenate([ref[...].astype(BF16) for ref in refs[:-3]], 0)


def low_weight(pieces, passed):
    depth, columns = pieces[0].shape
    steps = 2
    return pl.pallas_call(
        low_weight_kernel,
        grid=(steps,),
        in_specs=[pl.BlockSpec((depth, columns // steps), lambda g: (0, g))] * len(pieces)
        + [pl.BlockSpec(memory_space=pl.ANY)],
        out_specs=[
            pl.BlockSpec((depth * len(pieces), columns // steps), lambda g: (0, g)),
            pl.BlockSpec(memory_space=pl.ANY),
        ],
        out_shape=[
            jax.ShapeDtypeStruct((depth * len(pieces), columns), BF16),
            jax.ShapeDtypeStruct(passed.shape, passed.dtype),
        ],
        input_output_aliases={len(pieces): 1},
        compiler_params=params(),
        cost_estimate=LIGHT,
        name="low_weight",
    )(*pieces, passed)


def first_kernel(
    raw_ref,
    input_ref,
    gain_ref,
    mix_ref,
    rates_ref,
    outgate_ref,
    normed_ref,
    mixing_ref,
    rates_out_ref,
    outgate_out_ref,
    edge_ref,
):
    gain = gain_ref[...].astype(F32)

    def norm(values):
        scale = lax.rsqrt(jnp.mean(values * values, -1, keepdims=True) + EPSILON)
        return (values * scale * gain).astype(BF16)

    normed = norm(input_ref[...].astype(F32))
    normed_ref[...] = normed
    mixing_ref[...] = dot1(normed, mix_ref[...], NN)
    rates_out_ref[...] = jnp.zeros_like(rates_out_ref)
    rates_out_ref[:, : rates_ref.shape[0]] = dot1(normed, rates_ref[...], NT)
    outgate_out_ref[...] = dot1(normed, outgate_ref[...], NN)

    @pl.when(pl.program_id(0) == 0)
    def _():
        edge_ref[...] = dot1(norm(raw_ref[...]), mix_ref[...], NN)


def first_projections(raw, block_input, gain, w_mix, w_rates, w_outgate):
    rows, model = block_input.shape
    steps = 4
    tile = rows // steps
    flat = lambda size: pl.BlockSpec((tile, size), lambda g: (g, 0))
    weights = (w_mix, w_rates, w_outgate)
    sizes = (w_mix.shape[1], LANES, w_outgate.shape[1])
    return pl.pallas_call(
        first_kernel,
        grid=(steps,),
        in_specs=[whole(raw.shape), flat(model), whole((1, model))]
        + [whole(weight.shape) for weight in weights],
        out_specs=[flat(model)] + [flat(size) for size in sizes] + [whole((EDGE, sizes[0]))],
        out_shape=[jax.ShapeDtypeStruct((rows, model), BF16)]
        + [jax.ShapeDtypeStruct((rows, size), F32) for size in sizes]
        + [jax.ShapeDtypeStruct((EDGE, sizes[0]), F32)],
        compiler_params=params(),
        cost_estimate=LIGHT,
        name="first_projections",
    )(raw, block_input, gain, *weights)


def grad_activ_kernel(grad_ref, weight_ref, out_ref):
    out_ref[...] = dot1(grad_ref[...], weight_ref[...], NT)


def grad_activ_of(grad, w_down):
    rows, model = grad.shape
    hidden = w_down.shape[0]
    steps = 4
    tile = rows // steps
    return pl.pallas_call(
        grad_activ_kernel,
        grid=(steps,),
        in_specs=[pl.BlockSpec((tile, model), lambda g: (g, 0)), whole(w_down.shape)],
        out_specs=pl.BlockSpec((tile, hidden), lambda g: (g, 0)),
        out_shape=jax.ShapeDtypeStruct((rows, hidden), F32),
        compiler_params=params(),
        cost_estimate=LIGHT,
        name="grad_activ",
    )(grad, w_down)


def dense_kernel(parts, *refs):
    gated_refs = refs[1 : 1 + parts]
    (
        weight_ref,
        input_ref,
        gain_ref,
        ffn_ref,
        down_ref,
        grad_activ_ref,
    ) = refs[1 + parts : 7 + parts]
    (
        middle_ref,
        normed_ref,
        activ_ref,
        *some_refs,
        back_ref,
        fore_ref,
    ) = refs[-6 - len(CUTS) :]
    hidden = down_ref.shape[0]
    gated = jnp.concatenate([ref[...].astype(BF16) for ref in gated_refs], 1)
    middle = input_ref[...].astype(F32) + dot1(gated, weight_ref[...], NN)
    middle_ref[...] = middle
    scale = lax.rsqrt(jnp.mean(middle * middle, -1, keepdims=True) + EPSILON)
    normed = (middle * scale * gain_ref[...].astype(F32)).astype(BF16)
    normed_ref[...] = normed
    both = dot1(normed, ffn_ref[...], NN)
    gate, up = both[:, :hidden], both[:, hidden:]
    grad_activ = grad_activ_ref[...]
    sigma = jax.nn.sigmoid(gate)
    silu = gate * sigma
    activ = (silu * up).astype(BF16)
    activ_ref[:, :hidden] = activ
    activ_ref[:, hidden:] = jnp.zeros_like(activ_ref[:, hidden:])
    grad_gate = grad_activ * up * (sigma * (1.0 + gate * (1.0 - sigma)))
    grad_both = jnp.concatenate([grad_gate, grad_activ * silu], 1).astype(BF16)
    for ref, low, high in zip(some_refs, (0,) + CUTS, CUTS + (2 * hidden,)):
        ref[...] = grad_both[:, low:high]
    back_ref[...] = dot1(grad_both, ffn_ref[...], NT)
    fore_ref[...] = dot1(activ, down_ref[...], NN)


DENSE_STEPS = 2
CUTS = (384, 768)


def dense_half(half, gated_near, weight, block_input, gain, ffn, w_down, grad_activ, filled):
    parts = len(gated_near)
    rows, model = block_input.shape
    steps = DENSE_STEPS
    tile = rows // (2 * steps)
    depth = gated_near[0].shape[1]
    hidden = w_down.shape[0]

    def fixed(*shape):
        return pl.BlockSpec(shape, lambda g, at: (0,) * len(shape))

    def flat(size):
        return pl.BlockSpec((tile, size), lambda g, at: (at[0] * steps + g, 0))

    sizes = [
        (model, F32),
        (model, BF16),
        (hidden + -hidden % LANES, BF16),
    ] + [(high - low, BF16) for low, high in zip((0,) + CUTS, CUTS + (2 * hidden,))]
    operands = [half, *gated_near, weight, block_input, gain, ffn, w_down, grad_activ]
    in_specs = [flat(depth)] * parts + [
        fixed(parts * depth, model),
        flat(model),
        fixed(1, model),
        fixed(model, 2 * hidden),
        fixed(hidden, model),
        flat(hidden),
    ]
    aliases = {}
    if filled is not None:
        aliases = {len(operands) + index: index for index in range(len(filled))}
        in_specs = in_specs + [pl.BlockSpec(memory_space=pl.ANY)] * len(filled)
        operands = operands + list(filled)
    return pl.pallas_call(
        partial(dense_kernel, parts),
        grid_spec=pltpu.PrefetchScalarGridSpec(
            num_scalar_prefetch=1,
            grid=(steps,),
            in_specs=in_specs,
            out_specs=[flat(size) for size, _ in sizes]
            + [pl.BlockSpec((tile, model), lambda g, at: (g, 0))] * 2,
        ),
        out_shape=[jax.ShapeDtypeStruct((rows, size), kind) for size, kind in sizes]
        + [jax.ShapeDtypeStruct((rows // 2, model), F32)] * 2,
        input_output_aliases=aliases,
        compiler_params=params(),
        cost_estimate=LIGHT,
        name="dense_half",
    )(*operands)


def first_back_kernel(count, place_ref, *refs):
    grad_refs, weight_refs = refs[:count], refs[count : 2 * count]
    sent_ref, kept_ref = refs[2 * count :]
    result = sum(
        dot1(grad_ref[...], weight_ref[...], NT)
        for grad_ref, weight_ref in zip(grad_refs, weight_refs)
    )
    half = pl.num_programs(0) // 2

    @pl.when(pl.program_id(0) < half)
    def _():
        sent_ref[...] = result

    @pl.when(pl.program_id(0) >= half)
    def _():
        kept_ref[...] = result


def first_back(half, grads, weights):
    rows = grads[0].shape[0]
    model = weights[0].shape[0]
    steps = 4
    tile = rows // steps
    side = steps // 2

    def rows_at(g, at):
        kept = (g >= side).astype(jnp.int32)
        return (kept * at[0] + (1 - kept) * (1 - at[0])) * side + g - kept * side

    def spec_of(grad):
        return pl.BlockSpec((tile, grad.shape[1]), lambda g, at: (rows_at(g, at), 0))

    return pl.pallas_call(
        partial(first_back_kernel, len(grads)),
        grid_spec=pltpu.PrefetchScalarGridSpec(
            num_scalar_prefetch=1,
            grid=(steps,),
            in_specs=[spec_of(grad) for grad in grads]
            + [pl.BlockSpec(weight.shape, lambda g, at: (0, 0)) for weight in weights],
            out_specs=[
                pl.BlockSpec((tile, model), lambda g, at: (jnp.minimum(g, side - 1), 0)),
                pl.BlockSpec((tile, model), lambda g, at: (jnp.maximum(g - side, 0), 0)),
            ],
        ),
        out_shape=[jax.ShapeDtypeStruct((rows // 2, model), F32)] * 2,
        compiler_params=params(),
        cost_estimate=LIGHT,
        name="first_back",
    )(half, *grads, *weights)


def back_kernel(
    heads,
    offset_ref,
    leaving_ref,
    term_ref,
    phi_ref,
    state_ref,
    fresh_ref,
    grad_ref,
    score_ref,
    x_ref,
    n_ref,
    cumul_ref,
    q_ref,
    k_ref,
    rates_ref,
    log_rate_ref,
    rate_bias_ref,
    conv_ref,
    edge_ref,
    halo_ref,
    mix_ref,
    taps_ref,
    grad_mix_ref,
    last_ref,
    before_ref,
    grad_rates_ref,
    decay_sum_ref,
    grad_taps_ref,
    run_ref,
    next_ref,
    act_ref,
):
    step = pl.program_id(0)
    steps = pl.num_programs(0)
    group = steps - 1 - step
    rows = mix_ref.shape[0]
    offset = offset_ref[0]
    width = LANES
    virt = STEPS * SPAN
    strict, _, _ = strict_mask()
    lane = iota((SPAN, width), 1)

    @pl.when(step == 0)
    def _():
        run_ref[...] = leaving_ref[...]
        next_ref[...] = jnp.zeros_like(next_ref)
        decay_sum_ref[...] = jnp.zeros_like(decay_sum_ref)
        grad_taps_ref[...] = jnp.zeros_like(grad_taps_ref)

    tok_row, tok_col = iota((SPAN, SPAN), 0), iota((SPAN, SPAN), 1)
    later = (tok_col >= tok_row).astype(BF16)
    earlier = tok_col < tok_row
    sums = jnp.concatenate([later, earlier.astype(BF16)], 1)
    beta_all, decay_all, slope_all = rate_parts(
        rates_ref[...], lane_row(log_rate_ref, heads), lane_row(rate_bias_ref, heads)
    )
    chains = [(pos, head) for pos in reversed(range(rows // SPAN)) for head in range(heads)]
    leavings = []
    for pos, head in chains:
        leaving = run_ref[head]
        leavings.append(leaving)
        run_ref[head] = dot3(phi_ref[head, pos], leaving, TN) + term_ref[head, pos]
    betas, parts_of, ratios, masked = [], [], [], []
    for pos, head in chains:
        here = slice(pos * SPAN, (pos + 1) * SPAN)
        begin = group * rows + pos * SPAN
        first_lane = head * (STEPS + 1)
        beta = jnp.concatenate(
            [
                spread(beta_all[here, first_lane + sub : first_lane + sub + 1])
                for sub in range(STEPS)
            ],
            0,
        )
        cumul = cumul_ref[head, pos]
        betas.append(beta)
        parts_of.append(decay_parts(cumul, begin, offset))
        ratio = decay_ratio(cumul, begin, offset)
        ratios.append(ratio)
        masked.append(jnp.where(strict, beta * twice(ratio), 0.0))
    lows = [leaving.astype(BF16) for leaving in leavings]
    grads = [
        grad_ref[pos * SPAN : (pos + 1) * SPAN, head * width : (head + 1) * width]
        for pos, head in chains
    ]
    scores_low = [score_ref[head, pos].astype(BF16) for pos, head in chains]
    states = [state_ref[head, pos].astype(BF16) for pos, head in chains]
    freshes = [fresh_ref[head, pos].astype(BF16) for pos, head in chains]
    queries = [q_ref[head, pos] for pos, head in chains]
    keys = [k_ref[head, pos] for pos, head in chains]
    key_leavings = [
        twice(tail) * dot1(key, low, NN) for key, low, (_, tail) in zip(keys, lows, parts_of)
    ]
    grad_freshes = [
        dot1(scores, grad, TN) + key_leaving
        for scores, grad, key_leaving in zip(scores_low, grads, key_leavings)
    ]
    solveds = [
        dot1(x_ref[head, pos], grad_fresh, TN)
        for (pos, head), grad_fresh in zip(chains, grad_freshes)
    ]
    scaleds = [beta * solved for beta, solved in zip(betas, solveds)]
    grad_scores = [dot1(grad, fresh, NT) for grad, fresh in zip(grads, freshes)]
    grad_systems = [-dot1(solved, fresh, NT) for solved, fresh in zip(solveds, freshes)]
    grad_states = [
        carried * dot1(grad, state, NT)
        for grad, state, (carried, _) in zip(grads, states, parts_of)
    ]
    scaled_states = [
        twice(carried) * dot1(scaled, state, NT)
        for scaled, state, (carried, _) in zip(scaleds, states, parts_of)
    ]
    boths = [
        jnp.concatenate([grad_score * ratio, grad_system * mask], 0).astype(BF16)
        for grad_score, ratio, grad_system, mask in zip(grad_scores, ratios, grad_systems, masked)
    ]
    from_keys = [dot1(both, key, NN) for both, key in zip(boths, keys)]
    to_keys = [
        dot1(both, jnp.concatenate([query.astype(BF16), key], 0), TN)
        for both, query, key in zip(boths, queries, keys)
    ]
    from_leavings = [
        twice(tail) * dot1(fresh, low, NT) for fresh, low, (_, tail) in zip(freshes, lows, parts_of)
    ]
    all_pairs = []
    for index, (pos, head) in enumerate(chains):
        system_pairs = grad_systems[index] * n_ref[head, pos].astype(F32)
        pairs = grad_scores[index] * score_ref[head, pos]
        pairs = pairs + system_pairs[:SPAN] + system_pairs[SPAN:]
        all_pairs.append(pairs[:, :SPAN] + pairs[:, SPAN:])
    crossed = [jnp.where(earlier, dot1(later, pairs, NN), 0.0) for pairs in all_pairs]
    all_ends = []
    for index, (pos, head) in enumerate(chains):
        read = scaled_states[index] * keys[index].astype(F32)
        arriving = grad_states[index] * queries[index] - read[:SPAN] - read[SPAN:]
        written = key_leavings[index] * fresh_ref[head, pos]
        written = written[:SPAN] + written[SPAN:]
        all_ends.append(dot1(sums, jnp.concatenate([arriving, written], 0), NN))
    rates_of = [jnp.zeros((SPAN, width), F32) for _ in range(rows // SPAN)]
    for index, (pos, head) in enumerate(chains):
        here = slice(pos * SPAN, (pos + 1) * SPAN)
        first_lane = head * (STEPS + 1)
        grad_query = from_keys[index][:SPAN] + grad_states[index]
        grad_key = (
            from_keys[index][SPAN:]
            - scaled_states[index]
            + to_keys[index]
            + from_leavings[index]
        )
        scaled = scaleds[index]
        for place_of, part in enumerate(
            (grad_query, grad_key[:SPAN], grad_key[SPAN:], scaled[:SPAN], scaled[SPAN:])
        ):
            at = (head * GROUPS + place_of) * width
            act_ref[here, at : at + width] = part
        fresh = fresh_ref[head, pos]
        step_part = (1.0 - betas[index]) * jnp.sum(solveds[index] * fresh, -1, keepdims=True)
        kept = parts_of[index][0][SPAN - 1 :] * jnp.sum(
            leavings[index] * state_ref[head, pos], 0, keepdims=True
        )
        grad_decay = jnp.sum(crossed[index], -1, keepdims=True) + jnp.sum(
            all_ends[index] + kept, -1, keepdims=True
        )
        for sub in range(STEPS):
            rates_of[pos] = jnp.where(
                lane == first_lane + sub,
                step_part[sub * SPAN : (sub + 1) * SPAN],
                rates_of[pos],
            )
        rates_of[pos] = jnp.where(lane == first_lane + STEPS, spread(grad_decay), rates_of[pos])
    is_decay = lane % (STEPS + 1) == STEPS
    for pos, grad_rates in enumerate(rates_of):
        here = slice(pos * SPAN, (pos + 1) * SPAN)
        decay_part = jnp.where(is_decay, grad_rates * decay_all[here], 0.0)
        grad_rates = jnp.where(is_decay, grad_rates * slope_all[here], grad_rates)
        grad_rates_ref[here] = grad_rates.astype(BF16)
        decay_sum_ref[0:1] += jnp.sum(decay_part, 0, keepdims=True)
        decay_sum_ref[1:2] += jnp.sum(jnp.where(is_decay, grad_rates, 0.0), 0, keepdims=True)

    place = group * rows + iota((rows, width), 0)
    keep_back = [1.0 - crossing(place - back, back, offset).astype(F32) for back in range(CONV)]
    keep_fore = [1.0 - crossing(place, fore, offset).astype(F32) for fore in range(CONV)]
    edge_place = iota((EDGE, width), 0) - EDGE
    keep_edge = [1.0 - crossing(edge_place, fore, offset).astype(F32) for fore in range(CONV)]
    for part in range(heads * GROUPS):
        cols = slice(part * width, (part + 1) * width)
        conv = conv_ref[:, cols]
        grad = act_ref[:, cols]
        sigma = jax.nn.sigmoid(conv)
        if 1 <= part % GROUPS < 1 + STEPS:
            act = conv * sigma
            scale = lax.rsqrt(jnp.sum(act * act, -1, keepdims=True) + EPSILON)
            unit = act * scale
            grad = scale * (grad - unit * jnp.sum(unit * grad, -1, keepdims=True))
        grad_conv = grad * (sigma * (1.0 + conv * (1.0 - sigma)))
        wide = jnp.concatenate([grad_conv, next_ref[:, cols]], 0)
        before = jnp.concatenate([jnp.zeros((EDGE, width), F32), grad_conv[:EDGE]], 0)
        above = jnp.where(group == 0, edge_ref[:, cols], halo_ref[:, cols])
        mix_wide = jnp.concatenate([above, mix_ref[:, cols]], 0)
        taps = taps_ref[:, cols].astype(F32)
        tap = taps[CONV - 1 : CONV]
        grad_mix = tap * grad_conv
        grad_before = jnp.zeros((EDGE, width), F32)
        sums_of = jnp.sum(grad_conv * mix_wide[EDGE:], 0, keepdims=True)
        grad_taps_ref[CONV - 1 : CONV, cols] += sums_of
        for shift in range(1, CONV):
            tap = taps[CONV - 1 - shift : CONV - shift]
            moved = pltpu.roll(wide, rows + EDGE - shift, 0)[:rows]
            grad_mix = grad_mix + tap * (moved * keep_fore[shift])
            moved = pltpu.roll(before, 2 * EDGE - shift, 0)[:EDGE]
            grad_before = grad_before + tap * (moved * keep_edge[shift])
            moved = pltpu.roll(mix_wide, shift, 0)[EDGE:] * keep_back[shift]
            grad_taps_ref[CONV - 1 - shift : CONV - shift, cols] += jnp.sum(
                grad_conv * moved, 0, keepdims=True
            )
        next_ref[:, cols] = grad_conv[:EDGE]
        grad_mix_ref[:, cols] = grad_mix.astype(BF16)
        before_ref[:, cols] = grad_before

        @pl.when(step == 0)
        def _():
            last_ref[:, cols] = grad_mix[rows - 2 * EDGE :]


def recurrence_back(offset, leaving, saved, rates, log_rate, rate_bias, conv, edge, mixing, taps):
    term, phi, state, fresh, grad, scores, x, n, cumul, q, k = saved
    rows, columns = mixing.shape
    heads, blocks = term.shape[:2]
    width = LANES
    virt = STEPS * SPAN
    tile = PACK * SPAN
    steps = blocks // PACK

    def per_block(*dims):
        return pl.BlockSpec(
            (heads, PACK) + dims, lambda g: (0, steps - 1 - g) + (0,) * len(dims)
        )

    def flat(size):
        return pl.BlockSpec((tile, size), lambda g: (steps - 1 - g, 0))

    return pl.pallas_call(
        partial(back_kernel, heads),
        grid=(steps,),
        in_specs=[
            SCALARS,
            whole((heads, width, width)),
            per_block(width, width),
            per_block(width, width),
            per_block(width, width),
            per_block(virt, width),
            flat(heads * width),
            per_block(SPAN, virt),
            per_block(virt, virt),
            per_block(virt, virt),
            per_block(SPAN, width),
            per_block(SPAN, width),
            per_block(virt, width),
            flat(LANES),
            SCALARS,
            SCALARS,
            flat(columns),
            whole((EDGE, columns)),
            pl.BlockSpec(
                (EDGE, columns),
                lambda g: (jnp.maximum((steps - 1 - g) * (tile // EDGE) - 1, 0), 0),
            ),
            flat(columns),
            whole(taps.shape),
        ],
        out_specs=[
            flat(columns),
            whole((2 * EDGE, columns)),
            whole((EDGE, columns)),
            flat(LANES),
            whole((8, LANES)),
            whole((8, columns)),
        ],
        out_shape=[
            jax.ShapeDtypeStruct((rows, columns), BF16),
            jax.ShapeDtypeStruct((2 * EDGE, columns), F32),
            jax.ShapeDtypeStruct((EDGE, columns), F32),
            jax.ShapeDtypeStruct((rows, LANES), BF16),
            jax.ShapeDtypeStruct((8, LANES), F32),
            jax.ShapeDtypeStruct((8, columns), F32),
        ],
        scratch_shapes=[
            pltpu.VMEM((heads, width, width), F32),
            pltpu.VMEM((EDGE, columns), F32),
            pltpu.VMEM((tile, columns), F32),
        ],
        compiler_params=params(),
        cost_estimate=LIGHT,
        name="recurrence_back",
    )(
        offset, leaving, term, phi, state, fresh, grad, scores, x, n, cumul, q, k,
        rates, log_rate, rate_bias, conv, edge, mixing, mixing, taps,
    )


def piece_at(index, total, low, mine, bit):
    half = total // 2
    later = (index >= half).astype(jnp.int32)
    rest = index - later * half
    side = (mine // bit) % 2
    picked = later * side + (1 - later) * (1 - side)
    return ((rest >> low) << (low + 1)) | (picked << low) | (rest & ((1 << low) - 1))


def sent_at(index, total):
    return jnp.minimum(index, total // 2 - 1)


def kept_at(index, total):
    return jnp.maximum(index - total // 2, 0)


def grad_kernel(half, pairs, *refs):
    sent_ref, kept_ref = refs[-2:]
    depth = sent_ref.shape[1]

    def put(out_ref):
        place = 0
        for index in range(pairs):
            first = 1 + index * (half + 1)
            left = jnp.concatenate([ref[...] for ref in refs[first : first + half]], 1)
            right_ref = refs[first + half]
            size = right_ref.shape[1]
            result = dot1(left, right_ref[...], TN)
            for piece in range(half):
                out_ref[piece, :, place : place + size] = result[piece * depth : (piece + 1) * depth]
            place += size

    @pl.when(pl.program_id(0) == 0)
    def _():
        put(sent_ref)

    @pl.when(pl.program_id(0) == 1)
    def _():
        put(kept_ref)


def weight_grad(mine, bit, total, pairs):
    low = bit.bit_length() - 1
    half = total // 2
    rows = pairs[0][0].shape[0]
    depth = pairs[0][0].shape[1] // total

    def pick(piece):
        return lambda g, at: (0, piece_at(g * half + piece, total, low, at[0], bit))

    def fixed(place):
        return lambda g, at: (0, place)

    in_specs, operands, width = [], [], 0
    for left, right, place, size in pairs:
        in_specs += [pl.BlockSpec((rows, depth), pick(piece)) for piece in range(half)]
        in_specs.append(pl.BlockSpec((rows, size), fixed(place)))
        operands += [left] * half + [right]
        width += size
    out = (half, depth, width)
    return pl.pallas_call(
        partial(grad_kernel, half, len(pairs)),
        grid_spec=pltpu.PrefetchScalarGridSpec(
            num_scalar_prefetch=1,
            grid=(2,),
            in_specs=in_specs,
            out_specs=[pl.BlockSpec(out, lambda g, at: (0, 0, 0))] * 2,
        ),
        out_shape=[jax.ShapeDtypeStruct(out, F32)] * 2,
        compiler_params=params(),
        cost_estimate=LIGHT,
        name="weight_grad",
    )(mine, *operands)


def down_grad_kernel(grad_ref, activ_ref, out_ref):
    out_ref[...] = dot1(grad_ref[...], activ_ref[...], TN)


def down_grad(grad, activ):
    rows, model = grad.shape
    steps = 4
    tile = model // steps
    return pl.pallas_call(
        down_grad_kernel,
        grid=(steps,),
        in_specs=[pl.BlockSpec((rows, tile), lambda g: (0, g)), whole(activ.shape)],
        out_specs=pl.BlockSpec((tile, activ.shape[1]), lambda g: (g, 0)),
        out_shape=jax.ShapeDtypeStruct((model, activ.shape[1]), F32),
        compiler_params=params(),
        cost_estimate=LIGHT,
        name="down_grad",
    )(grad, activ)


def combine_kernel(bit, mine_ref, kept_ref, arrived_ref, sent_ref, next_ref):
    side = (mine_ref[0] // bit) % 2
    sent_ref[...] = (kept_ref[:, 1 - side] + arrived_ref[:, 1 - side]).reshape(sent_ref.shape)
    next_ref[...] = (kept_ref[:, side] + arrived_ref[:, side]).reshape(next_ref.shape)


IN_VMEM = pl.BlockSpec(memory_space=pltpu.VMEM)


def combine(mine, bit, low, kept, arrived):
    total, rows, columns = kept.shape
    half = total // 2
    view = lambda array: array.reshape((half >> low, 2, 1 << low, rows, columns))
    return pl.pallas_call(
        partial(combine_kernel, bit),
        in_specs=[SCALARS, IN_VMEM, IN_VMEM],
        out_specs=[IN_VMEM, IN_VMEM],
        out_shape=[jax.ShapeDtypeStruct((half, rows, columns), F32)] * 2,
        compiler_params=params(),
        cost_estimate=LIGHT,
        name="combine",
    )(mine, view(kept), view(arrived))


def norm_back_kernel(
    place_ref, kept_ref, arrived_ref, value_ref, gain_ref, residual_ref, out_ref
):
    step = pl.program_id(0)
    tile = kept_ref.shape[0]
    rows = out_ref.shape[0] - EDGE
    values = value_ref[...].astype(F32)
    grad = kept_ref[...] + arrived_ref[...]
    scale = lax.rsqrt(jnp.mean(values * values, -1, keepdims=True) + EPSILON)
    normed = values * scale
    through = grad * gain_ref[...].astype(F32)
    back = scale * (through - normed * jnp.mean(through * normed, -1, keepdims=True))
    out_ref[pl.ds(pl.multiple_of(step * tile, tile), tile)] = back + residual_ref[...].astype(F32)
    sums = jnp.sum((grad * normed).reshape(-1, EDGE, grad.shape[1]), 0)

    @pl.when(step == 0)
    def _():
        out_ref[rows:] = sums

    @pl.when(step != 0)
    def _():
        out_ref[rows:] += sums


def norm_back(place, kept, arrived, values, gain, residual):
    rows, model = kept.shape
    steps = 2
    tile = rows // steps
    local = pl.BlockSpec((tile, model), lambda g, at: (g, 0))

    def spec_of(array):
        if array.shape[0] == rows + EDGE:
            return local
        return pl.BlockSpec((tile, model), lambda g, at: (at[0] * steps + g, 0))

    return pl.pallas_call(
        norm_back_kernel,
        grid_spec=pltpu.PrefetchScalarGridSpec(
            num_scalar_prefetch=1,
            grid=(steps,),
            in_specs=[
                local,
                local,
                spec_of(values),
                pl.BlockSpec((1, model), lambda g, at: (0, 0)),
                spec_of(residual),
            ],
            out_specs=pl.BlockSpec((rows + EDGE, model), lambda g, at: (0, 0)),
        ),
        out_shape=jax.ShapeDtypeStruct((rows + EDGE, model), F32),
        compiler_params=params(),
        cost_estimate=LIGHT,
        name="norm_back",
    )(place, kept, arrived, values, gain, residual)


def own_output_kernel(kept_ref, arrived_ref, middle_ref, gain_ref, out_ref):
    rows, model = kept_ref.shape
    width = gain_ref.shape[1]
    out_ref[:rows] = kept_ref[...] + arrived_ref[...] + middle_ref[...]
    out_ref[rows:] = jnp.concatenate(
        [gain_ref[...], jnp.zeros((EDGE, model - width), F32)], 1
    )


def own_output(place, kept, arrived, middle, grad_gain):
    rows, model = kept.shape
    return pl.pallas_call(
        lambda place_ref, *refs: own_output_kernel(*refs),
        grid_spec=pltpu.PrefetchScalarGridSpec(
            num_scalar_prefetch=1,
            grid=(1,),
            in_specs=[
                pl.BlockSpec((rows, model), lambda g, at: (0, 0)),
                pl.BlockSpec((rows, model), lambda g, at: (0, 0)),
                pl.BlockSpec((rows, model), lambda g, at: (at[0], 0)),
                pl.BlockSpec(grad_gain.shape, lambda g, at: (0, 0)),
            ],
            out_specs=pl.BlockSpec((rows + EDGE, model), lambda g, at: (0, 0)),
        ),
        out_shape=jax.ShapeDtypeStruct((rows + EDGE, model), F32),
        compiler_params=params(),
        cost_estimate=LIGHT,
        name="own_output",
    )(place, kept, arrived, middle, grad_gain)


def pack_kernel(parts, heads, *refs):
    pieces, (second_ref, gain_ref) = refs[:parts], refs[parts : parts + 2]
    decay_refs, taps_refs = refs[parts + 2 : parts + 2 + heads], refs[parts + 2 + heads : -1]
    out_ref = refs[-1]
    place = 0
    for rows in (sum(ref[...] for ref in pieces), second_ref[...]):
        total = jnp.sum(rows, 0, keepdims=True)
        for start in range(0, total.shape[1], LANES):
            out_ref[place : place + 1] = total[:, start : start + LANES]
            place += 1
    for ref in taps_refs:
        for start in range(0, ref.shape[1], LANES):
            out_ref[place : place + EDGE] = ref[:, start : start + LANES]
            place += EDGE
    out_ref[place : place + EDGE] = gain_ref[:, :LANES]
    out_ref[place + EDGE : place + 2 * EDGE] = sum(ref[...] for ref in decay_refs)


def pack_small(pieces, second, gain, decays, taps):
    model = second.shape[1]
    columns = sum(part.shape[1] for part in taps)
    rows = 2 * (model // LANES) + EDGE * (columns // LANES) + 2 * EDGE
    below = pieces[0].shape[0] // EDGE - 1
    others = (second, gain, *decays, *taps)
    return pl.pallas_call(
        partial(pack_kernel, len(pieces), len(decays)),
        grid=(1,),
        in_specs=[pl.BlockSpec((EDGE, model), lambda g: (below, 0))] * len(pieces)
        + [whole(part.shape) for part in others],
        out_specs=whole((rows, LANES)),
        out_shape=jax.ShapeDtypeStruct((rows, LANES), F32),
        compiler_params=params(),
        cost_estimate=LIGHT,
        name="pack_small",
    )(*pieces, *others)


def unpack_kernel(
    mine_ref, small_ref, first_ref, second_ref, gain_ref, decay_ref, taps_ref, *, count, model
):
    blocks = model // LANES
    size = model // count
    index = mine_ref[0]
    for base, ref in ((0, first_ref), (blocks, second_ref)):
        row = small_ref[pl.ds(base + index * size // LANES, 1)]
        if size < LANES:
            row = pltpu.roll(row, (LANES - index * size % LANES) % LANES, 1)
        ref[...] = row[:, :size]
    place = 2 * blocks
    for start in range(0, taps_ref.shape[1], LANES):
        taps_ref[:, start : start + LANES] = small_ref[place : place + CONV]
        place += EDGE
    gain_ref[...] = jnp.sum(small_ref[place : place + EDGE], 0, keepdims=True)
    decay_ref[...] = small_ref[place + EDGE : place + 2 * EDGE]


def unpack_small(mine, small, count, model, columns):
    size = model // count
    shapes = [(1, size), (1, size), (1, LANES), (EDGE, LANES), (CONV, columns)]
    return pl.pallas_call(
        partial(unpack_kernel, count=count, model=model),
        in_specs=[SCALARS, IN_VMEM],
        out_shape=[jax.ShapeDtypeStruct(shape, F32) for shape in shapes],
        compiler_params=params(),
        cost_estimate=LIGHT,
        name="unpack_small",
    )(mine, small)


def exchange(value, axis, bit):
    count = lax.axis_size(axis)
    return lax.ppermute(value, axis, [(place, place ^ bit) for place in range(count)])


def shifted(value, axis, steps):
    count = lax.axis_size(axis)
    first, last = (max(0, -steps), min(count, count - steps))
    return lax.ppermute(value, axis, [(source, source + steps) for source in range(first, last)])


def bits_of(axis):
    count = lax.axis_size(axis)
    return [1 << power for power in range(count.bit_length() - 1)]


class GatherNear:
    def __init__(self, value, axis):
        self.axis = axis
        self.bits = bits_of(axis)
        self.found = {0: value}
        for bit in self.bits[::-1]:
            self.found[bit] = exchange(value, axis, bit)

    def finish(self, *others):
        for bit in self.bits[::-1]:
            if others and bit == self.bits[-1]:
                self.found[bit] = after(self.found[bit], *others)
            for near in sorted(self.found):
                if near > bit and not near & bit and near | bit not in self.found:
                    self.found[near | bit] = exchange(self.found[near], self.axis, bit)
        return [self.found[near] for near in sorted(self.found)]


def gather_near(value, axis, *others):
    start = GatherNear(value, axis)
    others = sum([list(one()) if callable(one) else [one] for one in others], [])
    return start.finish(*others)


def after(value, *others):
    return lax.optimization_barrier((value,) + others)[0]


def join(*values):
    return lax.optimization_barrier(values)


class Scatter:
    def __init__(self, mine, axis, order, kept, sent):
        self.mine = mine
        self.axis = axis
        self.bits = sorted(order)
        self.order = list(order)
        self.kept = kept
        self.sent = sent

    def send(self):
        bit = self.order.pop(0)
        self.bits.remove(bit)
        self.arrived = exchange(self.sent, self.axis, bit)
        self.sent = None
        return self

    def add(self):
        if self.order:
            bit = self.order[0]
            self.sent, self.kept = combine(
                self.mine, bit, self.bits.index(bit), self.kept, self.arrived
            )
        else:
            self.total = self.kept[0] + self.arrived[0]
        return self

    def step(self):
        self.add()
        return self.send() if self.order else self


class WholeSum:
    def __init__(self, pairs):
        self.kept = self.sent = jnp.concatenate(
            [
                contract(left, lax.slice_in_dim(right, place * size, (place + 1) * size, axis=1), 0, 0)
                for left, right, place, size in pairs
            ],
            1,
        )
        self.order = []

    def send(self):
        self.arrived = lax.psum_scatter(self.sent, "seq", scatter_dimension=0, tiled=True)
        return self

    def add(self):
        self.total = self.kept = self.arrived
        return self

    def step(self):
        return self.add()


def arrive(*scatters, also=()):
    found = join(*[one.arrived for one in scatters], *also)
    for one, value in zip(scatters, found):
        one.arrived = value
    return found[len(scatters) :]


def contract(left, right, left_dim, right_dim):
    return lax.dot_general(
        left, right, (((left_dim,), (right_dim,)), ((), ())), preferred_element_type=F32
    )


def carried_in(total, own, axis, backward, maps=None):
    count = lax.axis_size(axis)
    sign = -1 if backward else 1
    reach = count - DOCS - 1
    if reach > DOCS - 1:
        reach = count - 1
    dims = (1, 1) if backward else (2, 1)
    width = LANES

    def move(map_of, state):
        return lax.dot_general(
            map_of, state, (((dims[0],), (1,)), ((0,), (0,))), precision=lax.Precision.HIGHEST
        )

    if reach < count - 1:
        if own is None:
            both = [shifted(total, axis, sign * step) for step in range(1, reach)]
            maps = [pair[..., :width] for pair in both]
            terms = [pair[..., width:] for pair in both]
            terms.append(shifted(total[..., width:], axis, sign * reach))
        else:
            terms = [shifted(own, axis, sign * step) for step in range(1, reach + 1)]
    else:
        every_map = lax.all_gather(total[..., :width], axis)
        every_term = lax.all_gather(total[..., width:] if own is None else own, axis)
        mine = lax.axis_index(axis)

        def at(array, step):
            place = mine - sign * step
            picked = lax.dynamic_index_in_dim(array, jnp.clip(place, 0, count - 1), 0, False)
            return jnp.where((place >= 0) & (place < count), picked, 0.0)

        maps = [at(every_map, step) for step in range(1, reach)]
        terms = [at(every_term, step) for step in range(1, reach + 1)]
    state = terms[-1]
    for map_of, term in zip(reversed(maps), reversed(terms[:-1])):
        state = move(map_of, state) + term
    return state


def maps_between(total, axis):
    count = lax.axis_size(axis)
    reach = count - DOCS - 1
    if reach > DOCS - 1:
        return None
    return [shifted(total[..., :LANES], axis, -step) for step in range(1, reach)]


def normalize(values):
    return values * lax.rsqrt(jnp.mean(values * values, -1, keepdims=True) + EPSILON)


def lanes_of(per_head):
    row = jnp.repeat(per_head, STEPS + 1)
    return jnp.pad(row, (0, LANES - row.shape[0]))[None]


def body(
    block_input,
    first_gain,
    w_mix,
    conv_taps,
    w_rates,
    log_rate,
    rate_bias,
    w_outgate,
    head_gain,
    w_out,
    second_gain,
    w_ffn,
    w_down,
    grad_output,
    seq_starts,
):
    rows, model = block_input.shape
    heads = log_rate.shape[0]
    parts = lax.axis_size("head")
    quarter = rows // parts
    head_index = lax.axis_index("head")
    seq, seq_index = lax.axis_size("seq"), lax.axis_index("seq")
    rate_lanes = w_rates.shape[1]
    ffn_flat = w_ffn.reshape(model, -1)

    head_bits = bits_of("head")
    core = head_index % 2
    kept_half, sent_half = core[None], (1 - core)[None]

    def block_of(index):
        return sum(
            ((index // bit) % 2) * (parts // (2 * bit)) for bit in head_bits
        )

    places = jnp.stack([block_of(head_index ^ near) for near in range(parts)]).astype(jnp.int32)
    own_block = places[0]
    own_rows = lambda array: lax.dynamic_slice_in_dim(array, own_block * quarter, quarter, 0)

    head_mine, seq_mine = head_index[None], seq_index[None]
    head_order, seq_bits = head_bits, bits_of("seq")

    raw_edge = shifted(block_input[rows - EDGE :].astype(F32), "seq", 1)
    w_out_start = GatherNear(w_out.astype(F32), "head")
    normed1_low, mixing, rates, outgate, edge = first_projections(
        raw_edge, block_input, first_gain[None], w_mix, w_rates.T, w_outgate
    )
    w_out_near = w_out_start.finish()
    conv, q, k, x, system, cumul, u, w, scores, query_map, prefix, phi, total = local_maps(
        seq_starts, log_rate, rate_bias, edge, mixing, conv_taps, rates
    )
    width = LANES
    incoming = carried_in(total, None, "seq", False)
    head_gain_row = after(head_gain, total)[None]
    state, fresh, mixed, gated = outputs_of(
        seq_starts, incoming, (prefix, u, w, scores, q, cumul), outgate, head_gain_row, F32
    )
    gain2_row = after(second_gain, gated)[None]
    w_rates_wide = jnp.pad(after(w_rates, gated), ((0, 0), (0, LANES - rate_lanes)))
    gated_start = GatherNear(gated, "head")
    w_out_low, ffn_flat = low_weight([after(piece, gated) for piece in w_out_near], ffn_flat)
    maps = maps_between(after(total, gated), "seq") or ()
    grad_activ = grad_activ_of(after(grad_output, w_out_low), w_down)
    ffn_flat, w_out_low, gain2_row, w_rates_wide, grad_activ, *maps = join(
        ffn_flat, w_out_low, gain2_row, w_rates_wide, grad_activ, *maps
    )
    gated_near = gated_start.finish(ffn_flat, w_out_low)

    dense = lambda half, filled: dense_half(
        half, gated_near, w_out_low, block_input, gain2_row, ffn_flat, w_down, grad_activ, filled
    )
    *filled, back_sent, fore_sent = dense(sent_half, None)
    split = lambda half: half.reshape(parts // 2, quarter, model)
    back = Scatter(head_mine, "head", head_order, None, split(back_sent)).send()
    *filled, back_kept, fore_kept = dense(kept_half, filled)
    middle, normed2_low, activ_low, *grads_both = filled
    back.kept = split(back_kept)
    back.step()

    near_first, far_first = seq_bits, seq_bits[1:] + seq_bits[:1]
    tiled = model // seq % LANES == 0

    def grad_sum(order, *pairs, tie=()):
        (left, *rest), *others = pairs
        pairs = [(after(left, *tie), *rest)] + others
        if not tiled:
            return WholeSum(pairs)
        sent, kept = weight_grad(seq_mine, order[0], seq, pairs)
        return Scatter(seq_mine, "seq", order, kept, sent)

    def total_of(one):
        while one.order:
            one.step()
        return one.add().total

    ffn_sums, tie = [], back.kept
    for order, right in zip((near_first, far_first, near_first), grads_both):
        ffn_sums.append(grad_sum(order, (normed2_low, right, 0, right.shape[1]), tie=(tie,)))
        tie = ffn_sums[-1].kept
    ffn_one, ffn_two, ffn_three = ffn_sums
    ffn_one.send()
    ffn_two.send()
    fore = Scatter(
        head_mine, "head", head_order, split(fore_kept), after(split(fore_sent), back.kept)
    ).send()
    down_sum = grad_sum(
        near_first, (grad_output, activ_low, 0, activ_low.shape[1]), tie=(ffn_three.kept,)
    )
    ffn_three.sent, down_sum.sent = arrive(
        back, fore, ffn_one, ffn_two, also=(ffn_three.sent, down_sum.sent)
    )
    grad_middle_own = norm_back(
        places[:1], back.kept[0], back.arrived[0], middle, gain2_row, grad_output
    )

    middle_start = GatherNear(grad_middle_own, "head")
    ffn_three.sent = after(ffn_three.sent, grad_middle_own)
    ffn_three.send()
    tie = grad_middle_own
    for one in (ffn_one, ffn_two):
        one.arrived = after(one.arrived, tie)
        one.step()
        tie = one.kept
    fore.arrived = after(fore.arrived, tie)
    fore.add()
    backed = partial(
        gate_back, weight=w_out, mixed=mixed, outgate=outgate, gain=head_gain_row, query=query_map, prefix=prefix
    )
    near_half = parts // 2
    near_pieces = [grad_middle_own, after(middle_start.found[1], fore.kept)]
    first_backed = backed(places[:near_half], near_pieces, before=None)
    middle_start.found[1], middle_start.found[2], fore.sent, *first_backed = arrive(
        *ffn_sums, also=(near_pieces[1], middle_start.found[2], fore.sent, *first_backed)
    )

    fore.send()
    grad_gain, grad_total, grad_second_gain, grad_branch, grad_mixed, outgate_low, term = backed(
        places[near_half:], middle_start.finish()[near_half:], before=first_backed
    )
    leaving = carried_in(total, grad_total, "seq", True, maps)
    out_width, outgate_width = gated.shape[1], outgate_low.shape[1]
    side_sum = grad_sum(
        near_first,
        (grad_branch, gated.astype(BF16), 0, out_width),
        (normed1_low, outgate_low, 0, outgate_width),
        tie=(grad_total,),
    )
    tie = side_sum.kept
    for one in (ffn_three, ffn_one):
        one.arrived = after(one.arrived, tie)
        one.add()
        tie = one.kept
    leaving, side_sum.sent, ffn_three.sent, ffn_one.sent, down_sum.sent = arrive(
        fore, also=(leaving, side_sum.sent, ffn_three.sent, ffn_one.sent, down_sum.sent)
    )
    output_own = own_output(places[:1], fore.kept[0], fore.arrived[0], middle, grad_gain)

    output_start = GatherNear(output_own, "head")
    down_sum.send()
    ffn_three.send()
    ffn_one.send()
    leaving, output_start.found[1] = join(after(leaving, output_own), output_start.found[1])
    grad_mix_rows, last_rows, before_rows, rate_low, decay_sums, grad_taps = recurrence_back(
        seq_starts,
        leaving,
        (term, phi, state, fresh, grad_mixed, scores, x, system, cumul, q, k),
        rates,
        log_rate,
        rate_bias,
        conv,
        edge,
        mixing,
        conv_taps,
    )
    before_rows, output_start.found[2] = arrive(
        ffn_one, ffn_three, down_sum, also=(before_rows, output_start.found[2])
    )

    returned = shifted(before_rows, "seq", -1)
    down_sum.add()
    ffn_three.arrived = after(ffn_three.arrived, down_sum.kept)
    ffn_three.add()
    returned, side_sum.sent, down_sum.sent, ffn_three.sent = join(
        returned, side_sum.sent, down_sum.sent, ffn_three.sent
    )
    for one in (side_sum, down_sum, ffn_three):
        one.send()
    last_rows = last_rows + jnp.pad(returned, ((EDGE, 0), (0, 0)))
    mixing_low = lax.dynamic_update_slice_in_dim(
        grad_mix_rows, last_rows.astype(BF16), rows - 2 * EDGE, 0
    )
    columns = mixing_low.shape[1]
    half_columns, narrow = columns // 2, columns // 10
    mix_one = grad_sum(near_first, (normed1_low, mixing_low, 0, half_columns))
    part_sent, part_kept = first_back(
        kept_half,
        (after(mixing_low, mix_one.kept), outgate_low, rate_low),
        (w_mix, w_outgate, w_rates_wide),
    )
    output_near = output_start.finish()
    part_sent, part_kept, mix_one.sent, *output_near = arrive(
        side_sum, down_sum, ffn_three,
        also=(part_sent, part_kept, mix_one.sent, *output_near),
    )
    part = Scatter(head_mine, "head", head_order, split(part_kept), split(part_sent)).send()
    part.step()
    mix_one.send()
    tie = part.kept
    for one in (side_sum, down_sum):
        one.arrived = after(one.arrived, tie)
        one.step()
        tie = one.kept

    mix_two = grad_sum(
        near_first,
        *[(normed1_low, mixing_low, 5 + piece, narrow) for piece in range(3)],
        tie=(tie,),
    ).send()
    output, grad_head_gain = place_rows(
        places, [after(piece, mix_two.kept) for piece in output_near], BF16
    )
    mix_three = grad_sum(
        near_first,
        *[(normed1_low, mixing_low, 8 + piece, narrow) for piece in range(2)],
        (normed1_low, rate_low, 0, LANES),
        tie=(output,),
    )
    mix_one.arrived = after(mix_one.arrived, mix_three.kept)
    mix_one.step()
    mix_three.sent, _ = arrive(
        part, side_sum, down_sum, also=(mix_three.sent, mix_one.kept)
    )
    grad_input_own = norm_back(
        places[:1], part.kept[0], part.arrived[0], block_input, first_gain[None], grad_middle_own
    )

    input_start = GatherNear(grad_input_own, "head")
    mix_three.sent, side_sum.sent, _ = join(mix_three.sent, side_sum.sent, grad_input_own)
    mix_three.send()
    tie = grad_input_own
    for one in (side_sum, mix_two):
        one.arrived = after(one.arrived, tie)
        one.step()
        tie = one.kept
    ffn_two.arrived = after(ffn_two.arrived, tie)
    ffn_two.step()
    down_sum.arrived = after(down_sum.arrived, ffn_two.kept)
    grad_down = total_of(down_sum)[:, : w_down.shape[0]].T
    mix_one.arrived, side_sum.arrived, _ = join(mix_one.arrived, side_sum.arrived, grad_down)
    mix_one.step()
    input_start.found[2], grad_down, _ = arrive(
        mix_two, mix_three, ffn_two, also=(input_start.found[2], grad_down, mix_one.kept)
    )
    input_near = input_start.finish()
    mix_three.step()
    mix_two.arrived = after(mix_two.arrived, mix_three.kept)
    mix_two.step()
    input_near[0] = after(input_near[0], mix_two.kept)
    small = pack_small(
        input_near, grad_second_gain, grad_head_gain, [decay_sums], [grad_taps]
    )
    arrived = exchange(small, "seq", seq_bits[0])
    input_near[0] = after(input_near[0], small)
    grad_input, _ = place_rows(places, input_near, F32)
    mix_three.arrived = after(mix_three.arrived, grad_input)
    mix_three.step()
    small = small + after(arrived, mix_three.kept)
    for bit in seq_bits[1:]:
        small = small + exchange(small, "seq", bit)
        for one in (mix_one, mix_two, side_sum, *ffn_sums):
            one.arrived = after(one.arrived, small)
    gain1_own, gain2_own, gain_sum, decay_sum, taps_sum = unpack_small(
        seq_mine, small, seq, model, mixing.shape[1]
    )
    decay_lanes = decay_sum[:, STEPS : heads * (STEPS + 1) : STEPS + 1]

    side_total = total_of(side_sum)
    ffn_total = jnp.concatenate([total_of(one) for one in ffn_sums], 1)
    mix_total = jnp.concatenate([total_of(one) for one in (mix_one, mix_two, mix_three)], 1)
    return (
        output,
        grad_input,
        gain1_own[0],
        mix_total[:, :columns],
        taps_sum,
        mix_total[:, columns : columns + rate_lanes],
        decay_lanes[0],
        decay_lanes[1],
        side_total[:, out_width:],
        gain_sum[0],
        side_total[:, :out_width].T,
        gain2_own[0],
        ffn_total.reshape((-1,) + w_ffn.shape[1:]),
        grad_down,
    )


def solution(mesh):
    return jax.shard_map(
        body,
        mesh=mesh,
        in_specs=(
            P("seq", None),
            P(),
            P(None, "head"),
            P(None, "head"),
            P(None, "head"),
            P("head"),
            P("head"),
            P(None, "head"),
            P(),
            P("head", None),
            P(),
            P(None, None, "head"),
            P("head", None),
            P("seq", None),
            P("seq"),
        ),
        out_specs=(
            P("seq", None),
            P("seq", None),
            P("seq"),
            P("seq", "head"),
            P(None, "head"),
            P("seq", "head"),
            P("head"),
            P("head"),
            P("seq", "head"),
            P(),
            P("head", "seq"),
            P("seq"),
            P("seq", None, "head"),
            P("head", "seq"),
        ),
        check_vma=False,
    )
```

```python
from functools import partial

import jax
import jax.numpy as jnp
from jax import lax
from jax.experimental import pallas as pl
from jax.experimental.pallas import tpu as pltpu
from jax.sharding import PartitionSpec as P

STEPS = 2
CONV = 4
SPAN = 64
EDGE = 8
LANES = 128
GROUPS = 1 + 2 * STEPS
PACK = 4
DOCS = 4
EPSILON = 1e-06
VMEM_LIMIT = 56 * 1024 * 1024

F32 = jnp.float32
BF16 = jnp.bfloat16
NN = (1, 0)
NT = (1, 1)
TN = (0, 0)


def dot1(left, right, dims):
    return lax.dot_general(
        left.astype(BF16),
        right.astype(BF16),
        (((dims[0],), (dims[1],)), ((), ())),
        preferred_element_type=F32,
    )


def halves(value):
    high = value.astype(BF16)
    return high, (value - high.astype(F32)).astype(BF16)


def dot3(left, right, dims):
    left_high, left_low = halves(left)
    right_high, right_low = halves(right)
    return dot1(
        jnp.concatenate([left_high, left_low, left_high], dims[0]),
        jnp.concatenate([right_high, right_high, right_low], dims[1]),
        dims,
    )


def iota(shape, dim):
    return lax.broadcasted_iota(jnp.int32, shape, dim)


def twice(value):
    return jnp.concatenate([value, value], 0)


def spread(column):
    return jnp.broadcast_to(column, (column.shape[0], LANES))


def crossing(place, reach, offset):
    return (place < offset) & (offset <= place + reach)


def lane_row(ref, heads):
    lane = iota((1, LANES), 1)
    row = jnp.zeros((1, LANES), F32)
    for head in range(heads):
        here = (lane >= head * (STEPS + 1)) & (lane < (head + 1) * (STEPS + 1))
        row = jnp.where(here, ref[head], row)
    return row


def rate_parts(raw, rate_row, bias_row):
    shifted_raw = raw + bias_row
    soft = jnp.maximum(shifted_raw, 0.0) + jnp.log1p(jnp.exp(-jnp.abs(shifted_raw)))
    slope = -jnp.exp(rate_row)
    return jax.nn.sigmoid(raw), slope * soft, slope * jax.nn.sigmoid(shifted_raw)


def decay_parts(cumul, begin, offset):
    place = begin + iota(cumul.shape, 0)
    inside = offset >= begin
    carried = jnp.where(inside & (place >= offset), 0.0, jnp.exp(cumul))
    cut = (place < offset) & (offset <= begin + (SPAN - 1))
    tail = jnp.exp(jnp.where(cut, -1e30, cumul[SPAN - 1 :] - cumul))
    return carried, tail


def decay_ratio(cumul, begin, offset):
    across = jnp.transpose(twice(cumul))[:SPAN]
    row = iota(across.shape, 0)
    col = iota(across.shape, 1) & (SPAN - 1)
    cut = (begin + col < offset) & (offset <= begin + row)
    return jnp.exp(jnp.where((col <= row) & jnp.logical_not(cut), cumul - across, -1e30))


def strict_mask():
    shape = (STEPS * SPAN, STEPS * SPAN)
    row, col = iota(shape, 0), iota(shape, 1)
    row_tok, col_tok = row & (SPAN - 1), col & (SPAN - 1)
    strict = (col_tok < row_tok) | ((col_tok == row_tok) & (col < row))
    return strict, row_tok ^ col_tok, (row == col).astype(F32)


def local_kernel(
    heads,
    offset_ref,
    log_rate_ref,
    rate_bias_ref,
    edge_ref,
    halo_ref,
    mix_ref,
    taps_ref,
    rates_ref,
    conv_ref,
    q_ref,
    k_ref,
    x_ref,
    n_ref,
    cumul_ref,
    u_ref,
    w_ref,
    score_ref,
    query_ref,
    prefix_ref,
    phi_ref,
    total_ref,
    run_ref,
):
    step = pl.program_id(0)
    rows = mix_ref.shape[0]
    offset = offset_ref[0]
    width = LANES
    strict, apart, eye = strict_mask()

    @pl.when(step == 0)
    def _():
        run_ref[...] = jnp.concatenate([jnp.broadcast_to(eye, run_ref.shape[:2] + (width,)), jnp.zeros(run_ref.shape[:2] + (width,), F32)], 2)

    place = step * rows + iota((rows, width), 0)
    keep = [1.0 - crossing(place - back, back, offset).astype(F32) for back in range(CONV)]
    acts = []
    for part in range(heads * GROUPS):
        cols = slice(part * width, (part + 1) * width)
        before = jnp.where(step == 0, edge_ref[:, cols], halo_ref[:, cols])
        wide = jnp.concatenate([before, mix_ref[:, cols]], 0)
        taps = taps_ref[:, cols].astype(F32)
        conv = taps[CONV - 1 : CONV] * wide[EDGE:]
        for back in range(1, CONV):
            moved = pltpu.roll(wide, back, 0)[EDGE:]
            conv = conv + taps[CONV - 1 - back : CONV - back] * (moved * keep[back])
        conv_ref[:, cols] = conv
        act = conv * jax.nn.sigmoid(conv)
        if 1 <= part % GROUPS < 1 + STEPS:
            act = act * lax.rsqrt(jnp.sum(act * act, -1, keepdims=True) + EPSILON)
        acts.append(act)

    beta_all, decay_all, _ = rate_parts(
        rates_ref[...], lane_row(log_rate_ref, heads), lane_row(rate_bias_ref, heads)
    )
    lower = (iota((SPAN, SPAN), 1) <= iota((SPAN, SPAN), 0)).astype(F32)
    chains = [(pos, head) for pos in range(rows // SPAN) for head in range(heads)]
    cumuls = [
        jnp.dot(
            lower,
            decay_all[pos * SPAN : (pos + 1) * SPAN],
            precision=lax.Precision.HIGHEST,
            preferred_element_type=F32,
        )
        for pos in range(rows // SPAN)
    ]
    queries, keys, scaleds, tails, carries, ratios, systems = [], [], [], [], [], [], []
    for pos, head in chains:
        here = slice(pos * SPAN, (pos + 1) * SPAN)
        begin = step * rows + pos * SPAN
        query, key1, key2, value1, value2 = (
            act[here] for act in acts[head * GROUPS : (head + 1) * GROUPS]
        )
        key = jnp.concatenate([key1, key2], 0)
        value = jnp.concatenate([value1, value2], 0)
        lane = head * (STEPS + 1)
        beta = jnp.concatenate(
            [spread(beta_all[here, lane + sub : lane + sub + 1]) for sub in range(STEPS)], 0
        )
        cumul = spread(cumuls[pos][:, lane + STEPS : lane + STEPS + 1])
        cumul_ref[head, pos] = cumul
        carried, tail = decay_parts(cumul, begin, offset)
        ratio = decay_ratio(cumul, begin, offset)
        key_low = key.astype(BF16)
        q_ref[head, pos] = query
        k_ref[head, pos] = key_low
        queries.append(query)
        keys.append(key)
        tails.append(twice(tail))
        carries.append(carried)
        ratios.append(ratio)
        scaleds.append(jnp.concatenate([beta * value, beta * twice(carried) * key], 1))
        systems.append(jnp.where(strict, beta * twice(ratio), 0.0) * dot3(key, key, NT))
    inverses = [eye - jnp.where(apart == 0, system, 0.0) for system in systems]
    for level in range(SPAN.bit_length() - 1):
        off_blocks = [jnp.where((apart >> level) == 1, system, 0.0) for system in systems]
        lows = [inverse.astype(BF16) for inverse in inverses]
        halfway = [dot1(low, off, NN) for low, off in zip(lows, off_blocks)]
        inverses = [
            inverse - dot1(half, low, NN) for inverse, half, low in zip(inverses, halfway, lows)
        ]
    residues = [
        (eye - inverse) - dot3(system, inverse, NN) for inverse, system in zip(inverses, systems)
    ]
    inverses = [
        inverse + dot1(inverse, residue, NN) for inverse, residue in zip(inverses, residues)
    ]
    solveds = [dot3(inverse, scaled, NN) for inverse, scaled in zip(inverses, scaleds)]
    all_scores = [ratio * dot3(query, key, NT) for ratio, query, key in zip(ratios, queries, keys)]
    all_maps = [
        dot3(
            key,
            jnp.concatenate([tail * solved[:, width:], tail * solved[:, :width]], 1),
            TN,
        )
        for key, tail, solved in zip(keys, tails, solveds)
    ]
    inner = [dot1(scores, solved[:, width:], NN) for scores, solved in zip(all_scores, solveds)]
    for index, (pos, head) in enumerate(chains):
        solved, maps, carried = solveds[index], all_maps[index], carries[index]
        phi = carried[SPAN - 1 :] * eye - maps[:, :width]
        x_ref[head, pos] = inverses[index].astype(BF16)
        n_ref[head, pos] = systems[index].astype(BF16)
        u_ref[head, pos] = solved[:, :width]
        w_ref[head, pos] = solved[:, width:]
        score_ref[head, pos] = all_scores[index]
        query_ref[head, pos] = carried * queries[index] - inner[index]
        phi_ref[head, pos] = phi
        run = run_ref[head]
        prefix_ref[head, pos] = run
        moved_run = dot3(phi, run, NN)
        run_ref[head] = jnp.concatenate(
            [moved_run[:, :width], moved_run[:, width:] + maps[:, width:]], 1
        )
    total_ref[...] = run_ref[...]


def specs_of(heads, pack):
    def per_block(*dims):
        return pl.BlockSpec((heads, pack) + dims, lambda g: (0, g) + (0,) * len(dims))

    return per_block


def whole(shape):
    return pl.BlockSpec(shape, lambda g: (0,) * len(shape))


SCALARS = pl.BlockSpec(memory_space=pltpu.SMEM)


def params():
    return pltpu.CompilerParams(vmem_limit_bytes=VMEM_LIMIT)


LIGHT = pl.CostEstimate(flops=1, bytes_accessed=1, transcendentals=0)


def local_maps(offset, log_rate, rate_bias, edge, mixing, taps, rates):
    rows, columns = mixing.shape
    width = LANES
    heads = columns // (GROUPS * width)
    blocks = rows // SPAN
    virt = STEPS * SPAN
    tile = PACK * SPAN
    per_block = specs_of(heads, PACK)
    saved = [
        (per_block(SPAN, width), (SPAN, width), F32),
        (per_block(virt, width), (virt, width), BF16),
        (per_block(virt, virt), (virt, virt), BF16),
        (per_block(virt, virt), (virt, virt), BF16),
        (per_block(SPAN, width), (SPAN, width), F32),
        (per_block(virt, width), (virt, width), F32),
        (per_block(virt, width), (virt, width), F32),
        (per_block(SPAN, virt), (SPAN, virt), F32),
        (per_block(SPAN, width), (SPAN, width), F32),
        (per_block(width, 2 * width), (width, 2 * width), F32),
        (per_block(width, width), (width, width), F32),
    ]
    return pl.pallas_call(
        partial(local_kernel, heads),
        grid=(blocks // PACK,),
        in_specs=[
            SCALARS,
            SCALARS,
            SCALARS,
            whole((EDGE, columns)),
            pl.BlockSpec((EDGE, columns), lambda g: (jnp.maximum(g * (tile // EDGE) - 1, 0), 0)),
            pl.BlockSpec((tile, columns), lambda g: (g, 0)),
            whole(taps.shape),
            pl.BlockSpec((tile, LANES), lambda g: (g, 0)),
        ],
        out_specs=[pl.BlockSpec((tile, columns), lambda g: (g, 0))]
        + [spec for spec, _, _ in saved]
        + [whole((heads, width, 2 * width))],
        out_shape=[jax.ShapeDtypeStruct((rows, columns), F32)]
        + [jax.ShapeDtypeStruct((heads, blocks) + dims, kind) for _, dims, kind in saved]
        + [jax.ShapeDtypeStruct((heads, width, 2 * width), F32)],
        scratch_shapes=[pltpu.VMEM((heads, width, 2 * width), F32)],
        compiler_params=params(),
        cost_estimate=LIGHT,
        name="local_maps",
    )(offset, log_rate, rate_bias, edge, mixing, mixing, taps, rates)


def output_kernel(
    heads,
    offset_ref,
    incoming_ref,
    prefix_ref,
    u_ref,
    w_ref,
    score_ref,
    q_ref,
    cumul_ref,
    outgate_ref,
    gain_ref,
    state_ref,
    fresh_ref,
    mixed_ref,
    gated_ref,
):
    step = pl.program_id(0)
    pack = prefix_ref.shape[1]
    width = LANES
    offset = offset_ref[0]
    chains = [(pos, head) for pos in range(pack) for head in range(heads)]
    states = [
        dot3(prefix_ref[head, pos, :, :width], incoming_ref[head], NN)
        + prefix_ref[head, pos, :, width:]
        for pos, head in chains
    ]
    freshes = [
        u_ref[head, pos] - dot3(w_ref[head, pos], state, NN)
        for (pos, head), state in zip(chains, states)
    ]
    outs = []
    for (pos, head), state, fresh in zip(chains, states, freshes):
        carried, _ = decay_parts(cumul_ref[head, pos], (step * pack + pos) * SPAN, offset)
        outs.append(
            dot3(
                jnp.concatenate([carried * q_ref[head, pos], score_ref[head, pos]], 1),
                jnp.concatenate([state, fresh], 0),
                NN,
            )
        )
    for (pos, head), state, fresh, mixed in zip(chains, states, freshes, outs):
        here = slice(pos * SPAN, (pos + 1) * SPAN)
        cols = slice(head * width, (head + 1) * width)
        state_ref[head, pos] = state
        fresh_ref[head, pos] = fresh
        mixed_ref[here, cols] = mixed
        scale = lax.rsqrt(jnp.mean(mixed * mixed, -1, keepdims=True) + EPSILON)
        outgate = outgate_ref[here, cols]
        gated = mixed * scale * gain_ref[...].astype(F32) * (outgate * jax.nn.sigmoid(outgate))
        gated_ref[here, cols] = gated.astype(BF16).astype(gated_ref.dtype)


def outputs_of(offset, incoming, saved, outgate, gain, gated_type):
    prefix, u, w, scores, q, cumul = saved
    heads, blocks = prefix.shape[:2]
    width = LANES
    virt = STEPS * SPAN
    tile = PACK * SPAN
    rows = outgate.shape[0]
    per_block = specs_of(heads, PACK)
    flat = pl.BlockSpec((tile, heads * width), lambda g: (g, 0))
    return pl.pallas_call(
        partial(output_kernel, heads),
        grid=(blocks // PACK,),
        in_specs=[
            SCALARS,
            whole((heads, width, width)),
            per_block(width, 2 * width),
            per_block(virt, width),
            per_block(virt, width),
            per_block(SPAN, virt),
            per_block(SPAN, width),
            per_block(SPAN, width),
            flat,
            whole((1, width)),
        ],
        out_specs=[per_block(width, width), per_block(virt, width), flat, flat],
        out_shape=[
            jax.ShapeDtypeStruct((heads, blocks, width, width), F32),
            jax.ShapeDtypeStruct((heads, blocks, virt, width), F32),
            jax.ShapeDtypeStruct((rows, heads * width), F32),
            jax.ShapeDtypeStruct((rows, heads * width), gated_type),
        ],
        compiler_params=params(),
        cost_estimate=LIGHT,
        name="mixer_outputs",
    )(offset, incoming, prefix, u, w, scores, q, cumul, outgate, gain)


def gate_back_kernel(
    heads,
    parts,
    place_ref,
    *refs,
):
    piece_refs = refs[:parts]
    (
        weight_ref,
        mixed_ref,
        outgate_ref,
        gain_ref,
        query_ref,
        prefix_ref,
    ) = refs[parts : parts + 6]
    before = refs[parts + 6 : -7]
    (
        grad_gain_ref,
        total_ref,
        sum_ref,
        branch_ref,
        grad_mixed_ref,
        grad_outgate_ref,
        term_ref,
    ) = refs[-7:]
    step = pl.program_id(0)
    pack = prefix_ref.shape[1]
    width = LANES
    rows = branch_ref.shape[0]

    @pl.when(step == 0)
    def _():
        sum_ref[...] = sum(ref[rows:] for ref in piece_refs)
        grad_gain_ref[...] = jnp.zeros_like(grad_gain_ref)
        total_ref[...] = jnp.zeros_like(total_ref)
        if before:
            grad_gain_ref[...] = before[0][...]
            total_ref[...] = before[1][...]
            sum_ref[...] += before[2][...]

    for near in range(parts):

        @pl.when(step == near)
        def _():
            branch_ref[...] = piece_refs[near][:rows].astype(BF16)

    grad_all = dot1(branch_ref[...], weight_ref[...], NT)
    gain = gain_ref[...].astype(F32)
    grads_mixed = []
    for head in range(heads):
        cols = slice(head * width, (head + 1) * width)
        mixed = mixed_ref[:, cols]
        outgate = outgate_ref[:, cols]
        grad = grad_all[:, cols]
        scale = lax.rsqrt(jnp.mean(mixed * mixed, -1, keepdims=True) + EPSILON)
        normed = mixed * scale
        sigma = jax.nn.sigmoid(outgate)
        silu = outgate * sigma
        grad_outgate = grad * normed * gain * (sigma * (1.0 + outgate * (1.0 - sigma)))
        grad_outgate_ref[:, cols] = grad_outgate.astype(BF16)
        through = grad * silu
        product = through * normed
        grad_gain_ref[...] += jnp.sum(product.reshape(-1, 8, width), 0)
        grad_normed = through * gain
        grad_mixed = scale * (
            grad_normed - normed * jnp.mean(grad_normed * normed, -1, keepdims=True)
        )
        grad_mixed_ref[:, cols] = grad_mixed.astype(BF16)
        grads_mixed.append(grad_mixed)
    chains = [(pos, head) for pos in range(pack) for head in range(heads)]
    terms = [
        dot3(query_ref[head, pos], grads_mixed[head][pos * SPAN : (pos + 1) * SPAN], TN)
        for pos, head in chains
    ]
    moved = [dot3(prefix_ref[head, pos], term, TN) for (pos, head), term in zip(chains, terms)]
    totals = [total_ref[head] for head in range(heads)]
    for (pos, head), term, part in zip(chains, terms, moved):
        term_ref[head, pos] = term
        totals[head] = totals[head] + part
    for head in range(heads):
        total_ref[head] = totals[head]


def gate_back(place, pieces, weight, mixed, outgate, gain, query, prefix, before):
    heads, blocks = prefix.shape[:2]
    width = LANES
    parts = len(pieces)
    model = pieces[0].shape[1]
    rows = mixed.shape[0]
    tile = pieces[0].shape[0] - EDGE
    pack = tile // SPAN

    def fixed(*shape):
        return pl.BlockSpec(shape, lambda g, at: (0,) * len(shape))

    def per_block(*dims):
        return pl.BlockSpec((heads, pack) + dims, lambda g, at: (0, at[g]) + (0,) * len(dims))

    def flat(size):
        return pl.BlockSpec((tile, size), lambda g, at: (at[g], 0))

    in_specs = [fixed(tile + EDGE, model)] * parts + [
        fixed(*weight.shape),
        flat(heads * width),
        flat(heads * width),
        fixed(1, width),
        per_block(SPAN, width),
        per_block(width, width),
    ]
    operands = [place, *pieces, weight, mixed, outgate, gain, query, prefix]
    totals = [(8, width), (heads, width, width), (EDGE, model)]
    aliases = {}
    if before is not None:
        aliases = {len(operands) + 3 + index: 3 + index for index in range(4)}
        in_specs += [fixed(*shape) for shape in totals]
        in_specs += [pl.BlockSpec(memory_space=pl.ANY)] * 4
        operands += list(before)
    return pl.pallas_call(
        partial(gate_back_kernel, heads, parts),
        grid_spec=pltpu.PrefetchScalarGridSpec(
            num_scalar_prefetch=1,
            grid=(parts,),
            in_specs=in_specs,
            out_specs=[fixed(*shape) for shape in totals]
            + [flat(model), flat(heads * width), flat(heads * width), per_block(width, width)],
        ),
        out_shape=[jax.ShapeDtypeStruct(shape, F32) for shape in totals]
        + [
            jax.ShapeDtypeStruct((rows, model), BF16),
            jax.ShapeDtypeStruct((rows, heads * width), BF16),
            jax.ShapeDtypeStruct((rows, heads * width), BF16),
            jax.ShapeDtypeStruct((heads, blocks, width, width), F32),
        ],
        input_output_aliases=aliases,
        compiler_params=params(),
        cost_estimate=LIGHT,
        name="gate_back",
    )(*operands)


def place_kernel(parts, place_ref, *refs):
    out_ref, sum_ref = refs[parts:]
    rows = refs[0].shape[0] - EDGE
    for near in range(parts):
        here = pl.ds(pl.multiple_of(place_ref[near] * rows, rows), rows)
        out_ref[here] = refs[near][:rows].astype(out_ref.dtype)
    sum_ref[...] = sum(ref[rows:] for ref in refs[:parts])


def place_rows(place, pieces, kind):
    parts = len(pieces)
    rows, columns = pieces[0].shape
    return pl.pallas_call(
        partial(place_kernel, parts),
        in_specs=[SCALARS] + [IN_VMEM] * parts,
        out_specs=[IN_VMEM, IN_VMEM],
        out_shape=[
            jax.ShapeDtypeStruct((parts * (rows - EDGE), columns), kind),
            jax.ShapeDtypeStruct((EDGE, columns), F32),
        ],
        compiler_params=params(),
        cost_estimate=LIGHT,
        name="place_rows",
    )(place, *pieces)


def low_weight_kernel(*refs):
    refs[-2][...] = jnp.concatenate([ref[...].astype(BF16) for ref in refs[:-3]], 0)


def low_weight(pieces, passed):
    depth, columns = pieces[0].shape
    steps = 2
    return pl.pallas_call(
        low_weight_kernel,
        grid=(steps,),
        in_specs=[pl.BlockSpec((depth, columns // steps), lambda g: (0, g))] * len(pieces)
        + [pl.BlockSpec(memory_space=pl.ANY)],
        out_specs=[
            pl.BlockSpec((depth * len(pieces), columns // steps), lambda g: (0, g)),
            pl.BlockSpec(memory_space=pl.ANY),
        ],
        out_shape=[
            jax.ShapeDtypeStruct((depth * len(pieces), columns), BF16),
            jax.ShapeDtypeStruct(passed.shape, passed.dtype),
        ],
        input_output_aliases={len(pieces): 1},
        compiler_params=params(),
        cost_estimate=LIGHT,
        name="low_weight",
    )(*pieces, passed)


def first_kernel(
    raw_ref,
    input_ref,
    gain_ref,
    mix_ref,
    rates_ref,
    outgate_ref,
    normed_ref,
    mixing_ref,
    rates_out_ref,
    outgate_out_ref,
    edge_ref,
):
    gain = gain_ref[...].astype(F32)

    def norm(values):
        scale = lax.rsqrt(jnp.mean(values * values, -1, keepdims=True) + EPSILON)
        return (values * scale * gain).astype(BF16)

    normed = norm(input_ref[...].astype(F32))
    normed_ref[...] = normed
    mixing_ref[...] = dot1(normed, mix_ref[...], NN)
    rates_out_ref[...] = jnp.zeros_like(rates_out_ref)
    rates_out_ref[:, : rates_ref.shape[0]] = dot1(normed, rates_ref[...], NT)
    outgate_out_ref[...] = dot1(normed, outgate_ref[...], NN)

    @pl.when(pl.program_id(0) == 0)
    def _():
        edge_ref[...] = dot1(norm(raw_ref[...]), mix_ref[...], NN)


def first_projections(raw, block_input, gain, w_mix, w_rates, w_outgate):
    rows, model = block_input.shape
    steps = 4
    tile = rows // steps
    flat = lambda size: pl.BlockSpec((tile, size), lambda g: (g, 0))
    weights = (w_mix, w_rates, w_outgate)
    sizes = (w_mix.shape[1], LANES, w_outgate.shape[1])
    return pl.pallas_call(
        first_kernel,
        grid=(steps,),
        in_specs=[whole(raw.shape), flat(model), whole((1, model))]
        + [whole(weight.shape) for weight in weights],
        out_specs=[flat(model)] + [flat(size) for size in sizes] + [whole((EDGE, sizes[0]))],
        out_shape=[jax.ShapeDtypeStruct((rows, model), BF16)]
        + [jax.ShapeDtypeStruct((rows, size), F32) for size in sizes]
        + [jax.ShapeDtypeStruct((EDGE, sizes[0]), F32)],
        compiler_params=params(),
        cost_estimate=LIGHT,
        name="first_projections",
    )(raw, block_input, gain, *weights)


def grad_activ_kernel(grad_ref, weight_ref, out_ref):
    out_ref[...] = dot1(grad_ref[...], weight_ref[...], NT)


def grad_activ_of(grad, w_down):
    rows, model = grad.shape
    hidden = w_down.shape[0]
    steps = 4
    tile = rows // steps
    return pl.pallas_call(
        grad_activ_kernel,
        grid=(steps,),
        in_specs=[pl.BlockSpec((tile, model), lambda g: (g, 0)), whole(w_down.shape)],
        out_specs=pl.BlockSpec((tile, hidden), lambda g: (g, 0)),
        out_shape=jax.ShapeDtypeStruct((rows, hidden), F32),
        compiler_params=params(),
        cost_estimate=LIGHT,
        name="grad_activ",
    )(grad, w_down)


def dense_kernel(parts, *refs):
    gated_refs = refs[1 : 1 + parts]
    (
        weight_ref,
        input_ref,
        gain_ref,
        ffn_ref,
        down_ref,
        grad_activ_ref,
    ) = refs[1 + parts : 7 + parts]
    (
        middle_ref,
        normed_ref,
        activ_ref,
        *some_refs,
        back_ref,
        fore_ref,
    ) = refs[-6 - len(CUTS) :]
    hidden = down_ref.shape[0]
    gated = jnp.concatenate([ref[...].astype(BF16) for ref in gated_refs], 1)
    middle = input_ref[...].astype(F32) + dot1(gated, weight_ref[...], NN)
    middle_ref[...] = middle
    scale = lax.rsqrt(jnp.mean(middle * middle, -1, keepdims=True) + EPSILON)
    normed = (middle * scale * gain_ref[...].astype(F32)).astype(BF16)
    normed_ref[...] = normed
    both = dot1(normed, ffn_ref[...], NN)
    gate, up = both[:, :hidden], both[:, hidden:]
    grad_activ = grad_activ_ref[...]
    sigma = jax.nn.sigmoid(gate)
    silu = gate * sigma
    activ = (silu * up).astype(BF16)
    activ_ref[:, :hidden] = activ
    activ_ref[:, hidden:] = jnp.zeros_like(activ_ref[:, hidden:])
    grad_gate = grad_activ * up * (sigma * (1.0 + gate * (1.0 - sigma)))
    grad_both = jnp.concatenate([grad_gate, grad_activ * silu], 1).astype(BF16)
    for ref, low, high in zip(some_refs, (0,) + CUTS, CUTS + (2 * hidden,)):
        ref[...] = grad_both[:, low:high]
    back_ref[...] = dot1(grad_both, ffn_ref[...], NT)
    fore_ref[...] = dot1(activ, down_ref[...], NN)


DENSE_STEPS = 2
CUTS = (384, 768)


def dense_half(half, gated_near, weight, block_input, gain, ffn, w_down, grad_activ, filled):
    parts = len(gated_near)
    rows, model = block_input.shape
    steps = DENSE_STEPS
    tile = rows // (2 * steps)
    depth = gated_near[0].shape[1]
    hidden = w_down.shape[0]

    def fixed(*shape):
        return pl.BlockSpec(shape, lambda g, at: (0,) * len(shape))

    def flat(size):
        return pl.BlockSpec((tile, size), lambda g, at: (at[0] * steps + g, 0))

    sizes = [
        (model, F32),
        (model, BF16),
        (hidden + -hidden % LANES, BF16),
    ] + [(high - low, BF16) for low, high in zip((0,) + CUTS, CUTS + (2 * hidden,))]
    operands = [half, *gated_near, weight, block_input, gain, ffn, w_down, grad_activ]
    in_specs = [flat(depth)] * parts + [
        fixed(parts * depth, model),
        flat(model),
        fixed(1, model),
        fixed(model, 2 * hidden),
        fixed(hidden, model),
        flat(hidden),
    ]
    aliases = {}
    if filled is not None:
        aliases = {len(operands) + index: index for index in range(len(filled))}
        in_specs = in_specs + [pl.BlockSpec(memory_space=pl.ANY)] * len(filled)
        operands = operands + list(filled)
    return pl.pallas_call(
        partial(dense_kernel, parts),
        grid_spec=pltpu.PrefetchScalarGridSpec(
            num_scalar_prefetch=1,
            grid=(steps,),
            in_specs=in_specs,
            out_specs=[flat(size) for size, _ in sizes]
            + [pl.BlockSpec((tile, model), lambda g, at: (g, 0))] * 2,
        ),
        out_shape=[jax.ShapeDtypeStruct((rows, size), kind) for size, kind in sizes]
        + [jax.ShapeDtypeStruct((rows // 2, model), F32)] * 2,
        input_output_aliases=aliases,
        compiler_params=params(),
        cost_estimate=LIGHT,
        name="dense_half",
    )(*operands)


def first_back_kernel(count, place_ref, *refs):
    grad_refs, weight_refs = refs[:count], refs[count : 2 * count]
    sent_ref, kept_ref = refs[2 * count :]
    result = sum(
        dot1(grad_ref[...], weight_ref[...], NT)
        for grad_ref, weight_ref in zip(grad_refs, weight_refs)
    )
    half = pl.num_programs(0) // 2

    @pl.when(pl.program_id(0) < half)
    def _():
        sent_ref[...] = result

    @pl.when(pl.program_id(0) >= half)
    def _():
        kept_ref[...] = result


def first_back(half, grads, weights):
    rows = grads[0].shape[0]
    model = weights[0].shape[0]
    steps = 4
    tile = rows // steps
    side = steps // 2

    def rows_at(g, at):
        kept = (g >= side).astype(jnp.int32)
        return (kept * at[0] + (1 - kept) * (1 - at[0])) * side + g - kept * side

    def spec_of(grad):
        return pl.BlockSpec((tile, grad.shape[1]), lambda g, at: (rows_at(g, at), 0))

    return pl.pallas_call(
        partial(first_back_kernel, len(grads)),
        grid_spec=pltpu.PrefetchScalarGridSpec(
            num_scalar_prefetch=1,
            grid=(steps,),
            in_specs=[spec_of(grad) for grad in grads]
            + [pl.BlockSpec(weight.shape, lambda g, at: (0, 0)) for weight in weights],
            out_specs=[
                pl.BlockSpec((tile, model), lambda g, at: (jnp.minimum(g, side - 1), 0)),
                pl.BlockSpec((tile, model), lambda g, at: (jnp.maximum(g - side, 0), 0)),
            ],
        ),
        out_shape=[jax.ShapeDtypeStruct((rows // 2, model), F32)] * 2,
        compiler_params=params(),
        cost_estimate=LIGHT,
        name="first_back",
    )(half, *grads, *weights)


def back_kernel(
    heads,
    offset_ref,
    leaving_ref,
    term_ref,
    phi_ref,
    state_ref,
    fresh_ref,
    grad_ref,
    score_ref,
    x_ref,
    n_ref,
    cumul_ref,
    q_ref,
    k_ref,
    rates_ref,
    log_rate_ref,
    rate_bias_ref,
    conv_ref,
    edge_ref,
    halo_ref,
    mix_ref,
    taps_ref,
    grad_mix_ref,
    last_ref,
    before_ref,
    grad_rates_ref,
    decay_sum_ref,
    grad_taps_ref,
    run_ref,
    next_ref,
    act_ref,
):
    step = pl.program_id(0)
    steps = pl.num_programs(0)
    group = steps - 1 - step
    rows = mix_ref.shape[0]
    offset = offset_ref[0]
    width = LANES
    virt = STEPS * SPAN
    strict, _, _ = strict_mask()
    lane = iota((SPAN, width), 1)

    @pl.when(step == 0)
    def _():
        run_ref[...] = leaving_ref[...]
        next_ref[...] = jnp.zeros_like(next_ref)
        decay_sum_ref[...] = jnp.zeros_like(decay_sum_ref)
        grad_taps_ref[...] = jnp.zeros_like(grad_taps_ref)

    tok_row, tok_col = iota((SPAN, SPAN), 0), iota((SPAN, SPAN), 1)
    later = (tok_col >= tok_row).astype(BF16)
    earlier = tok_col < tok_row
    sums = jnp.concatenate([later, earlier.astype(BF16)], 1)
    beta_all, decay_all, slope_all = rate_parts(
        rates_ref[...], lane_row(log_rate_ref, heads), lane_row(rate_bias_ref, heads)
    )
    chains = [(pos, head) for pos in reversed(range(rows // SPAN)) for head in range(heads)]
    leavings = []
    for pos, head in chains:
        leaving = run_ref[head]
        leavings.append(leaving)
        run_ref[head] = dot3(phi_ref[head, pos], leaving, TN) + term_ref[head, pos]
    betas, parts_of, ratios, masked = [], [], [], []
    for pos, head in chains:
        here = slice(pos * SPAN, (pos + 1) * SPAN)
        begin = group * rows + pos * SPAN
        first_lane = head * (STEPS + 1)
        beta = jnp.concatenate(
            [
                spread(beta_all[here, first_lane + sub : first_lane + sub + 1])
                for sub in range(STEPS)
            ],
            0,
        )
        cumul = cumul_ref[head, pos]
        betas.append(beta)
        parts_of.append(decay_parts(cumul, begin, offset))
        ratio = decay_ratio(cumul, begin, offset)
        ratios.append(ratio)
        masked.append(jnp.where(strict, beta * twice(ratio), 0.0))
    lows = [leaving.astype(BF16) for leaving in leavings]
    grads = [
        grad_ref[pos * SPAN : (pos + 1) * SPAN, head * width : (head + 1) * width]
        for pos, head in chains
    ]
    scores_low = [score_ref[head, pos].astype(BF16) for pos, head in chains]
    states = [state_ref[head, pos].astype(BF16) for pos, head in chains]
    freshes = [fresh_ref[head, pos].astype(BF16) for pos, head in chains]
    queries = [q_ref[head, pos] for pos, head in chains]
    keys = [k_ref[head, pos] for pos, head in chains]
    key_leavings = [
        twice(tail) * dot1(key, low, NN) for key, low, (_, tail) in zip(keys, lows, parts_of)
    ]
    grad_freshes = [
        dot1(scores, grad, TN) + key_leaving
        for scores, grad, key_leaving in zip(scores_low, grads, key_leavings)
    ]
    solveds = [
        dot1(x_ref[head, pos], grad_fresh, TN)
        for (pos, head), grad_fresh in zip(chains, grad_freshes)
    ]
    scaleds = [beta * solved for beta, solved in zip(betas, solveds)]
    grad_scores = [dot1(grad, fresh, NT) for grad, fresh in zip(grads, freshes)]
    grad_systems = [-dot1(solved, fresh, NT) for solved, fresh in zip(solveds, freshes)]
    grad_states = [
        carried * dot1(grad, state, NT)
        for grad, state, (carried, _) in zip(grads, states, parts_of)
    ]
    scaled_states = [
        twice(carried) * dot1(scaled, state, NT)
        for scaled, state, (carried, _) in zip(scaleds, states, parts_of)
    ]
    boths = [
        jnp.concatenate([grad_score * ratio, grad_system * mask], 0).astype(BF16)
        for grad_score, ratio, grad_system, mask in zip(grad_scores, ratios, grad_systems, masked)
    ]
    from_keys = [dot1(both, key, NN) for both, key in zip(boths, keys)]
    to_keys = [
        dot1(both, jnp.concatenate([query.astype(BF16), key], 0), TN)
        for both, query, key in zip(boths, queries, keys)
    ]
    from_leavings = [
        twice(tail) * dot1(fresh, low, NT) for fresh, low, (_, tail) in zip(freshes, lows, parts_of)
    ]
    all_pairs = []
    for index, (pos, head) in enumerate(chains):
        system_pairs = grad_systems[index] * n_ref[head, pos].astype(F32)
        pairs = grad_scores[index] * score_ref[head, pos]
        pairs = pairs + system_pairs[:SPAN] + system_pairs[SPAN:]
        all_pairs.append(pairs[:, :SPAN] + pairs[:, SPAN:])
    crossed = [jnp.where(earlier, dot1(later, pairs, NN), 0.0) for pairs in all_pairs]
    all_ends = []
    for index, (pos, head) in enumerate(chains):
        read = scaled_states[index] * keys[index].astype(F32)
        arriving = grad_states[index] * queries[index] - read[:SPAN] - read[SPAN:]
        written = key_leavings[index] * fresh_ref[head, pos]
        written = written[:SPAN] + written[SPAN:]
        all_ends.append(dot1(sums, jnp.concatenate([arriving, written], 0), NN))
    rates_of = [jnp.zeros((SPAN, width), F32) for _ in range(rows // SPAN)]
    for index, (pos, head) in enumerate(chains):
        here = slice(pos * SPAN, (pos + 1) * SPAN)
        first_lane = head * (STEPS + 1)
        grad_query = from_keys[index][:SPAN] + grad_states[index]
        grad_key = (
            from_keys[index][SPAN:]
            - scaled_states[index]
            + to_keys[index]
            + from_leavings[index]
        )
        scaled = scaleds[index]
        for place_of, part in enumerate(
            (grad_query, grad_key[:SPAN], grad_key[SPAN:], scaled[:SPAN], scaled[SPAN:])
        ):
            at = (head * GROUPS + place_of) * width
            act_ref[here, at : at + width] = part
        fresh = fresh_ref[head, pos]
        step_part = (1.0 - betas[index]) * jnp.sum(solveds[index] * fresh, -1, keepdims=True)
        kept = parts_of[index][0][SPAN - 1 :] * jnp.sum(
            leavings[index] * state_ref[head, pos], 0, keepdims=True
        )
        grad_decay = jnp.sum(crossed[index], -1, keepdims=True) + jnp.sum(
            all_ends[index] + kept, -1, keepdims=True
        )
        for sub in range(STEPS):
            rates_of[pos] = jnp.where(
                lane == first_lane + sub,
                step_part[sub * SPAN : (sub + 1) * SPAN],
                rates_of[pos],
            )
        rates_of[pos] = jnp.where(lane == first_lane + STEPS, spread(grad_decay), rates_of[pos])
    is_decay = lane % (STEPS + 1) == STEPS
    for pos, grad_rates in enumerate(rates_of):
        here = slice(pos * SPAN, (pos + 1) * SPAN)
        decay_part = jnp.where(is_decay, grad_rates * decay_all[here], 0.0)
        grad_rates = jnp.where(is_decay, grad_rates * slope_all[here], grad_rates)
        grad_rates_ref[here] = grad_rates.astype(BF16)
        decay_sum_ref[0:1] += jnp.sum(decay_part, 0, keepdims=True)
        decay_sum_ref[1:2] += jnp.sum(jnp.where(is_decay, grad_rates, 0.0), 0, keepdims=True)

    place = group * rows + iota((rows, width), 0)
    keep_back = [1.0 - crossing(place - back, back, offset).astype(F32) for back in range(CONV)]
    keep_fore = [1.0 - crossing(place, fore, offset).astype(F32) for fore in range(CONV)]
    edge_place = iota((EDGE, width), 0) - EDGE
    keep_edge = [1.0 - crossing(edge_place, fore, offset).astype(F32) for fore in range(CONV)]
    for part in range(heads * GROUPS):
        cols = slice(part * width, (part + 1) * width)
        conv = conv_ref[:, cols]
        grad = act_ref[:, cols]
        sigma = jax.nn.sigmoid(conv)
        if 1 <= part % GROUPS < 1 + STEPS:
            act = conv * sigma
            scale = lax.rsqrt(jnp.sum(act * act, -1, keepdims=True) + EPSILON)
            unit = act * scale
            grad = scale * (grad - unit * jnp.sum(unit * grad, -1, keepdims=True))
        grad_conv = grad * (sigma * (1.0 + conv * (1.0 - sigma)))
        wide = jnp.concatenate([grad_conv, next_ref[:, cols]], 0)
        before = jnp.concatenate([jnp.zeros((EDGE, width), F32), grad_conv[:EDGE]], 0)
        above = jnp.where(group == 0, edge_ref[:, cols], halo_ref[:, cols])
        mix_wide = jnp.concatenate([above, mix_ref[:, cols]], 0)
        taps = taps_ref[:, cols].astype(F32)
        tap = taps[CONV - 1 : CONV]
        grad_mix = tap * grad_conv
        grad_before = jnp.zeros((EDGE, width), F32)
        sums_of = jnp.sum(grad_conv * mix_wide[EDGE:], 0, keepdims=True)
        grad_taps_ref[CONV - 1 : CONV, cols] += sums_of
        for shift in range(1, CONV):
            tap = taps[CONV - 1 - shift : CONV - shift]
            moved = pltpu.roll(wide, rows + EDGE - shift, 0)[:rows]
            grad_mix = grad_mix + tap * (moved * keep_fore[shift])
            moved = pltpu.roll(before, 2 * EDGE - shift, 0)[:EDGE]
            grad_before = grad_before + tap * (moved * keep_edge[shift])
            moved = pltpu.roll(mix_wide, shift, 0)[EDGE:] * keep_back[shift]
            grad_taps_ref[CONV - 1 - shift : CONV - shift, cols] += jnp.sum(
                grad_conv * moved, 0, keepdims=True
            )
        next_ref[:, cols] = grad_conv[:EDGE]
        grad_mix_ref[:, cols] = grad_mix.astype(BF16)
        before_ref[:, cols] = grad_before

        @pl.when(step == 0)
        def _():
            last_ref[:, cols] = grad_mix[rows - 2 * EDGE :]


def recurrence_back(offset, leaving, saved, rates, log_rate, rate_bias, conv, edge, mixing, taps):
    term, phi, state, fresh, grad, scores, x, n, cumul, q, k = saved
    rows, columns = mixing.shape
    heads, blocks = term.shape[:2]
    width = LANES
    virt = STEPS * SPAN
    tile = PACK * SPAN
    steps = blocks // PACK

    def per_block(*dims):
        return pl.BlockSpec(
            (heads, PACK) + dims, lambda g: (0, steps - 1 - g) + (0,) * len(dims)
        )

    def flat(size):
        return pl.BlockSpec((tile, size), lambda g: (steps - 1 - g, 0))

    return pl.pallas_call(
        partial(back_kernel, heads),
        grid=(steps,),
        in_specs=[
            SCALARS,
            whole((heads, width, width)),
            per_block(width, width),
            per_block(width, width),
            per_block(width, width),
            per_block(virt, width),
            flat(heads * width),
            per_block(SPAN, virt),
            per_block(virt, virt),
            per_block(virt, virt),
            per_block(SPAN, width),
            per_block(SPAN, width),
            per_block(virt, width),
            flat(LANES),
            SCALARS,
            SCALARS,
            flat(columns),
            whole((EDGE, columns)),
            pl.BlockSpec(
                (EDGE, columns),
                lambda g: (jnp.maximum((steps - 1 - g) * (tile // EDGE) - 1, 0), 0),
            ),
            flat(columns),
            whole(taps.shape),
        ],
        out_specs=[
            flat(columns),
            whole((2 * EDGE, columns)),
            whole((EDGE, columns)),
            flat(LANES),
            whole((8, LANES)),
            whole((8, columns)),
        ],
        out_shape=[
            jax.ShapeDtypeStruct((rows, columns), BF16),
            jax.ShapeDtypeStruct((2 * EDGE, columns), F32),
            jax.ShapeDtypeStruct((EDGE, columns), F32),
            jax.ShapeDtypeStruct((rows, LANES), BF16),
            jax.ShapeDtypeStruct((8, LANES), F32),
            jax.ShapeDtypeStruct((8, columns), F32),
        ],
        scratch_shapes=[
            pltpu.VMEM((heads, width, width), F32),
            pltpu.VMEM((EDGE, columns), F32),
            pltpu.VMEM((tile, columns), F32),
        ],
        compiler_params=params(),
        cost_estimate=LIGHT,
        name="recurrence_back",
    )(
        offset, leaving, term, phi, state, fresh, grad, scores, x, n, cumul, q, k,
        rates, log_rate, rate_bias, conv, edge, mixing, mixing, taps,
    )


def piece_at(index, total, low, mine, bit):
    half = total // 2
    later = (index >= half).astype(jnp.int32)
    rest = index - later * half
    side = (mine // bit) % 2
    picked = later * side + (1 - later) * (1 - side)
    return ((rest >> low) << (low + 1)) | (picked << low) | (rest & ((1 << low) - 1))


def sent_at(index, total):
    return jnp.minimum(index, total // 2 - 1)


def kept_at(index, total):
    return jnp.maximum(index - total // 2, 0)


def grad_kernel(half, pairs, *refs):
    sent_ref, kept_ref = refs[-2:]
    depth = sent_ref.shape[1]

    def put(out_ref):
        place = 0
        for index in range(pairs):
            first = 1 + index * (half + 1)
            left = jnp.concatenate([ref[...] for ref in refs[first : first + half]], 1)
            right_ref = refs[first + half]
            size = right_ref.shape[1]
            result = dot1(left, right_ref[...], TN)
            for piece in range(half):
                out_ref[piece, :, place : place + size] = result[piece * depth : (piece + 1) * depth]
            place += size

    @pl.when(pl.program_id(0) == 0)
    def _():
        put(sent_ref)

    @pl.when(pl.program_id(0) == 1)
    def _():
        put(kept_ref)


def weight_grad(mine, bit, total, pairs):
    low = bit.bit_length() - 1
    half = total // 2
    rows = pairs[0][0].shape[0]
    depth = pairs[0][0].shape[1] // total

    def pick(piece):
        return lambda g, at: (0, piece_at(g * half + piece, total, low, at[0], bit))

    def fixed(place):
        return lambda g, at: (0, place)

    in_specs, operands, width = [], [], 0
    for left, right, place, size in pairs:
        in_specs += [pl.BlockSpec((rows, depth), pick(piece)) for piece in range(half)]
        in_specs.append(pl.BlockSpec((rows, size), fixed(place)))
        operands += [left] * half + [right]
        width += size
    out = (half, depth, width)
    return pl.pallas_call(
        partial(grad_kernel, half, len(pairs)),
        grid_spec=pltpu.PrefetchScalarGridSpec(
            num_scalar_prefetch=1,
            grid=(2,),
            in_specs=in_specs,
            out_specs=[pl.BlockSpec(out, lambda g, at: (0, 0, 0))] * 2,
        ),
        out_shape=[jax.ShapeDtypeStruct(out, F32)] * 2,
        compiler_params=params(),
        cost_estimate=LIGHT,
        name="weight_grad",
    )(mine, *operands)


def down_grad_kernel(grad_ref, activ_ref, out_ref):
    out_ref[...] = dot1(grad_ref[...], activ_ref[...], TN)


def down_grad(grad, activ):
    rows, model = grad.shape
    steps = 4
    tile = model // steps
    return pl.pallas_call(
        down_grad_kernel,
        grid=(steps,),
        in_specs=[pl.BlockSpec((rows, tile), lambda g: (0, g)), whole(activ.shape)],
        out_specs=pl.BlockSpec((tile, activ.shape[1]), lambda g: (g, 0)),
        out_shape=jax.ShapeDtypeStruct((model, activ.shape[1]), F32),
        compiler_params=params(),
        cost_estimate=LIGHT,
        name="down_grad",
    )(grad, activ)


def combine_kernel(bit, mine_ref, kept_ref, arrived_ref, sent_ref, next_ref):
    side = (mine_ref[0] // bit) % 2
    sent_ref[...] = (kept_ref[:, 1 - side] + arrived_ref[:, 1 - side]).reshape(sent_ref.shape)
    next_ref[...] = (kept_ref[:, side] + arrived_ref[:, side]).reshape(next_ref.shape)


IN_VMEM = pl.BlockSpec(memory_space=pltpu.VMEM)


def combine(mine, bit, low, kept, arrived):
    total, rows, columns = kept.shape
    half = total // 2
    view = lambda array: array.reshape((half >> low, 2, 1 << low, rows, columns))
    return pl.pallas_call(
        partial(combine_kernel, bit),
        in_specs=[SCALARS, IN_VMEM, IN_VMEM],
        out_specs=[IN_VMEM, IN_VMEM],
        out_shape=[jax.ShapeDtypeStruct((half, rows, columns), F32)] * 2,
        compiler_params=params(),
        cost_estimate=LIGHT,
        name="combine",
    )(mine, view(kept), view(arrived))


def carry_kernel(count, dims, *refs):
    maps, terms, out_ref = refs[: count - 1], refs[count - 1 : -1], refs[-1]
    for head in range(out_ref.shape[0]):
        state = terms[-1][head]
        for map_ref, term_ref in zip(reversed(maps), reversed(terms[:-1])):
            state = dot3(map_ref[head], state, dims) + term_ref[head]
        out_ref[head] = state


def carry(maps, terms, dims):
    return pl.pallas_call(
        partial(carry_kernel, len(terms), dims),
        out_shape=jax.ShapeDtypeStruct(terms[0].shape, F32),
        compiler_params=params(),
        cost_estimate=LIGHT,
        name="carry",
    )(*maps, *terms)


def quarter_kernel(place_ref, kept_ref, near_ref, out_ref):
    out_ref[...] = kept_ref[...] + near_ref[...]


def quarter_sum(place, kept, near):
    rows, model = kept.shape
    steps = 2
    tile = rows // (2 * steps)
    other = pl.BlockSpec((tile, model), lambda g, at: ((1 - at[0] % 2) * steps + g, 0))
    return pl.pallas_call(
        quarter_kernel,
        grid_spec=pltpu.PrefetchScalarGridSpec(
            num_scalar_prefetch=1,
            grid=(steps,),
            in_specs=[other, other],
            out_specs=pl.BlockSpec((tile, model), lambda g, at: (g, 0)),
        ),
        out_shape=jax.ShapeDtypeStruct((rows // 2, model), F32),
        compiler_params=params(),
        cost_estimate=LIGHT,
        name="quarter_sum",
    )(place, kept, near)


def norm_back_kernel(
    place_ref, kept_ref, near_ref, arrived_ref, value_ref, gain_ref, residual_ref, out_ref
):
    step = pl.program_id(0)
    tile = kept_ref.shape[0]
    rows = out_ref.shape[0] - EDGE
    values = value_ref[...].astype(F32)
    grad = kept_ref[...] + near_ref[...] + arrived_ref[...]
    scale = lax.rsqrt(jnp.mean(values * values, -1, keepdims=True) + EPSILON)
    normed = values * scale
    through = grad * gain_ref[...].astype(F32)
    back = scale * (through - normed * jnp.mean(through * normed, -1, keepdims=True))
    out_ref[pl.ds(pl.multiple_of(step * tile, tile), tile)] = back + residual_ref[...].astype(F32)
    sums = jnp.sum((grad * normed).reshape(-1, EDGE, grad.shape[1]), 0)

    @pl.when(step == 0)
    def _():
        out_ref[rows:] = sums

    @pl.when(step != 0)
    def _():
        out_ref[rows:] += sums


def norm_back(place, kept, near, arrived, values, gain, residual):
    rows, model = arrived.shape
    steps = 2
    tile = rows // steps
    local = pl.BlockSpec((tile, model), lambda g, at: (g, 0))

    own = pl.BlockSpec((tile, model), lambda g, at: (at[0] % 2 * steps + g, 0))

    def spec_of(array):
        if array.shape[0] == rows + EDGE:
            return local
        return pl.BlockSpec((tile, model), lambda g, at: (at[0] * steps + g, 0))

    return pl.pallas_call(
        norm_back_kernel,
        grid_spec=pltpu.PrefetchScalarGridSpec(
            num_scalar_prefetch=1,
            grid=(steps,),
            in_specs=[
                own,
                own,
                local,
                spec_of(values),
                pl.BlockSpec((1, model), lambda g, at: (0, 0)),
                spec_of(residual),
            ],
            out_specs=pl.BlockSpec((rows + EDGE, model), lambda g, at: (0, 0)),
        ),
        out_shape=jax.ShapeDtypeStruct((rows + EDGE, model), F32),
        compiler_params=params(),
        cost_estimate=LIGHT,
        name="norm_back",
    )(place, kept, near, arrived, values, gain, residual)


def own_output_kernel(kept_ref, arrived_ref, middle_ref, gain_ref, out_ref):
    rows, model = kept_ref.shape
    width = gain_ref.shape[1]
    out_ref[:rows] = kept_ref[...] + arrived_ref[...] + middle_ref[...]
    out_ref[rows:] = jnp.concatenate(
        [gain_ref[...], jnp.zeros((EDGE, model - width), F32)], 1
    )


def own_output(place, kept, arrived, middle, grad_gain):
    rows, model = kept.shape
    return pl.pallas_call(
        lambda place_ref, *refs: own_output_kernel(*refs),
        grid_spec=pltpu.PrefetchScalarGridSpec(
            num_scalar_prefetch=1,
            grid=(1,),
            in_specs=[
                pl.BlockSpec((rows, model), lambda g, at: (0, 0)),
                pl.BlockSpec((rows, model), lambda g, at: (0, 0)),
                pl.BlockSpec((rows, model), lambda g, at: (at[0], 0)),
                pl.BlockSpec(grad_gain.shape, lambda g, at: (0, 0)),
            ],
            out_specs=pl.BlockSpec((rows + EDGE, model), lambda g, at: (0, 0)),
        ),
        out_shape=jax.ShapeDtypeStruct((rows + EDGE, model), F32),
        compiler_params=params(),
        cost_estimate=LIGHT,
        name="own_output",
    )(place, kept, arrived, middle, grad_gain)


def pack_kernel(parts, heads, *refs):
    pieces, (second_ref, gain_ref) = refs[:parts], refs[parts : parts + 2]
    decay_refs, taps_refs = refs[parts + 2 : parts + 2 + heads], refs[parts + 2 + heads : -1]
    out_ref = refs[-1]
    place = 0
    for rows in (sum(ref[...] for ref in pieces), second_ref[...]):
        total = jnp.sum(rows, 0, keepdims=True)
        for start in range(0, total.shape[1], LANES):
            out_ref[place : place + 1] = total[:, start : start + LANES]
            place += 1
    for ref in taps_refs:
        for start in range(0, ref.shape[1], LANES):
            out_ref[place : place + EDGE] = ref[:, start : start + LANES]
            place += EDGE
    out_ref[place : place + EDGE] = gain_ref[:, :LANES]
    out_ref[place + EDGE : place + 2 * EDGE] = sum(ref[...] for ref in decay_refs)


def pack_small(pieces, second, gain, decays, taps):
    model = second.shape[1]
    columns = sum(part.shape[1] for part in taps)
    rows = 2 * (model // LANES) + EDGE * (columns // LANES) + 2 * EDGE
    below = pieces[0].shape[0] // EDGE - 1
    others = (second, gain, *decays, *taps)
    return pl.pallas_call(
        partial(pack_kernel, len(pieces), len(decays)),
        grid=(1,),
        in_specs=[pl.BlockSpec((EDGE, model), lambda g: (below, 0))] * len(pieces)
        + [whole(part.shape) for part in others],
        out_specs=whole((rows, LANES)),
        out_shape=jax.ShapeDtypeStruct((rows, LANES), F32),
        compiler_params=params(),
        cost_estimate=LIGHT,
        name="pack_small",
    )(*pieces, *others)


def unpack_kernel(
    mine_ref, small_ref, first_ref, second_ref, gain_ref, decay_ref, taps_ref, *, count, model
):
    blocks = model // LANES
    size = model // count
    index = mine_ref[0]
    for base, ref in ((0, first_ref), (blocks, second_ref)):
        row = small_ref[pl.ds(base + index * size // LANES, 1)]
        if size < LANES:
            row = pltpu.roll(row, (LANES - index * size % LANES) % LANES, 1)
        ref[...] = row[:, :size]
    place = 2 * blocks
    for start in range(0, taps_ref.shape[1], LANES):
        taps_ref[:, start : start + LANES] = small_ref[place : place + CONV]
        place += EDGE
    gain_ref[...] = jnp.sum(small_ref[place : place + EDGE], 0, keepdims=True)
    decay_ref[...] = small_ref[place + EDGE : place + 2 * EDGE]


def unpack_small(mine, small, count, model, columns):
    size = model // count
    shapes = [(1, size), (1, size), (1, LANES), (EDGE, LANES), (CONV, columns)]
    return pl.pallas_call(
        partial(unpack_kernel, count=count, model=model),
        in_specs=[SCALARS, IN_VMEM],
        out_shape=[jax.ShapeDtypeStruct(shape, F32) for shape in shapes],
        compiler_params=params(),
        cost_estimate=LIGHT,
        name="unpack_small",
    )(mine, small)


def exchange(value, axis, bit):
    count = lax.axis_size(axis)
    return lax.ppermute(value, axis, [(place, place ^ bit) for place in range(count)])


def shifted(value, axis, steps):
    count = lax.axis_size(axis)
    first, last = (max(0, -steps), min(count, count - steps))
    return lax.ppermute(value, axis, [(source, source + steps) for source in range(first, last)])


def bits_of(axis):
    count = lax.axis_size(axis)
    return [1 << power for power in range(count.bit_length() - 1)]


class GatherNear:
    def __init__(self, value, axis):
        self.axis = axis
        self.bits = bits_of(axis)
        self.found = {0: value}
        for bit in self.bits[::-1]:
            self.found[bit] = exchange(value, axis, bit)

    def finish(self, *others):
        for bit in self.bits[::-1]:
            if others and bit == self.bits[-1]:
                self.found[bit] = after(self.found[bit], *others)
            for near in sorted(self.found):
                if near > bit and not near & bit and near | bit not in self.found:
                    self.found[near | bit] = exchange(self.found[near], self.axis, bit)
        return [self.found[near] for near in sorted(self.found)]


def gather_near(value, axis, *others):
    start = GatherNear(value, axis)
    others = sum([list(one()) if callable(one) else [one] for one in others], [])
    return start.finish(*others)


def after(value, *others):
    return lax.optimization_barrier((value,) + others)[0]


def join(*values):
    return lax.optimization_barrier(values)


class Scatter:
    def __init__(self, mine, axis, order, kept, sent):
        self.mine = mine
        self.axis = axis
        self.bits = sorted(order)
        self.order = list(order)
        self.kept = kept
        self.sent = sent

    def send(self):
        bit = self.order.pop(0)
        self.bits.remove(bit)
        self.arrived = exchange(self.sent, self.axis, bit)
        self.sent = None
        return self

    def add(self):
        if self.order:
            bit = self.order[0]
            self.sent, self.kept = combine(
                self.mine, bit, self.bits.index(bit), self.kept, self.arrived
            )
        else:
            self.total = self.kept[0] + self.arrived[0]
        return self

    def step(self):
        self.add()
        return self.send() if self.order else self


class HeadSum:
    def __init__(self, place, sent):
        self.place = place
        self.near = exchange(sent, "head", 1)

    def send(self, half):
        self.half = half
        self.kept = quarter_sum(self.place, half, self.near)
        self.arrived = exchange(self.kept, "head", 2)


class WholeSum:
    def __init__(self, pairs):
        self.kept = self.sent = jnp.concatenate(
            [
                contract(left, lax.slice_in_dim(right, place * size, (place + 1) * size, axis=1), 0, 0)
                for left, right, place, size in pairs
            ],
            1,
        )
        self.order = []

    def send(self):
        self.arrived = lax.psum_scatter(self.sent, "seq", scatter_dimension=0, tiled=True)
        return self

    def add(self):
        self.total = self.kept = self.arrived
        return self

    def step(self):
        return self.add()


def arrive(*scatters, also=()):
    found = join(*[one.arrived for one in scatters], *also)
    for one, value in zip(scatters, found):
        one.arrived = value
    return found[len(scatters) :]


def contract(left, right, left_dim, right_dim):
    return lax.dot_general(
        left, right, (((left_dim,), (right_dim,)), ((), ())), preferred_element_type=F32
    )


def carried_in(total, own, axis, backward, maps=None):
    count = lax.axis_size(axis)
    sign = -1 if backward else 1
    reach = count - DOCS - 1
    if reach > DOCS - 1:
        reach = count - 1
    dims = (1, 1) if backward else (2, 1)
    width = LANES

    def move(map_of, state):
        return lax.dot_general(
            map_of, state, (((dims[0],), (1,)), ((0,), (0,))), precision=lax.Precision.HIGHEST
        )

    if reach < count - 1:
        if own is None:
            both = [shifted(total, axis, sign * step) for step in range(1, reach)]
            maps = [pair[..., :width] for pair in both]
            terms = [pair[..., width:] for pair in both]
            terms.append(shifted(total[..., width:], axis, sign * reach))
        else:
            terms = [shifted(own, axis, sign * step) for step in range(1, reach + 1)]
    else:
        every_map = lax.all_gather(total[..., :width], axis)
        every_term = lax.all_gather(total[..., width:] if own is None else own, axis)
        mine = lax.axis_index(axis)

        def at(array, step):
            place = mine - sign * step
            picked = lax.dynamic_index_in_dim(array, jnp.clip(place, 0, count - 1), 0, False)
            return jnp.where((place >= 0) & (place < count), picked, 0.0)

        maps = [at(every_map, step) for step in range(1, reach)]
        terms = [at(every_term, step) for step in range(1, reach + 1)]
    if reach < count - 1:
        return carry(maps, terms, TN if backward else NN)
    state = terms[-1]
    for map_of, term in zip(reversed(maps), reversed(terms[:-1])):
        state = move(map_of, state) + term
    return state


def maps_between(total, axis):
    count = lax.axis_size(axis)
    reach = count - DOCS - 1
    if reach > DOCS - 1:
        return None
    return [shifted(total[..., :LANES], axis, -step) for step in range(1, reach)]


def normalize(values):
    return values * lax.rsqrt(jnp.mean(values * values, -1, keepdims=True) + EPSILON)


def lanes_of(per_head):
    row = jnp.repeat(per_head, STEPS + 1)
    return jnp.pad(row, (0, LANES - row.shape[0]))[None]


def body(
    block_input,
    first_gain,
    w_mix,
    conv_taps,
    w_rates,
    log_rate,
    rate_bias,
    w_outgate,
    head_gain,
    w_out,
    second_gain,
    w_ffn,
    w_down,
    grad_output,
    seq_starts,
):
    rows, model = block_input.shape
    heads = log_rate.shape[0]
    parts = lax.axis_size("head")
    quarter = rows // parts
    head_index = lax.axis_index("head")
    seq, seq_index = lax.axis_size("seq"), lax.axis_index("seq")
    rate_lanes = w_rates.shape[1]
    ffn_flat = w_ffn.reshape(model, -1)

    head_bits = bits_of("head")
    core = head_index % 2
    kept_half, sent_half = core[None], (1 - core)[None]

    def block_of(index):
        return sum(
            ((index // bit) % 2) * (parts // (2 * bit)) for bit in head_bits
        )

    places = jnp.stack([block_of(head_index ^ near) for near in range(parts)]).astype(jnp.int32)
    own_block = places[0]
    own_rows = lambda array: lax.dynamic_slice_in_dim(array, own_block * quarter, quarter, 0)

    head_mine, seq_mine = head_index[None], seq_index[None]
    head_order, seq_bits = head_bits, bits_of("seq")

    raw_edge = shifted(block_input[rows - EDGE :].astype(F32), "seq", 1)
    w_out_start = GatherNear(w_out.astype(F32), "head")
    normed1_low, mixing, rates, outgate, edge = first_projections(
        raw_edge, block_input, first_gain[None], w_mix, w_rates.T, w_outgate
    )
    w_out_near = w_out_start.finish()
    conv, q, k, x, system, cumul, u, w, scores, query_map, prefix, phi, total = local_maps(
        seq_starts, log_rate, rate_bias, edge, mixing, conv_taps, rates
    )
    width = LANES
    incoming = carried_in(total, None, "seq", False)
    head_gain_row = after(head_gain, total)[None]
    state, fresh, mixed, gated = outputs_of(
        seq_starts, incoming, (prefix, u, w, scores, q, cumul), outgate, head_gain_row, F32
    )
    gain2_row = after(second_gain, gated)[None]
    w_rates_wide = jnp.pad(after(w_rates, gated), ((0, 0), (0, LANES - rate_lanes)))
    gated_start = GatherNear(gated, "head")
    w_out_low, ffn_flat = low_weight([after(piece, gated) for piece in w_out_near], ffn_flat)
    maps = maps_between(after(total, gated), "seq") or ()
    grad_activ = grad_activ_of(after(grad_output, w_out_low), w_down)
    ffn_flat, w_out_low, gain2_row, w_rates_wide, grad_activ, *maps = join(
        ffn_flat, w_out_low, gain2_row, w_rates_wide, grad_activ, *maps
    )
    gated_near = gated_start.finish(ffn_flat, w_out_low)

    dense = lambda half, filled: dense_half(
        half, gated_near, w_out_low, block_input, gain2_row, ffn_flat, w_down, grad_activ, filled
    )
    *filled, back_sent, fore_sent = dense(sent_half, None)
    split = lambda half: half.reshape(parts // 2, quarter, model)
    back = HeadSum(places[:1], back_sent)
    *filled, back_kept, fore_kept = dense(kept_half, filled)
    middle, normed2_low, activ_low, *grads_both = filled
    back.send(back_kept)

    near_first, far_first = seq_bits, seq_bits[1:] + seq_bits[:1]
    tiled = model // seq % LANES == 0

    def grad_sum(order, *pairs, tie=()):
        (left, *rest), *others = pairs
        pairs = [(after(left, *tie), *rest)] + others
        if not tiled:
            return WholeSum(pairs)
        sent, kept = weight_grad(seq_mine, order[0], seq, pairs)
        return Scatter(seq_mine, "seq", order, kept, sent)

    def total_of(one):
        while one.order:
            one.step()
        return one.add().total

    ffn_sums, tie = [], back.kept
    for order, right in zip((near_first, far_first, near_first), grads_both):
        ffn_sums.append(grad_sum(order, (normed2_low, right, 0, right.shape[1]), tie=(tie,)))
        tie = ffn_sums[-1].kept
    ffn_one, ffn_two, ffn_three = ffn_sums
    ffn_one.send()
    ffn_two.send()
    fore = Scatter(
        head_mine, "head", head_order, split(fore_kept), after(split(fore_sent), back.kept)
    ).send()
    down_sum = grad_sum(
        near_first, (grad_output, activ_low, 0, activ_low.shape[1]), tie=(ffn_three.kept,)
    )
    ffn_three.sent, down_sum.sent = arrive(
        back, fore, ffn_one, ffn_two, also=(ffn_three.sent, down_sum.sent)
    )
    grad_middle_own = norm_back(
        places[:1], back.half, back.near, back.arrived, middle, gain2_row, grad_output
    )

    middle_start = GatherNear(grad_middle_own, "head")
    ffn_three.sent = after(ffn_three.sent, grad_middle_own)
    ffn_three.send()
    tie = grad_middle_own
    for one in (ffn_one, ffn_two):
        one.arrived = after(one.arrived, tie)
        one.step()
        tie = one.kept
    fore.arrived = after(fore.arrived, tie)
    fore.add()
    backed = partial(
        gate_back, weight=w_out, mixed=mixed, outgate=outgate, gain=head_gain_row, query=query_map, prefix=prefix
    )
    near_half = parts // 2
    near_pieces = [grad_middle_own, after(middle_start.found[1], fore.kept)]
    first_backed = backed(places[:near_half], near_pieces, before=None)
    middle_start.found[1], middle_start.found[2], fore.sent, *first_backed = arrive(
        *ffn_sums, also=(near_pieces[1], middle_start.found[2], fore.sent, *first_backed)
    )

    fore.send()
    grad_gain, grad_total, grad_second_gain, grad_branch, grad_mixed, outgate_low, term = backed(
        places[near_half:], middle_start.finish()[near_half:], before=first_backed
    )
    leaving = carried_in(total, grad_total, "seq", True, maps)
    out_width, outgate_width = gated.shape[1], outgate_low.shape[1]
    side_sum = grad_sum(
        near_first,
        (grad_branch, gated.astype(BF16), 0, out_width),
        (normed1_low, outgate_low, 0, outgate_width),
        tie=(grad_total,),
    )
    tie = side_sum.kept
    for one in (ffn_three, ffn_one):
        one.arrived = after(one.arrived, tie)
        one.add()
        tie = one.kept
    leaving, side_sum.sent, ffn_three.sent, ffn_one.sent, down_sum.sent = arrive(
        fore, also=(leaving, side_sum.sent, ffn_three.sent, ffn_one.sent, down_sum.sent)
    )
    output_own = own_output(places[:1], fore.kept[0], fore.arrived[0], middle, grad_gain)

    output_start = GatherNear(output_own, "head")
    down_sum.send()
    ffn_three.send()
    ffn_one.send()
    leaving, output_start.found[1] = join(after(leaving, output_own), output_start.found[1])
    grad_mix_rows, last_rows, before_rows, rate_low, decay_sums, grad_taps = recurrence_back(
        seq_starts,
        leaving,
        (term, phi, state, fresh, grad_mixed, scores, x, system, cumul, q, k),
        rates,
        log_rate,
        rate_bias,
        conv,
        edge,
        mixing,
        conv_taps,
    )
    before_rows, output_start.found[2] = arrive(
        ffn_one, ffn_three, down_sum, also=(before_rows, output_start.found[2])
    )

    returned = shifted(before_rows, "seq", -1)
    down_sum.add()
    ffn_three.arrived = after(ffn_three.arrived, down_sum.kept)
    ffn_three.add()
    returned, side_sum.sent, down_sum.sent, ffn_three.sent = join(
        returned, side_sum.sent, down_sum.sent, ffn_three.sent
    )
    for one in (side_sum, down_sum, ffn_three):
        one.send()
    last_rows = last_rows + jnp.pad(returned, ((EDGE, 0), (0, 0)))
    mixing_low = lax.dynamic_update_slice_in_dim(
        grad_mix_rows, last_rows.astype(BF16), rows - 2 * EDGE, 0
    )
    columns = mixing_low.shape[1]
    half_columns, narrow = columns // 2, columns // 10
    mix_one = grad_sum(near_first, (normed1_low, mixing_low, 0, half_columns))
    part_sent, part_kept = first_back(
        kept_half,
        (after(mixing_low, mix_one.kept), outgate_low, rate_low),
        (w_mix, w_outgate, w_rates_wide),
    )
    output_near = output_start.finish()
    part_sent, part_kept, mix_one.sent, *output_near = arrive(
        side_sum, down_sum, ffn_three,
        also=(part_sent, part_kept, mix_one.sent, *output_near),
    )
    part = HeadSum(places[:1], part_sent)
    part.send(part_kept)
    mix_one.send()
    tie = part.kept
    for one in (side_sum, down_sum):
        one.arrived = after(one.arrived, tie)
        one.step()
        tie = one.kept

    mix_two = grad_sum(
        near_first,
        *[(normed1_low, mixing_low, 5 + piece, narrow) for piece in range(3)],
        tie=(tie,),
    ).send()
    output, grad_head_gain = place_rows(
        places, [after(piece, mix_two.kept) for piece in output_near], BF16
    )
    mix_three = grad_sum(
        near_first,
        *[(normed1_low, mixing_low, 8 + piece, narrow) for piece in range(2)],
        (normed1_low, rate_low, 0, LANES),
        tie=(output,),
    )
    mix_one.arrived = after(mix_one.arrived, mix_three.kept)
    mix_one.step()
    mix_three.sent, _ = arrive(
        part, side_sum, down_sum, also=(mix_three.sent, mix_one.kept)
    )
    grad_input_own = norm_back(
        places[:1], part.half, part.near, part.arrived, block_input, first_gain[None], grad_middle_own
    )

    input_start = GatherNear(grad_input_own, "head")
    mix_three.sent, side_sum.sent, _ = join(mix_three.sent, side_sum.sent, grad_input_own)
    mix_three.send()
    tie = grad_input_own
    for one in (side_sum, mix_two):
        one.arrived = after(one.arrived, tie)
        one.step()
        tie = one.kept
    ffn_two.arrived = after(ffn_two.arrived, tie)
    ffn_two.step()
    down_sum.arrived = after(down_sum.arrived, ffn_two.kept)
    grad_down = total_of(down_sum)[:, : w_down.shape[0]].T
    mix_one.arrived, side_sum.arrived, _ = join(mix_one.arrived, side_sum.arrived, grad_down)
    mix_one.step()
    input_start.found[2], grad_down, _ = arrive(
        mix_two, mix_three, ffn_two, also=(input_start.found[2], grad_down, mix_one.kept)
    )
    input_near = input_start.finish()
    mix_three.step()
    mix_two.arrived = after(mix_two.arrived, mix_three.kept)
    mix_two.step()
    input_near[0] = after(input_near[0], mix_two.kept)
    small = pack_small(
        input_near, grad_second_gain, grad_head_gain, [decay_sums], [grad_taps]
    )
    arrived = exchange(small, "seq", seq_bits[0])
    input_near[0] = after(input_near[0], small)
    grad_input, _ = place_rows(places, input_near, F32)
    mix_three.arrived = after(mix_three.arrived, grad_input)
    mix_three.step()
    small = small + after(arrived, mix_three.kept)
    for bit in seq_bits[1:]:
        small = small + exchange(small, "seq", bit)
        for one in (mix_one, mix_two, side_sum, *ffn_sums):
            one.arrived = after(one.arrived, small)
    gain1_own, gain2_own, gain_sum, decay_sum, taps_sum = unpack_small(
        seq_mine, small, seq, model, mixing.shape[1]
    )
    decay_lanes = decay_sum[:, STEPS : heads * (STEPS + 1) : STEPS + 1]

    side_total = total_of(side_sum)
    ffn_total = jnp.concatenate([total_of(one) for one in ffn_sums], 1)
    mix_total = jnp.concatenate([total_of(one) for one in (mix_one, mix_two, mix_three)], 1)
    return (
        output,
        grad_input,
        gain1_own[0],
        mix_total[:, :columns],
        taps_sum,
        mix_total[:, columns : columns + rate_lanes],
        decay_lanes[0],
        decay_lanes[1],
        side_total[:, out_width:],
        gain_sum[0],
        side_total[:, :out_width].T,
        gain2_own[0],
        ffn_total.reshape((-1,) + w_ffn.shape[1:]),
        grad_down,
    )


def solution(mesh):
    return jax.shard_map(
        body,
        mesh=mesh,
        in_specs=(
            P("seq", None),
            P(),
            P(None, "head"),
            P(None, "head"),
            P(None, "head"),
            P("head"),
            P("head"),
            P(None, "head"),
            P(),
            P("head", None),
            P(),
            P(None, None, "head"),
            P("head", None),
            P("seq", None),
            P("seq"),
        ),
        out_specs=(
            P("seq", None),
            P("seq", None),
            P("seq"),
            P("seq", "head"),
            P(None, "head"),
            P("seq", "head"),
            P("head"),
            P("head"),
            P("seq", "head"),
            P(),
            P("head", "seq"),
            P("seq"),
            P("seq", None, "head"),
            P("head", "seq"),
        ),
        check_vma=False,
    )
```
